128 devices in a mesh: gx: 32 (over x, z, core), gy: 4 (over y).
Axes of the slice: x: 4, y: 4, z: 4, core: 2. Of those that a mesh axis runs over, the one named last changes fastest.
Arguments:
- point_feats: bfloat16 [4096, 32, 128], P(('gx', 'gy')), may hold values from -6 to 6
- point_offsets: bfloat16 [4096, 3, 128], P(('gx', 'gy')), may hold values from 0 to 1
- base_cells: int32 [4096, 128], P(('gx', 'gy')), may hold values from 0 to 1784
- block_owners: int32 [4096, 1], P(('gx', 'gy')), may hold values from 0 to 31; in each aligned block of 32 rows (0 to 31, 32 to 63, ...) at most 2 rows name the same one
- point_counts: int32 [128], P(('gx', 'gy')), may hold values from 1 to 4096, 393216 in all
- lift_weight: bfloat16 [32, 32], replicated, may hold values from -1 to 1
- conv_weight: bfloat16 [27, 32, 32], replicated, may hold values from -0.21875 to 0.21875
- read_weight: bfloat16 [32], replicated, may hold values from -1 to 1
- cotangent: float32 [4096, 128], P(('gx', 'gy')), may hold values from -24 to 24
Outputs:
- prediction: float32 [4096, 128], P(('gx', 'gy'))
- grad_feats: bfloat16 [4096, 32, 128], P(('gx', 'gy'))
- grad_conv: float32 [27, 32, 32], replicated
The draws below stay inside these ranges and needn't reach their ends.
Inputs may be any that keep to these rules, and one draw needn't show every extreme that they name: `block_owners`: among the blocks of one device, at most 2 name the same owner; some owner is named by exactly 2 of them. `base_cells`: decoded as in the reference program, the base corner lies in the owner's slab with all eight neighbour cells inside it. `point_counts`: the counts sum to 393216; one device is full.
All inputs are finite; a program needn't handle non-finite values.
Results may differ from the reference program's by a relative error of at most 0.015.
Values may be sent and summed in bfloat16 or wider, within the bound.
A program may use at most 64 MiB of HBM per device.

```python
import math
import jax
import jax.numpy as jnp
import numpy as np
from jax import lax

C = 32
CX = 2
CY = 8
NZ = 256
NB_DEV = 32
BLK = 128
CAP = 2
NX = 64
NY = 32
NB_TOTAL = 4096
N_GX = 32
N_GY = 4
DEVICES = 128


def touch_ends(entries, rng, smallest, top_value):
    index_at = [jax.random.randint(jax.random.fold_in(rng, axis), (), 0, length) for axis, length in enumerate(entries.shape)]
    longest = entries.shape.index(max(entries.shape))
    next_to = index_at[:longest] + [(index_at[longest] + 1) % entries.shape[longest]] + index_at[longest + 1:]
    return entries.at[tuple(index_at)].set(smallest).at[tuple(next_to)].set(top_value)


def shard_levels(rng, extent, cuts, low, high):
    def one(dim, parts):
        draws = jax.random.uniform(jax.random.fold_in(jax.random.fold_in(rng, 6), dim), (parts,), jnp.float32, low / len(cuts), high / len(cuts))
        return jnp.repeat(jnp.exp(draws), extent[dim] // parts).reshape((-1,) + (1,) * (len(extent) - dim - 1))

    loudness = one(*cuts[0])
    for cut in cuts[1:]:
        loudness = loudness * one(*cut)
    return loudness


def profile(count, total, most, skew):
    loads = [(1 << 20) // math.isqrt(rank ** skew) + 1 for rank in range(2, count + 1)]
    spare, holding = total - most - (count - 1), [1] * (count - 1)
    while spare > 0:
        free = [i for i in range(count - 1) if holding[i] < most]
        pool, remaining = sum([loads[i] for i in free]), spare
        for i in free:
            extra = min(most - holding[i], max(1, remaining * loads[i] // pool), spare)
            holding[i] = holding[i] + extra
            spare = spare - extra
    return np.array([most] + holding)


def uneven(own_key, number_of, total, most, lean):
    if number_of == 2:
        one = jax.random.randint(own_key, (), max(1, total - most), min(most, total - 1) + 1)
        return jnp.stack([one, total - one])
    lengths = jnp.asarray(profile(number_of, total, most, lean), jnp.int32)
    pairs = (number_of - 1) // 2
    giver, taker = lengths[1:1 + 2 * pairs:2], lengths[2:2 + 2 * pairs:2]
    margin = jnp.minimum(giver - 1, most - taker)
    shifted = jax.random.randint(jax.random.fold_in(own_key, 1), (pairs,), 0, 1 << 20) % (margin + 1)
    lengths = lengths.at[1:1 + 2 * pairs:2].set(giver - shifted).at[2:2 + 2 * pairs:2].set(taker + shifted)
    return lengths[jax.random.permutation(jax.random.fold_in(own_key, 2), number_of)]


def routed_block(key, own, number, rows, count, top, reach, skew):
    order = jax.random.permutation(key, count)
    packed, usual = portions_of(count, rows * top, reach, skew, True), portions_of(count, rows * top, reach, skew, False)
    places = jnp.arange(count)

    def named(tallies, rotation):
        used = int((tallies > 0).sum())
        fixed = max(1, used // 4)
        passed = fixed + (places - fixed + rotation * (used - fixed)) % max(1, count - fixed)
        return jnp.zeros((count,), jnp.int32).at[order[jnp.where(places < fixed, places, passed)]].set(jnp.asarray(tallies, jnp.int32))

    tallies = jnp.where(number % 4 == 0, named(packed, number // 4), named(usual, number - number // 4 - 1))
    mixed = jax.random.permutation(jax.random.fold_in(own, 3), count)
    donor, taker = mixed[0:count // 2 * 2:2], mixed[1:count // 2 * 2:2]
    room = jnp.minimum(tallies[donor] - 1, reach - tallies[taker]) // 2
    room = jnp.where((donor == order[0]) | (taker == order[0]) | (tallies[taker] == 0), 0, jnp.maximum(room, 0))
    passed = jax.random.randint(jax.random.fold_in(own, 4), (count // 2,), 0, 1 << 20) % (room + 1)
    tallies = tallies.at[donor].add(-passed).at[taker].add(passed)
    items = jnp.searchsorted(jnp.cumsum(tallies), jnp.arange(rows * top), side="right").astype(jnp.int32)
    listing = items.reshape(top, rows).T
    listing = listing[jax.random.permutation(jax.random.fold_in(own, 1), rows)]
    rotation = jax.random.randint(jax.random.fold_in(own, 2), (rows, 1), 0, top)
    return jnp.take_along_axis(listing, (jnp.arange(top)[None, :] + rotation) % top, axis=1)


def portions_of(number_of, total, reach, skew, full):
    portions = [(1 << 20) // math.isqrt(rank ** skew) + 1 for rank in range(1, number_of + 1)]
    largest = reach if full else min(reach, max(-(-total // number_of), total * portions[0] // sum(portions)))
    least = 1 if total - largest >= number_of - 1 else 0
    given, rest = [largest] + [least] * (number_of - 1), total - largest - least * (number_of - 1)
    while rest > 0:
        candidates = [i for i in range(1, number_of) if given[i] < largest] or [i for i in range(1, number_of) if given[i] < reach]
        pool, remaining = sum([portions[i] for i in candidates]), rest
        for i in candidates:
            addition = min(reach - given[i], max(1, remaining * portions[i] // pool), rest)
            given[i] = given[i] + addition
            rest = rest - addition
    return np.array(given)


def normal_values(own_key, extent, scale, reach, shards=(), held_as=jnp.bfloat16):
    result = jax.random.normal(own_key, extent, jnp.float32) * scale
    if len(shards) > 0:
        result = shard_levels(own_key, extent, shards, -0.22, 0.18) * result
    return jnp.clip(result, min=-reach, max=reach).astype(held_as)


def setup_inputs(seed: int = 0) -> dict:
    seeds = jax.random.split(jax.random.key(seed), 10)
    point_feats = normal_values(seeds[0], (NB_TOTAL, C, BLK), 1.0, 6.0, ((0, 128),))
    point_offsets = jnp.clip(1.0 * jax.random.uniform(seeds[1], (NB_TOTAL, 3, BLK), jnp.float32) ** shard_levels(seeds[1], (NB_TOTAL, 3, BLK), ((0, 128),), -0.2, 0.2), 0.0, 1.0).astype(jnp.bfloat16)
    base_cells = touch_ends(jax.random.randint(seeds[2], (NB_TOTAL, BLK), 0, (CX - 1) * (CY - 1) * (NZ - 1)), jax.random.fold_in(seeds[2], 1), 0, ((CX - 1) * (CY - 1) * (NZ - 1)) - 1).astype(jnp.int32)
    block_owners_keys = jax.random.split(jax.random.fold_in(seeds[3], 1), NB_TOTAL // NB_DEV)
    block_owners_turns = jax.random.permutation(jax.random.fold_in(seeds[3], 3), NB_TOTAL // NB_DEV)
    block_owners = jax.vmap(lambda own, number: routed_block(jax.random.fold_in(seeds[3], 2), own, number, NB_DEV, N_GX, 1, CAP, 2))(block_owners_keys, block_owners_turns).reshape((NB_TOTAL, 1))
    point_counts = uneven(seeds[4], DEVICES, 3 * DEVICES * NB_DEV * BLK // 4, NB_DEV * BLK, 2).astype(jnp.int32)
    lift_weight = normal_values(seeds[5], (C, C), C ** -0.5, 1.0)
    conv_weight = normal_values(seeds[6], (27, C, C), (27 * C) ** -0.5, 0.21875)
    read_weight = normal_values(seeds[7], (C,), C ** -0.5, 1.0)
    cotangent = normal_values(seeds[8], (NB_TOTAL, BLK), 4.0, 24.0, ((0, 128),), jnp.float32)
    return dict(point_feats=point_feats, point_offsets=point_offsets, base_cells=base_cells, block_owners=block_owners, point_counts=point_counts, lift_weight=lift_weight, conv_weight=conv_weight, read_weight=read_weight, cotangent=cotangent)


width_sq = 0.5

def corner_steps():
    corners = jnp.arange(8, dtype=jnp.int32)
    return (corners // 4, corners // 2 % 2, corners % 2)

def corner_weights(offsets):
    spots = offsets.astype(jnp.float32)
    along_x, along_y, along_z = corner_steps()
    dist = (spots[:, 0:1, :] - along_x.astype(jnp.float32)[None, :, None]) ** 2
    dist = dist + (spots[:, 1:2, :] - along_y.astype(jnp.float32)[None, :, None]) ** 2
    dist = dist + (spots[:, 2:3, :] - along_z.astype(jnp.float32)[None, :, None]) ** 2
    return jnp.exp(-dist / width_sq)

def spread(values, weights, cell_ids, channels, cell_count):
    contrib = values[:, None, :, :] * weights[:, :, None, :]
    flat = jnp.transpose(contrib, (2, 0, 1, 3)).reshape(channels, -1)
    return jnp.zeros((channels, cell_count), jnp.float32).at[:, cell_ids.reshape(-1)].add(flat)

def sample(field, weights, cell_ids):
    picked = field[:, cell_ids.reshape(-1)].reshape((field.shape[0],) + cell_ids.shape).astype(jnp.float32)
    summed = lax.optimization_barrier(jnp.sum(picked * weights[None], axis=2))
    return jnp.transpose(summed, (1, 0, 2))

def convolve_whole(field, kernel):
    channels = field.shape[0]
    taps = jnp.transpose(kernel.reshape(3, 3, 3, channels, channels), (4, 3, 0, 1, 2))
    return lax.conv_general_dilated(field[None], taps, (1, 1, 1), ((1, 1), (1, 1), (1, 1)), dimension_numbers=('NCDHW', 'OIDHW', 'NCDHW'), precision=lax.Precision.HIGHEST)[0]

def reference(point_feats, point_offsets, base_cells, block_owners, point_counts, lift_weight, conv_weight, read_weight, cotangent):
    channels = point_feats.shape[1]
    block_ids = jnp.arange(NB_TOTAL, dtype=jnp.int32)
    device_of = block_ids // NB_DEV
    row_of = device_of % N_GY
    positions = (block_ids % NB_DEV)[:, None] * BLK + jnp.arange(BLK, dtype=jnp.int32)[None, :]
    alive_pts = positions < point_counts[device_of][:, None]
    inner = (CY - 1) * (NZ - 1)
    corner_a = base_cells // inner
    corner_b = base_cells // (NZ - 1) % (CY - 1)
    corner_c = base_cells % (NZ - 1)
    along_x, along_y, along_z = corner_steps()
    owners = block_owners[:, 0]
    cell_x = (owners * CX)[:, None, None] + corner_a[:, None, :] + along_x[None, :, None]
    cell_y = (row_of * CY)[:, None, None] + corner_b[:, None, :] + along_y[None, :, None]
    cell_z = corner_c[:, None, :] + along_z[None, :, None]
    cell_ids = ((cell_x * NY + cell_y) * NZ + cell_z).astype(jnp.int32)
    cell_count = NX * NY * NZ
    masked = jnp.where(alive_pts[:, None, :], point_feats, jnp.zeros_like(point_feats))
    lifted = jnp.einsum('io,bip->bop', lift_weight.astype(jnp.float32), masked.astype(jnp.float32), precision=lax.Precision.HIGHEST).astype(jnp.bfloat16)
    weights = corner_weights(point_offsets)
    latent = spread(lifted.astype(jnp.float32), weights, cell_ids, channels, cell_count).astype(jnp.bfloat16)
    latent = latent.reshape(channels, NX, NY, NZ)
    pre_act = convolve_whole(latent.astype(jnp.float32), conv_weight.astype(jnp.float32))
    activated, gelu_back = jax.vjp(jax.nn.gelu, pre_act)
    latent_out = (latent.astype(jnp.float32) + activated).astype(jnp.bfloat16)
    sampled = sample(latent_out.reshape(channels, cell_count), weights, cell_ids).astype(jnp.bfloat16)
    prediction = jnp.einsum('c,bcp->bp', read_weight.astype(jnp.float32), sampled.astype(jnp.float32), precision=lax.Precision.HIGHEST)
    prediction = jnp.where(alive_pts, prediction, jnp.float32(0.0))
    grad_pred = jnp.where(alive_pts, cotangent, jnp.float32(0.0))
    grad_sampled = (read_weight.astype(jnp.float32)[None, :, None] * grad_pred[:, None, :]).astype(jnp.bfloat16)
    grad_out = spread(grad_sampled.astype(jnp.float32), weights, cell_ids, channels, cell_count)
    grad_out = grad_out.reshape(channels, NX, NY, NZ)
    grad_pre = gelu_back(grad_out)[0].astype(jnp.bfloat16)
    unused, conv_back = jax.vjp(convolve_whole, latent.astype(jnp.float32), conv_weight.astype(jnp.float32))
    conv_in_grad, kernel_grad = conv_back(grad_pre.astype(jnp.float32))
    grad_latent = grad_out + conv_in_grad
    grad_lifted = sample(grad_latent.reshape(channels, cell_count), weights, cell_ids).astype(jnp.bfloat16)
    feats_grad = jnp.einsum('io,bop->bip', lift_weight.astype(jnp.float32), grad_lifted.astype(jnp.float32), precision=lax.Precision.HIGHEST)
    grad_feats = jnp.where(alive_pts[:, None, :], feats_grad, jnp.float32(0.0)).astype(jnp.bfloat16)
    return (prediction, grad_feats, kernel_grad / N_GX)
```

```python
import functools

import jax
import jax.numpy as jnp
from jax import lax
from jax.experimental import pallas as pl
from jax.experimental.pallas import tpu as pltpu
from jax.sharding import PartitionSpec as P

C = 32
CX = 2
CY = 8
NZ = 256
NB = 32
BLK = 128
GX = 32
GY = 4
CAP = 2
PTS = CAP * BLK
COLS = CX * CY
TAPS = 27
MESH = pl.DeviceIdType.MESH
BF = jnp.bfloat16
F32 = jnp.float32


def dot(a, b, ca=1, cb=0):
    return lax.dot_general(a, b, (((ca,), (cb,)), ((), ())), preferred_element_type=F32)


def slots_kernel(owners, inv, slot, cnt):
    @pl.loop(0, GX)
    def _(o):
        cnt[o] = 0
        inv[CAP * o] = -1
        inv[CAP * o + 1] = -1

    @pl.loop(0, NB)
    def _(j):
        o = owners[j, 0]
        r = cnt[o]
        cnt[o] = r + 1
        s = CAP * o + r
        inv[s] = j
        slot[j] = s


def slot_tables(owners):
    smem = pl.BlockSpec(memory_space=pltpu.SMEM)
    return pl.pallas_call(
        slots_kernel,
        out_shape=(
            jax.ShapeDtypeStruct((GX * CAP,), jnp.int32),
            jax.ShapeDtypeStruct((NB,), jnp.int32),
        ),
        in_specs=[smem],
        out_specs=(smem, smem),
        scratch_shapes=[pltpu.SMEM((GX,), jnp.int32)],
    )(owners)


def shifted(values, step):
    lanes = lax.broadcasted_iota(jnp.int32, values.shape, 1)
    if step == 1:
        return jnp.where(lanes == 0, 0.0, pltpu.roll(values, 1, 1))
    return jnp.where(lanes == NZ - 1, 0.0, pltpu.roll(values, NZ - 1, 1))


def conv_pair(weights, padded, pair):
    window = padded[2 * pair : 2 * pair + 4].reshape(4 * 4 * C, NZ)
    part = dot(weights[...], window)
    return shifted(part[0:128], 1) + part[128:256] + shifted(part[256:384], -1)


def kernel(
    inv, slot, count, feats, offsets, base, cot, lift, conv, read,
    pred_out, feats_out, conv_out,
    bmat, cmat, ghi, glo, send, recv, acc, zs, planes, latp, gp, gs, wf, wb,
    gout, field, gl, predmsg, predr, gfs, gfr, redsrc, red1, red2, red3,
    s_send, s_recv, h_send, h_recv, i_send, i_recv, p_send, p_recv,
    f_send, f_recv, a_send, a_recv, b_send, b_recv, c_send, c_recv,
):
    mx = lax.axis_index("gx")
    my = lax.axis_index("gy")
    right, left = lax.rem(mx + 1, GX), lax.rem(mx + GX - 1, GX)
    up, down = lax.rem(my + 1, GY), lax.rem(my + GY - 1, GY)

    barrier = pltpu.get_barrier_semaphore()

    @pl.loop(1, GX)
    def _(k):
        pl.semaphore_signal(barrier, inc=1, device_id=(lax.rem(mx + k, GX), my), device_id_type=MESH)

    for k in range(1, GY):
        pl.semaphore_signal(barrier, inc=1, device_id=(mx, lax.rem(my + k, GY)), device_id_type=MESH)
    for px in (left, right):
        for py in (down, up):
            pl.semaphore_signal(barrier, inc=1, device_id=(px, py), device_id_type=MESH)

    cells = base[...].astype(F32)
    rows_b = jnp.floor((cells + 0.5) * (1.0 / (NZ - 1)))
    bmat[...] = rows_b
    cmat[...] = cells - rows_b * (NZ - 1.0)
    live_count = count[0]
    position = lax.broadcasted_iota(jnp.int32, (NB, BLK), 0) * BLK + lax.broadcasted_iota(
        jnp.int32, (NB, BLK), 1
    )
    grad = jnp.where(position < live_count, cot[...], 0.0)
    high = grad.astype(BF).astype(F32)
    ghi[...] = high
    glo[...] = grad - high
    lane32 = lax.broadcasted_iota(jnp.int32, (C, BLK), 1)
    sub8 = lax.broadcasted_iota(jnp.int32, (8, BLK), 0)

    def place(o):
        tails = []
        for r in range(CAP):
            j = inv[CAP * o + r]
            jj = jnp.maximum(j, 0)
            live = jnp.where(j >= 0, live_count - jj * BLK, 0)
            block = jnp.where(lane32 < live, feats[jj].astype(F32), 0.0)
            send[o, r * C : (r + 1) * C, :] = block.astype(BF)
            off = offsets[jj].astype(F32)
            here = jnp.where(j >= 0, 1.0, 0.0)
            tail = jnp.where(sub8 == 0, off[0:1], 0.0)
            tail = jnp.where(sub8 == 1, off[1:2], tail)
            tail = jnp.where(sub8 == 2, off[2:3], tail)
            tail = jnp.where(sub8 == 3, bmat[pl.ds(jj, 1), :], tail)
            tail = jnp.where(sub8 == 4, cmat[pl.ds(jj, 1), :], tail)
            tail = jnp.where(sub8 == 5, ghi[pl.ds(jj, 1), :] * here, tail)
            tail = jnp.where(sub8 == 6, glo[pl.ds(jj, 1), :] * here, tail)
            tails.append(tail)
        send[o, CAP * C : CAP * C + 16, :] = jnp.concatenate(tails, axis=0).astype(BF)

    @pl.loop(0, GX)
    def _(o):
        place(o)

    pl.semaphore_wait(barrier, GX - 1 + GY - 1 + 4)

    def points_copy(k):
        to = lax.rem(mx + k, GX)
        return pltpu.make_async_remote_copy(
            src_ref=send.at[to], dst_ref=recv.at[mx],
            send_sem=s_send.at[k], recv_sem=s_recv.at[k],
            device_id=(to, my), device_id_type=MESH,
        )

    @pl.loop(1, GX)
    def _(k):
        points_copy(k).start()

    def place_tap(xp):
        lanes = lax.broadcasted_iota(jnp.int32, (C, 128), 1)
        rows = lax.broadcasted_iota(jnp.int32, (C, 128), 0)
        return jnp.where(lanes == rows + C * xp, 1.0, 0.0).astype(BF)

    spots = [place_tap(xp) for xp in range(4)]
    wf[...] = jnp.zeros(wf.shape, BF)
    wb[...] = jnp.zeros(wb.shape, BF)
    for dz in range(3):
        for dy in range(3):
            for xo in range(2):
                tile_f = sum(
                    dot(conv[9 * dx + 3 * dy + dz], spots[dx + xo], 0, 0) for dx in range(3)
                ).astype(BF)
                tile_b = sum(
                    dot(conv[9 * (2 - dx) + 3 * (2 - dy) + (2 - dz)], spots[dx + xo])
                    for dx in range(3)
                ).astype(BF)
                for yo in range(2):
                    row = ((dz * 2 + yo) * 2 + xo) * C
                    lane = (yo + dy) * 128
                    wf[row : row + C, lane : lane + 128] = tile_f
                    wb[row : row + C, lane : lane + 128] = tile_b
    eye = jnp.where(
        lax.broadcasted_iota(jnp.int32, (C, C), 0) == lax.broadcasted_iota(jnp.int32, (C, C), 1),
        1.0, 0.0,
    )
    read_col = dot((eye * read[...].astype(F32)).astype(BF), jnp.ones((C, NZ), BF))
    lift_w = lift[...]

    sub_z = lax.broadcasted_iota(jnp.int32, (NZ, PTS), 0).astype(F32)
    sub_y = lax.broadcasted_iota(jnp.int32, (CY, PTS), 0).astype(F32)

    def spread(msg, k):
        block = jnp.concatenate([msg[0:C], msg[C : 2 * C]], axis=1)
        tail = msg[2 * C : 2 * C + 16].astype(F32)
        tail = jnp.concatenate([tail[0:8], tail[8:16]], axis=1)
        near = jnp.exp(-2.0 * tail * tail)
        far = jnp.exp(-2.0 * (tail - 1.0) * (tail - 1.0))
        at_y, at_z = tail[3:4], tail[4:5]
        slope = tail[5:6] + tail[6:7]
        wy = jnp.where(sub_y == at_y, near[1:2], jnp.where(sub_y == at_y + 1.0, far[1:2], 0.0))
        plane = (near[0:1] * wy, far[0:1] * wy)
        planes[k, 0:CY, :] = plane[0]
        planes[k, CY : 2 * CY, :] = plane[1]
        z = jnp.where(sub_z == at_z, near[2:3], jnp.where(sub_z == at_z + 1.0, far[2:3], 0.0))
        z = z.astype(BF)
        zs[k] = z
        lifted = dot(lift_w, block, 0, 0).astype(BF).astype(F32)
        rows = [
            (lifted * plane[x][y : y + 1]).astype(BF) for y in range(CY) for x in range(CX)
        ]
        rows.append(jnp.concatenate([plane[0] * slope, plane[1] * slope], axis=0).astype(BF))
        return dot(jnp.concatenate(rows, axis=0), z, 1, 1)

    acc[...] = spread(send[mx], 0)

    @pl.loop(1, GX)
    def _(k):
        points_copy(k).wait_recv()
        acc[...] += spread(recv[lax.rem(mx - k + GX, GX)], k)

    def halo_copies(buf, sends, recvs):
        ends = (
            (right, my, buf.at[1:9, 2], buf.at[1:9, 0]),
            (left, my, buf.at[1:9, 1], buf.at[1:9, 3]),
            (mx, up, buf.at[8, 1:3], buf.at[0, 1:3]),
            (mx, down, buf.at[1, 1:3], buf.at[9, 1:3]),
            (right, up, buf.at[8, 2], buf.at[0, 0]),
            (right, down, buf.at[1, 2], buf.at[9, 0]),
            (left, up, buf.at[8, 1], buf.at[0, 3]),
            (left, down, buf.at[1, 1], buf.at[9, 3]),
        )
        return [
            pltpu.make_async_remote_copy(
                src_ref=src, dst_ref=dst, send_sem=sends.at[n], recv_sem=recvs.at[n],
                device_id=(px, py), device_id_type=MESH,
            )
            for n, (px, py, src, dst) in enumerate(ends)
        ]

    def clear_ends(buf):
        @pl.when(mx == 0)
        def _():
            buf[:, 0] = jnp.zeros((10, C, NZ), BF)

        @pl.when(mx == GX - 1)
        def _():
            buf[:, 3] = jnp.zeros((10, C, NZ), BF)

        @pl.when(my == 0)
        def _():
            buf[0] = jnp.zeros((4, C, NZ), BF)

        @pl.when(my == GY - 1)
        def _():
            buf[9] = jnp.zeros((4, C, NZ), BF)

    for y in range(CY):
        for x in range(CX):
            row = (y * CX + x) * C
            latp[y + 1, x + 1] = acc[row : row + C, :].astype(BF)
    halos = halo_copies(latp, h_send, h_recv)
    for copy in halos:
        copy.start()
    for copy in halos:
        copy.wait_recv()
    for copy in halos:
        copy.wait_send()
    clear_ends(latp)

    for pair in range(4):
        pre = conv_pair(wf, latp, pair)
        cube = pre * pre
        th = jnp.tanh(0.7978845608028654 * pre * (1.0 + 0.044715 * cube))
        half = 0.5 * (1.0 + th)
        slope = half + 0.5 * pre * (1.0 - th * th) * (
            0.7978845608028654 * (1.0 + 3.0 * 0.044715 * cube)
        )
        own = latp[2 * pair + 1 : 2 * pair + 3, 1:3].reshape(4 * C, NZ).astype(F32)
        out = (own + pre * half).astype(BF).astype(F32)
        grads = []
        for yo in range(2):
            for x in range(CX):
                row = x * CY + 2 * pair + yo
                n = (yo * CX + x) * C
                field[row : row + 1, :] = jnp.sum(
                    out[n : n + C] * read_col, axis=0, keepdims=True
                )
                grads.append(read_col * acc[COLS * C + row : COLS * C + row + 1, :])
        grad_out = jnp.concatenate(grads, axis=0)
        gout[128 * pair : 128 * pair + 128, :] = grad_out
        grad_pre = (grad_out * slope).astype(BF)
        gp[2 * pair + 1 : 2 * pair + 3, 1:3] = grad_pre.reshape(2, 2, C, NZ)
        wide = grad_pre.astype(F32)
        gs[pair, 0:128, :] = shifted(wide, -1).astype(BF)
        gs[pair, 128:256, :] = grad_pre
        gs[pair, 256:384, :] = shifted(wide, 1).astype(BF)
    halos2 = halo_copies(gp, i_send, i_recv)
    for copy in halos2:
        copy.start()

    tap = jnp.zeros((4 * 4 * C, 3 * 128), F32)
    for pair in range(4):
        window = latp[2 * pair : 2 * pair + 4].reshape(4 * 4 * C, NZ)
        tap = tap + dot(window, gs[pair], 1, 1)
    quarter = lax.broadcasted_iota(jnp.int32, (C, 128), 1) // C
    quarter8 = lax.broadcasted_iota(jnp.int32, (8, 128), 1) // C
    for dx in range(3):
        for dy in range(3):
            for dz in range(3):
                total = jnp.zeros((C, 128), F32)
                for yo in range(2):
                    for xo in range(2):
                        n = ((yo + dy) * 4 + xo + dx) * C
                        piece = tap[n : n + C, dz * 128 : dz * 128 + 128]
                        total = jnp.where(quarter == 2 * yo + xo, piece, total)
                total = total + pltpu.roll(total, 64, 1)
                total = total + pltpu.roll(total, 32, 1)
                packed = total[0:8]
                for q in range(1, 4):
                    packed = jnp.where(quarter8 == q, total[8 * q : 8 * q + 8], packed)
                redsrc[9 * dx + 3 * dy + dz] = packed
    redsrc[TAPS:GX] = jnp.zeros((GX - TAPS, 8, 128), F32)

    def taps_copy(k):
        to = lax.rem(mx + k, GX)
        return pltpu.make_async_remote_copy(
            src_ref=redsrc.at[to], dst_ref=red1.at[mx],
            send_sem=a_send.at[k], recv_sem=a_recv.at[k],
            device_id=(to, my), device_id_type=MESH,
        )

    @pl.loop(1, GX)
    def _(k):
        taps_copy(k).start()

    scalar = field[...]
    scalar_hi = scalar.astype(BF)
    scalar_lo = (scalar - scalar_hi.astype(F32)).astype(BF)
    scalars = jnp.concatenate([scalar_hi, scalar_lo], axis=0)

    def read_points(k):
        got = dot(scalars, zs[k])
        total = jnp.sum((got[0:COLS] + got[COLS:]) * planes[k], axis=0, keepdims=True)
        return total[:, 0:BLK], total[:, BLK:]

    def pred_copy(k):
        to = lax.rem(mx - k + GX, GX)
        return pltpu.make_async_remote_copy(
            src_ref=predmsg.at[k], dst_ref=predr.at[mx],
            send_sem=p_send.at[k], recv_sem=p_recv.at[k],
            device_id=(to, my), device_id_type=MESH,
        )

    first, second = read_points(0)
    predr[mx, 0:1, :] = first
    predr[mx, 1:2, :] = second

    @pl.loop(1, GX)
    def _(k):
        one, two = read_points(k)
        predmsg[k, 0:1, :] = one
        predmsg[k, 1:2, :] = two
        predmsg[k, 2:8, :] = jnp.zeros((6, BLK), F32)
        pred_copy(k).start()

    for copy in halos2:
        copy.wait_recv()
    for copy in halos2:
        copy.wait_send()
    clear_ends(gp)
    for pair in range(4):
        back = conv_pair(wb, gp, pair)
        gl[128 * pair : 128 * pair + 128, :] = (
            gout[128 * pair : 128 * pair + 128, :] + back
        ).astype(BF)

    red1[mx] = redsrc[mx]

    @pl.loop(1, GX)
    def _(k):
        taps_copy(k).wait_recv()

    red2[my] = jnp.sum(red1[...], axis=0)

    def rows_copy(k):
        return pltpu.make_async_remote_copy(
            src_ref=red2.at[my], dst_ref=red2.at[my],
            send_sem=b_send.at[k], recv_sem=b_recv.at[k],
            device_id=(mx, lax.rem(my + k, GY)), device_id_type=MESH,
        )

    for k in range(1, GY):
        rows_copy(k).start()

    def gather(k):
        got = dot(gl[...], zs[k])
        total = jnp.zeros((C, PTS), F32)
        for y in range(CY):
            for x in range(CX):
                n = (y * CX + x) * C
                total = total + got[n : n + C] * planes[k, x * CY + y : x * CY + y + 1, :]
        back = dot(lift_w, total.astype(BF)).astype(BF)
        return back[:, 0:BLK], back[:, BLK:]

    def feats_copy(k):
        to = lax.rem(mx - k + GX, GX)
        return pltpu.make_async_remote_copy(
            src_ref=gfs.at[k], dst_ref=gfr.at[pl.ds(CAP * mx, CAP)],
            send_sem=f_send.at[k], recv_sem=f_recv.at[k],
            device_id=(to, my), device_id_type=MESH,
        )

    def send_back(k):
        one, two = gather(k)
        gfs[k, 0] = one
        gfs[k, 1] = two
        feats_copy(k).start()

    @pl.loop(1, 12)
    def _(k):
        send_back(k)

    for k in range(1, GY):
        rows_copy(k).wait_recv()
    for k in range(1, GY):
        rows_copy(k).wait_send()
    red3[mx] = (red2[0] + red2[1] + red2[2] + red2[3]) * (1.0 / GX)

    def total_copy(k):
        to = lax.rem(mx + k, GX)
        return pltpu.make_async_remote_copy(
            src_ref=red3.at[mx], dst_ref=red3.at[mx],
            send_sem=c_send.at[k], recv_sem=c_recv.at[k],
            device_id=(to, my), device_id_type=MESH,
        )

    @pl.loop(1, GX)
    def _(k):
        total_copy(k).start()

    @pl.loop(12, GX)
    def _(k):
        send_back(k)

    first_gf, second_gf = gather(0)
    gfr[CAP * mx] = first_gf
    gfr[CAP * mx + 1] = second_gf

    @pl.loop(1, GX)
    def _(k):
        pred_copy(k).wait_recv()
        total_copy(k).wait_recv()

    for d in range(TAPS):
        packed = red3[d]
        for q in range(4):
            piece = packed if q == 0 else pltpu.roll(packed, 128 - C * q, 1)
            conv_out[d, 8 * q : 8 * q + 8, :] = piece[:, 0:C]

    @pl.loop(1, GX)
    def _(k):
        feats_copy(k).wait_recv()

    lane1 = lax.broadcasted_iota(jnp.int32, (1, BLK), 1)

    @pl.loop(0, NB)
    def _(j):
        s = slot[j]
        live = live_count - j * BLK
        feats_out[j] = jnp.where(lane32 < live, gfr[s].astype(F32), 0.0).astype(BF)
        both = predr[s // CAP]
        value = jnp.where(lax.rem(s, CAP) == 0, both[0:1], both[1:2])
        pred_out[pl.ds(j, 1), :] = jnp.where(lane1 < live, value, 0.0)

    @pl.loop(1, GX)
    def _(k):
        points_copy(k).wait_send()
        taps_copy(k).wait_send()
        pred_copy(k).wait_send()
        feats_copy(k).wait_send()
        total_copy(k).wait_send()


def local(
    point_feats, point_offsets, base_cells, block_owners, point_counts,
    lift_weight, conv_weight, read_weight, cotangent,
):
    inv, slot = slot_tables(block_owners)
    smem = pl.BlockSpec(memory_space=pltpu.SMEM)
    vmem = pl.BlockSpec(memory_space=pltpu.VMEM)
    dma = pltpu.SemaphoreType.DMA
    return pl.pallas_call(
        kernel,
        out_shape=(
            jax.ShapeDtypeStruct((NB, BLK), F32),
            jax.ShapeDtypeStruct((NB, C, BLK), BF),
            jax.ShapeDtypeStruct((TAPS, C, C), F32),
        ),
        in_specs=[smem, smem, smem] + [vmem] * 7,
        out_specs=(vmem, vmem, vmem),
        scratch_shapes=[
            pltpu.VMEM((NB, BLK), F32),
            pltpu.VMEM((NB, BLK), F32),
            pltpu.VMEM((NB, BLK), F32),
            pltpu.VMEM((NB, BLK), F32),
            pltpu.VMEM((GX, CAP * C + 16, BLK), BF),
            pltpu.VMEM((GX, CAP * C + 16, BLK), BF),
            pltpu.VMEM((COLS * C + COLS, NZ), F32),
            pltpu.VMEM((GX, NZ, PTS), BF),
            pltpu.VMEM((GX, COLS, PTS), F32),
            pltpu.VMEM((10, 4, C, NZ), BF),
            pltpu.VMEM((10, 4, C, NZ), BF),
            pltpu.VMEM((4, 3 * 128, NZ), BF),
            pltpu.VMEM((3 * 128, 512), BF),
            pltpu.VMEM((3 * 128, 512), BF),
            pltpu.VMEM((COLS * C, NZ), F32),
            pltpu.VMEM((COLS, NZ), F32),
            pltpu.VMEM((COLS * C, NZ), BF),
            pltpu.VMEM((GX, 8, BLK), F32),
            pltpu.VMEM((GX, 8, BLK), F32),
            pltpu.VMEM((GX, CAP, C, BLK), BF),
            pltpu.VMEM((GX * CAP, C, BLK), BF),
            pltpu.VMEM((GX, 8, 128), F32),
            pltpu.VMEM((GX, 8, 128), F32),
            pltpu.VMEM((GY, 8, 128), F32),
            pltpu.VMEM((GX, 8, 128), F32),
            dma((GX,)), dma((GX,)), dma((8,)), dma((8,)), dma((8,)), dma((8,)),
            dma((GX,)), dma((GX,)), dma((GX,)), dma((GX,)), dma((GX,)), dma((GX,)),
            dma((GY,)), dma((GY,)), dma((GX,)), dma((GX,)),
        ],
        compiler_params=pltpu.CompilerParams(
            collective_id=0, has_side_effects=True, vmem_limit_bytes=40 * 1024 * 1024
        ),
        cost_estimate=pl.CostEstimate(
            flops=8_000_000_000, bytes_accessed=2_000_000, transcendentals=1_000_000
        ),
    )(
        inv, slot, point_counts, point_feats, point_offsets, base_cells, cotangent,
        lift_weight, conv_weight, read_weight.reshape(1, C),
    )


def solution(mesh):
    in_specs = (
        P(("gx", "gy"), None, None),
        P(("gx", "gy"), None, None),
        P(("gx", "gy"), None),
        P(("gx", "gy"), None),
        P(("gx", "gy")),
        P(),
        P(),
        P(),
        P(("gx", "gy"), None),
    )
    out_specs = (P(("gx", "gy"), None), P(("gx", "gy"), None, None), P())
    return jax.shard_map(local, mesh=mesh, in_specs=in_specs, out_specs=out_specs, check_vma=False)
```

```python
import functools

import jax
import jax.numpy as jnp
from jax import lax
from jax.experimental import pallas as pl
from jax.experimental.pallas import tpu as pltpu
from jax.sharding import PartitionSpec as P

C = 32
CX = 2
CY = 8
NZ = 256
NB = 32
BLK = 128
GX = 32
GY = 4
CAP = 2
PTS = CAP * BLK
GROUP = 4
GROUPS = GX // GROUP
WIDE = GROUP * PTS
COLS = CX * CY
TAPS = 27
MESH = pl.DeviceIdType.MESH
BF = jnp.bfloat16
F32 = jnp.float32


def dot(a, b, ca=1, cb=0):
    return lax.dot_general(a, b, (((ca,), (cb,)), ((), ())), preferred_element_type=F32)


def shifted(values, step):
    lanes = lax.broadcasted_iota(jnp.int32, values.shape, 1)
    if step == 1:
        return jnp.where(lanes == 0, 0.0, pltpu.roll(values, 1, 1))
    return jnp.where(lanes == NZ - 1, 0.0, pltpu.roll(values, NZ - 1, 1))


def conv_pair(weights, padded, pair):
    window = padded[2 * pair : 2 * pair + 4].reshape(4 * 4 * C, NZ)
    part = dot(weights[...], window)
    return shifted(part[0:128], 1) + part[128:256] + shifted(part[256:384], -1)


def kernel(
    feats_hbm, offsets_hbm, base_hbm, owners_hbm, count_hbm, lift_hbm, conv_hbm, read_hbm, cot_hbm,
    pred_out, feats_out, conv_out,
    feats, offsets, base, owners, count, lift, conv, read, cot, table, slots, aux, in_sem, send, recv, acc, zs, planes, latp, gp, gs, wf, wb,
    gout, field, gl, predmsg, predr, gfs, gfr, redsrc, red1, red2, red3,
    s_send, s_recv, h_send, h_recv, i_send, i_recv, p_send, p_recv,
    f_send, f_recv, a_send, a_recv, b_send, b_recv, c_send, c_recv,
):
    mx = lax.axis_index("gx")
    my = lax.axis_index("gy")
    right, left = lax.rem(mx + 1, GX), lax.rem(mx + GX - 1, GX)
    up, down = lax.rem(my + 1, GY), lax.rem(my + GY - 1, GY)

    pairs = {
        "owners": (owners_hbm, owners), "offsets": (offsets_hbm, offsets), "base": (base_hbm, base),
        "count": (count_hbm, count), "cot": (cot_hbm, cot), "feats": (feats_hbm, feats),
        "lift": (lift_hbm, lift), "conv": (conv_hbm, conv), "read": (read_hbm, read),
    }
    fetched = {
        name: pltpu.make_async_copy(src, dst, in_sem.at[n])
        for n, (name, (src, dst)) in enumerate(pairs.items())
    }
    for copy in fetched.values():
        copy.start()

    barrier = pltpu.get_barrier_semaphore()

    @pl.loop(1, GX)
    def _(k):
        pl.semaphore_signal(barrier, inc=1, device_id=(lax.rem(mx + k, GX), my), device_id_type=MESH)

    for k in range(1, GY):
        pl.semaphore_signal(barrier, inc=1, device_id=(mx, lax.rem(my + k, GY)), device_id_type=MESH)
    for px in (left, right):
        for py in (down, up):
            pl.semaphore_signal(barrier, inc=1, device_id=(px, py), device_id_type=MESH)

    fetched["owners"].wait()
    named = owners[...]
    rows32 = lax.broadcasted_iota(jnp.int32, (NB, NB), 0)
    lanes32 = lax.broadcasted_iota(jnp.int32, (NB, NB), 1)
    named_col = jnp.sum(jnp.where(rows32 == lanes32, named, 0), axis=1, keepdims=True)
    earlier = (named_col == named) & (rows32 < lanes32)
    slot_row = CAP * named + jnp.sum(jnp.where(earlier, 1, 0), axis=0, keepdims=True)
    slot_col = jnp.sum(jnp.where(rows32 == lanes32, slot_row, 0), axis=1, keepdims=True)
    rows = lax.broadcasted_iota(jnp.int32, (NB, BLK), 0)
    lanes = lax.broadcasted_iota(jnp.int32, (NB, BLK), 1)
    table[0:1, :] = jnp.sum(jnp.where(slot_col == lanes, rows + 1, 0), axis=0, keepdims=True) - 1
    table[1:2, :] = jnp.sum(jnp.where(rows == lanes, slot_col, 0), axis=0, keepdims=True)
    table[2:8, :] = jnp.zeros((6, BLK), jnp.int32)
    to_slots = pltpu.make_async_copy(table, slots, in_sem.at[9])
    to_slots.start()

    for name in ("offsets", "base", "count", "cot"):
        fetched[name].wait()
    cells = base[...].astype(F32)
    cell_y = jnp.floor((cells + 0.5) * (1.0 / (NZ - 1)))
    alive = jnp.where(rows * BLK + lanes < count[...], 1.0, 0.0)
    grad = cot[...] * alive
    high = grad.astype(BF).astype(F32)
    tile_rows = [offsets[n].astype(F32) for n in range(3)]
    tile_rows += [cell_y, cells - cell_y * (NZ - 1.0), high, grad - high, alive]
    for n, value in enumerate(tile_rows):
        aux[:, n, :] = value
    fetched["feats"].wait()
    to_slots.wait()

    def place(o):
        tails = []
        for r in range(CAP):
            j = slots[0, CAP * o + r]
            jj = jnp.maximum(j, 0)
            here = jnp.where(j >= 0, 1.0, 0.0)
            tail = aux[jj] * here
            send[o, r * C : (r + 1) * C, :] = (feats[jj].astype(F32) * tail[7:8]).astype(BF)
            tails.append(tail)
        send[o, CAP * C : CAP * C + 16, :] = jnp.concatenate(tails, axis=0).astype(BF)

    def points_copy(k):
        to = lax.rem(mx + k, GX)
        return pltpu.make_async_remote_copy(
            src_ref=send.at[to], dst_ref=recv.at[mx],
            send_sem=s_send.at[k], recv_sem=s_recv.at[k],
            device_id=(to, my), device_id_type=MESH,
        )

    pl.semaphore_wait(barrier, GX - 1 + GY - 1 + 4)

    @pl.loop(1, GX)
    def _(k):
        place(lax.rem(mx + k, GX))
        points_copy(k).start()

    place(mx)
    recv[mx] = send[mx]

    for name in ("lift", "conv", "read"):
        fetched[name].wait()
    def place_tap(xp):
        lanes = lax.broadcasted_iota(jnp.int32, (C, 128), 1)
        rows = lax.broadcasted_iota(jnp.int32, (C, 128), 0)
        return jnp.where(lanes == rows + C * xp, 1.0, 0.0).astype(BF)

    spots = [place_tap(xp) for xp in range(4)]
    wf[...] = jnp.zeros(wf.shape, BF)
    wb[...] = jnp.zeros(wb.shape, BF)
    for dz in range(3):
        for dy in range(3):
            for xo in range(2):
                tile_f = sum(
                    dot(conv[9 * dx + 3 * dy + dz], spots[dx + xo], 0, 0) for dx in range(3)
                ).astype(BF)
                tile_b = sum(
                    dot(conv[9 * (2 - dx) + 3 * (2 - dy) + (2 - dz)], spots[dx + xo])
                    for dx in range(3)
                ).astype(BF)
                for yo in range(2):
                    row = ((dz * 2 + yo) * 2 + xo) * C
                    lane = (yo + dy) * 128
                    wf[row : row + C, lane : lane + 128] = tile_f
                    wb[row : row + C, lane : lane + 128] = tile_b
    eye = jnp.where(
        lax.broadcasted_iota(jnp.int32, (C, C), 0) == lax.broadcasted_iota(jnp.int32, (C, C), 1),
        1.0, 0.0,
    )
    read_col = dot((eye * read[...].astype(F32)).astype(BF), jnp.ones((C, NZ), BF))
    lift_w = lift[...]

    sub_z = lax.broadcasted_iota(jnp.int32, (NZ, WIDE), 0).astype(F32)
    sub_y = lax.broadcasted_iota(jnp.int32, (CY, WIDE), 0).astype(F32)
    acc[...] = jnp.zeros(acc.shape, F32)

    @pl.loop(0, GROUPS)
    def _(g):
        blocks, tails = [], []
        for n in range(GROUP):
            k = GROUP * g + n
            if n == 0:

                @pl.when(g > 0)
                def _():
                    points_copy(GROUP * g).wait_recv()

            else:
                points_copy(k).wait_recv()
        for n in range(GROUP):
            msg = recv[lax.rem(mx - (GROUP * g + n) + GX, GX)]
            blocks += [msg[0:C], msg[C : 2 * C]]
            tail = msg[2 * C : 2 * C + 16].astype(F32)
            tails += [tail[0:8], tail[8:16]]
        block = jnp.concatenate(blocks, axis=1)
        tail = jnp.concatenate(tails, axis=1)
        near = jnp.exp(-2.0 * tail * tail)
        far = jnp.exp(-2.0 * (tail - 1.0) * (tail - 1.0))
        at_y, at_z = tail[3:4], tail[4:5]
        slope = tail[5:6] + tail[6:7]
        wy = jnp.where(sub_y == at_y, near[1:2], jnp.where(sub_y == at_y + 1.0, far[1:2], 0.0))
        plane = (near[0:1] * wy, far[0:1] * wy)
        planes[g, 0:CY, :] = plane[0]
        planes[g, CY : 2 * CY, :] = plane[1]
        z = jnp.where(sub_z == at_z, near[2:3], jnp.where(sub_z == at_z + 1.0, far[2:3], 0.0))
        z = z.astype(BF)
        zs[g] = z
        lifted = dot(lift_w, block, 0, 0).astype(BF).astype(F32)
        rows = [
            (lifted * plane[x][y : y + 1]).astype(BF) for y in range(CY) for x in range(CX)
        ]
        rows.append(jnp.concatenate([plane[0] * slope, plane[1] * slope], axis=0).astype(BF))
        acc[...] += dot(jnp.concatenate(rows, axis=0), z, 1, 1)

    def halo_copies(buf, sends, recvs):
        ends = (
            (right, my, buf.at[1:9, 2], buf.at[1:9, 0]),
            (left, my, buf.at[1:9, 1], buf.at[1:9, 3]),
            (mx, up, buf.at[8, 1:3], buf.at[0, 1:3]),
            (mx, down, buf.at[1, 1:3], buf.at[9, 1:3]),
            (right, up, buf.at[8, 2], buf.at[0, 0]),
            (right, down, buf.at[1, 2], buf.at[9, 0]),
            (left, up, buf.at[8, 1], buf.at[0, 3]),
            (left, down, buf.at[1, 1], buf.at[9, 3]),
        )
        return [
            pltpu.make_async_remote_copy(
                src_ref=src, dst_ref=dst, send_sem=sends.at[n], recv_sem=recvs.at[n],
                device_id=(px, py), device_id_type=MESH,
            )
            for n, (px, py, src, dst) in enumerate(ends)
        ]

    def clear_ends(buf):
        @pl.when(mx == 0)
        def _():
            buf[:, 0] = jnp.zeros((10, C, NZ), BF)

        @pl.when(mx == GX - 1)
        def _():
            buf[:, 3] = jnp.zeros((10, C, NZ), BF)

        @pl.when(my == 0)
        def _():
            buf[0] = jnp.zeros((4, C, NZ), BF)

        @pl.when(my == GY - 1)
        def _():
            buf[9] = jnp.zeros((4, C, NZ), BF)

    for y in range(CY):
        for x in range(CX):
            row = (y * CX + x) * C
            latp[y + 1, x + 1] = acc[row : row + C, :].astype(BF)
    halos = halo_copies(latp, h_send, h_recv)
    for copy in halos:
        copy.start()
    for copy in halos:
        copy.wait_recv()
    for copy in halos:
        copy.wait_send()
    clear_ends(latp)

    for pair in range(4):
        pre = conv_pair(wf, latp, pair)
        cube = pre * pre
        th = jnp.tanh(0.7978845608028654 * pre * (1.0 + 0.044715 * cube))
        half = 0.5 * (1.0 + th)
        slope = half + 0.5 * pre * (1.0 - th * th) * (
            0.7978845608028654 * (1.0 + 3.0 * 0.044715 * cube)
        )
        own = latp[2 * pair + 1 : 2 * pair + 3, 1:3].reshape(4 * C, NZ).astype(F32)
        out = (own + pre * half).astype(BF).astype(F32)
        grads = []
        for yo in range(2):
            for x in range(CX):
                row = x * CY + 2 * pair + yo
                n = (yo * CX + x) * C
                field[row : row + 1, :] = jnp.sum(
                    out[n : n + C] * read_col, axis=0, keepdims=True
                )
                grads.append(read_col * acc[COLS * C + row : COLS * C + row + 1, :])
        grad_out = jnp.concatenate(grads, axis=0)
        gout[128 * pair : 128 * pair + 128, :] = grad_out
        grad_pre = (grad_out * slope).astype(BF)
        gp[2 * pair + 1 : 2 * pair + 3, 1:3] = grad_pre.reshape(2, 2, C, NZ)
        wide = grad_pre.astype(F32)
        gs[pair, 0:128, :] = shifted(wide, -1).astype(BF)
        gs[pair, 128:256, :] = grad_pre
        gs[pair, 256:384, :] = shifted(wide, 1).astype(BF)
    halos2 = halo_copies(gp, i_send, i_recv)
    for copy in halos2:
        copy.start()

    tap = jnp.zeros((4 * 4 * C, 3 * 128), F32)
    for pair in range(4):
        window = latp[2 * pair : 2 * pair + 4].reshape(4 * 4 * C, NZ)
        tap = tap + dot(window, gs[pair], 1, 1)
    quarter = lax.broadcasted_iota(jnp.int32, (C, 128), 1) // C
    quarter8 = lax.broadcasted_iota(jnp.int32, (8, 128), 1) // C
    for dx in range(3):
        for dy in range(3):
            for dz in range(3):
                total = jnp.zeros((C, 128), F32)
                for yo in range(2):
                    for xo in range(2):
                        n = ((yo + dy) * 4 + xo + dx) * C
                        piece = tap[n : n + C, dz * 128 : dz * 128 + 128]
                        total = jnp.where(quarter == 2 * yo + xo, piece, total)
                total = total + pltpu.roll(total, 64, 1)
                total = total + pltpu.roll(total, 32, 1)
                packed = total[0:8]
                for q in range(1, 4):
                    packed = jnp.where(quarter8 == q, total[8 * q : 8 * q + 8], packed)
                redsrc[9 * dx + 3 * dy + dz] = packed
    redsrc[TAPS:GX] = jnp.zeros((GX - TAPS, 8, 128), F32)

    def taps_copy(k):
        to = lax.rem(mx + k, GX)
        return pltpu.make_async_remote_copy(
            src_ref=redsrc.at[to], dst_ref=red1.at[mx],
            send_sem=a_send.at[k], recv_sem=a_recv.at[k],
            device_id=(to, my), device_id_type=MESH,
        )

    @pl.loop(1, GX)
    def _(k):
        taps_copy(k).start()

    scalar = field[...]
    scalar_hi = scalar.astype(BF)
    scalar_lo = (scalar - scalar_hi.astype(F32)).astype(BF)
    scalars = jnp.concatenate([scalar_hi, scalar_lo], axis=0)

    def pred_copy(k):
        to = lax.rem(mx - k + GX, GX)
        return pltpu.make_async_remote_copy(
            src_ref=predmsg.at[k], dst_ref=predr.at[mx],
            send_sem=p_send.at[k], recv_sem=p_recv.at[k],
            device_id=(to, my), device_id_type=MESH,
        )

    @pl.loop(0, GROUPS)
    def _(g):
        got = dot(scalars, zs[g])
        total = jnp.sum((got[0:COLS] + got[COLS:]) * planes[g], axis=0, keepdims=True)
        for n in range(GROUP):
            k = GROUP * g + n
            for r in range(CAP):
                lane = n * PTS + r * BLK
                predmsg[k, r : r + 1, :] = total[:, lane : lane + BLK]
            predmsg[k, CAP:8, :] = jnp.zeros((8 - CAP, BLK), F32)
            if n == 0:

                @pl.when(g > 0)
                def _():
                    pred_copy(GROUP * g).start()

            else:
                pred_copy(k).start()

    predr[mx] = predmsg[0]

    for copy in halos2:
        copy.wait_recv()
    for copy in halos2:
        copy.wait_send()
    clear_ends(gp)
    for pair in range(4):
        back = conv_pair(wb, gp, pair)
        gl[128 * pair : 128 * pair + 128, :] = (
            gout[128 * pair : 128 * pair + 128, :] + back
        ).astype(BF)

    red1[mx] = redsrc[mx]

    @pl.loop(1, GX)
    def _(k):
        taps_copy(k).wait_recv()

    red2[my] = jnp.sum(red1[...], axis=0)

    def rows_copy(k):
        return pltpu.make_async_remote_copy(
            src_ref=red2.at[my], dst_ref=red2.at[my],
            send_sem=b_send.at[k], recv_sem=b_recv.at[k],
            device_id=(mx, lax.rem(my + k, GY)), device_id_type=MESH,
        )

    for k in range(1, GY):
        rows_copy(k).start()

    def feats_copy(k):
        to = lax.rem(mx - k + GX, GX)
        return pltpu.make_async_remote_copy(
            src_ref=gfs.at[k], dst_ref=gfr.at[pl.ds(CAP * mx, CAP)],
            send_sem=f_send.at[k], recv_sem=f_recv.at[k],
            device_id=(to, my), device_id_type=MESH,
        )

    def send_back(g):
        got = dot(gl[...], zs[g])
        total = jnp.zeros((C, WIDE), F32)
        for y in range(CY):
            for x in range(CX):
                n = (y * CX + x) * C
                total = total + got[n : n + C] * planes[g, x * CY + y : x * CY + y + 1, :]
        back = dot(lift_w, total.astype(BF)).astype(BF)
        for n in range(GROUP):
            k = GROUP * g + n
            for r in range(CAP):
                lane = n * PTS + r * BLK
                gfs[k, r] = back[:, lane : lane + BLK]
            if n == 0:

                @pl.when(g > 0)
                def _():
                    feats_copy(GROUP * g).start()

            else:
                feats_copy(k).start()

    @pl.loop(1, 4)
    def _(g):
        send_back(g)

    for k in range(1, GY):
        rows_copy(k).wait_recv()
    for k in range(1, GY):
        rows_copy(k).wait_send()
    red3[mx] = (red2[0] + red2[1] + red2[2] + red2[3]) * (1.0 / GX)

    def total_copy(k):
        to = lax.rem(mx + k, GX)
        return pltpu.make_async_remote_copy(
            src_ref=red3.at[mx], dst_ref=red3.at[mx],
            send_sem=c_send.at[k], recv_sem=c_recv.at[k],
            device_id=(to, my), device_id_type=MESH,
        )

    @pl.loop(1, GX)
    def _(k):
        total_copy(k).start()

    @pl.loop(4, GROUPS + 1)
    def _(g):
        send_back(lax.rem(g, GROUPS))

    gfr[pl.ds(CAP * mx, CAP)] = gfs[0]

    @pl.loop(1, GX)
    def _(k):
        pred_copy(k).wait_recv()
        total_copy(k).wait_recv()

    for d in range(TAPS):
        packed = red3[d]
        for q in range(4):
            piece = packed if q == 0 else pltpu.roll(packed, 128 - C * q, 1)
            conv_out[d, 8 * q : 8 * q + 8, :] = piece[:, 0:C]

    @pl.loop(1, GX)
    def _(k):
        feats_copy(k).wait_recv()

    @pl.loop(0, NB)
    def _(j):
        s = slots[1, j]
        keep = aux[j, 7:8, :]
        feats_out[j] = (gfr[s].astype(F32) * keep).astype(BF)
        both = predr[s // CAP]
        value = jnp.where(lax.rem(s, CAP) == 0, both[0:1], both[1:2])
        pred_out[pl.ds(j, 1), :] = value * keep

    @pl.loop(1, GX)
    def _(k):
        points_copy(k).wait_send()
        taps_copy(k).wait_send()
        pred_copy(k).wait_send()
        feats_copy(k).wait_send()
        total_copy(k).wait_send()


def local(
    point_feats, point_offsets, base_cells, block_owners, point_counts,
    lift_weight, conv_weight, read_weight, cotangent,
):
    hbm = pl.BlockSpec(memory_space=pltpu.HBM)
    vmem = pl.BlockSpec(memory_space=pltpu.VMEM)
    dma = pltpu.SemaphoreType.DMA
    return pl.pallas_call(
        kernel,
        out_shape=(
            jax.ShapeDtypeStruct((NB, BLK), F32),
            jax.ShapeDtypeStruct((NB, C, BLK), BF),
            jax.ShapeDtypeStruct((TAPS, C, C), F32),
        ),
        in_specs=[hbm] * 9,
        out_specs=(vmem, vmem, vmem),
        scratch_shapes=[
            pltpu.VMEM((NB, C, BLK), BF),
            pltpu.VMEM((3, NB, BLK), BF),
            pltpu.VMEM((NB, BLK), jnp.int32),
            pltpu.VMEM((1, NB), jnp.int32),
            pltpu.VMEM((1, 1), jnp.int32),
            pltpu.VMEM((C, C), BF),
            pltpu.VMEM((TAPS, C, C), BF),
            pltpu.VMEM((1, C), BF),
            pltpu.VMEM((NB, BLK), F32),
            pltpu.VMEM((8, BLK), jnp.int32),
            pltpu.SMEM((8, BLK), jnp.int32),
            pltpu.VMEM((NB, 8, BLK), F32),
            dma((10,)),
            pltpu.VMEM((GX, CAP * C + 16, BLK), BF),
            pltpu.VMEM((GX, CAP * C + 16, BLK), BF),
            pltpu.VMEM((COLS * C + COLS, NZ), F32),
            pltpu.VMEM((GROUPS, NZ, WIDE), BF),
            pltpu.VMEM((GROUPS, COLS, WIDE), F32),
            pltpu.VMEM((10, 4, C, NZ), BF),
            pltpu.VMEM((10, 4, C, NZ), BF),
            pltpu.VMEM((4, 3 * 128, NZ), BF),
            pltpu.VMEM((3 * 128, 512), BF),
            pltpu.VMEM((3 * 128, 512), BF),
            pltpu.VMEM((COLS * C, NZ), F32),
            pltpu.VMEM((COLS, NZ), F32),
            pltpu.VMEM((COLS * C, NZ), BF),
            pltpu.VMEM((GX, 8, BLK), F32),
            pltpu.VMEM((GX, 8, BLK), F32),
            pltpu.VMEM((GX, CAP, C, BLK), BF),
            pltpu.VMEM((GX * CAP, C, BLK), BF),
            pltpu.VMEM((GX, 8, 128), F32),
            pltpu.VMEM((GX, 8, 128), F32),
            pltpu.VMEM((GY, 8, 128), F32),
            pltpu.VMEM((GX, 8, 128), F32),
            dma((GX,)), dma((GX,)), dma((8,)), dma((8,)), dma((8,)), dma((8,)),
            dma((GX,)), dma((GX,)), dma((GX,)), dma((GX,)), dma((GX,)), dma((GX,)),
            dma((GY,)), dma((GY,)), dma((GX,)), dma((GX,)),
        ],
        compiler_params=pltpu.CompilerParams(
            collective_id=0, has_side_effects=True, vmem_limit_bytes=63 * 1024 * 1024
        ),
        cost_estimate=pl.CostEstimate(
            flops=8_000_000_000, bytes_accessed=2_000_000, transcendentals=1_000_000
        ),
    )(
        point_feats, jnp.transpose(point_offsets, (1, 0, 2)), base_cells,
        block_owners.reshape(1, NB), point_counts.reshape(1, 1), lift_weight, conv_weight,
        read_weight.reshape(1, C), cotangent,
    )


def solution(mesh):
    in_specs = (
        P(("gx", "gy"), None, None),
        P(("gx", "gy"), None, None),
        P(("gx", "gy"), None),
        P(("gx", "gy"), None),
        P(("gx", "gy")),
        P(),
        P(),
        P(),
        P(("gx", "gy"), None),
    )
    out_specs = (P(("gx", "gy"), None), P(("gx", "gy"), None, None), P())
    return jax.shard_map(local, mesh=mesh, in_specs=in_specs, out_specs=out_specs, check_vma=False)
```

```python
import functools

import jax
import jax.numpy as jnp
from jax import lax
from jax.experimental import pallas as pl
from jax.experimental.pallas import tpu as pltpu
from jax.sharding import PartitionSpec as P

C = 32
CX = 2
CY = 8
NZ = 256
NB = 32
BLK = 128
GX = 32
GY = 4
CAP = 2
PTS = CAP * BLK
GROUP = 4
GROUPS = GX // GROUP
WIDE = GROUP * PTS
COLS = CX * CY
TAPS = 27
MESH = pl.DeviceIdType.MESH
BF = jnp.bfloat16
F32 = jnp.float32


def dot(a, b, ca=1, cb=0):
    return lax.dot_general(a, b, (((ca,), (cb,)), ((), ())), preferred_element_type=F32)


def shifted(values, step):
    lanes = lax.broadcasted_iota(jnp.int32, values.shape, 1)
    if step == 1:
        return jnp.where(lanes == 0, 0.0, pltpu.roll(values, 1, 1))
    return jnp.where(lanes == NZ - 1, 0.0, pltpu.roll(values, NZ - 1, 1))


def conv_pair(weights, padded, pair):
    window = padded[2 * pair : 2 * pair + 4].reshape(4 * 4 * C, NZ)
    part = dot(weights[...], window)
    return shifted(part[0:128], 1) + part[128:256] + shifted(part[256:384], -1)


def kernel(
    feats_hbm, offsets_hbm, base_hbm, owners_hbm, count_hbm, lift_hbm, conv_hbm, read_hbm, cot_hbm,
    gfr, predr, red3, alive_out, table,
    feats, offsets, base, owners, count, lift, conv, read, cot, slots, aux, in_sem, send, recv, acc, zs, planes, latp, gp, gs, wf, wb,
    gout, field, gl, predmsg, gfs, redsrc, red1, red2,
    s_send, s_recv, h_send, h_recv, i_send, i_recv, p_send, p_recv,
    f_send, f_recv, a_send, a_recv, b_send, b_recv, c_send, c_recv,
):
    mx = lax.axis_index("gx")
    my = lax.axis_index("gy")
    right, left = lax.rem(mx + 1, GX), lax.rem(mx + GX - 1, GX)
    up, down = lax.rem(my + 1, GY), lax.rem(my + GY - 1, GY)

    pairs = {
        "owners": (owners_hbm, owners), "offsets": (offsets_hbm, offsets), "base": (base_hbm, base),
        "count": (count_hbm, count), "cot": (cot_hbm, cot), "feats": (feats_hbm, feats),
        "lift": (lift_hbm, lift), "conv": (conv_hbm, conv), "read": (read_hbm, read),
    }
    fetched = {
        name: pltpu.make_async_copy(src, dst, in_sem.at[n])
        for n, (name, (src, dst)) in enumerate(pairs.items())
    }
    for copy in fetched.values():
        copy.start()

    barrier = pltpu.get_barrier_semaphore()

    @pl.loop(1, GX)
    def _(k):
        pl.semaphore_signal(barrier, inc=1, device_id=(lax.rem(mx + k, GX), my), device_id_type=MESH)

    for k in range(1, GY):
        pl.semaphore_signal(barrier, inc=1, device_id=(mx, lax.rem(my + k, GY)), device_id_type=MESH)
    for px in (left, right):
        for py in (down, up):
            pl.semaphore_signal(barrier, inc=1, device_id=(px, py), device_id_type=MESH)

    fetched["owners"].wait()
    named = owners[...]
    rows32 = lax.broadcasted_iota(jnp.int32, (NB, NB), 0)
    lanes32 = lax.broadcasted_iota(jnp.int32, (NB, NB), 1)
    named_col = jnp.sum(jnp.where(rows32 == lanes32, named, 0), axis=1, keepdims=True)
    earlier = (named_col == named) & (rows32 < lanes32)
    slot_row = CAP * named + jnp.sum(jnp.where(earlier, 1, 0), axis=0, keepdims=True)
    slot_col = jnp.sum(jnp.where(rows32 == lanes32, slot_row, 0), axis=1, keepdims=True)
    rows = lax.broadcasted_iota(jnp.int32, (NB, BLK), 0)
    lanes = lax.broadcasted_iota(jnp.int32, (NB, BLK), 1)
    table[0:1, :] = jnp.sum(jnp.where(slot_col == lanes, rows + 1, 0), axis=0, keepdims=True) - 1
    table[1:2, :] = jnp.sum(jnp.where(rows == lanes, slot_col, 0), axis=0, keepdims=True)
    table[2:8, :] = jnp.zeros((6, BLK), jnp.int32)
    to_slots = pltpu.make_async_copy(table, slots, in_sem.at[9])
    to_slots.start()

    for name in ("offsets", "base", "count", "cot"):
        fetched[name].wait()
    cells = base[...].astype(F32)
    cell_y = jnp.floor((cells + 0.5) * (1.0 / (NZ - 1)))
    alive = jnp.where(rows * BLK + lanes < count[...], 1.0, 0.0)
    alive_out[...] = alive
    grad = cot[...] * alive
    high = grad.astype(BF).astype(F32)
    tile_rows = [offsets[n].astype(F32) for n in range(3)]
    tile_rows += [cell_y, cells - cell_y * (NZ - 1.0), high, grad - high, alive]
    for n, value in enumerate(tile_rows):
        aux[:, n, :] = value
    fetched["feats"].wait()
    to_slots.wait()

    def place(o):
        tails = []
        for r in range(CAP):
            j = slots[0, CAP * o + r]
            jj = jnp.maximum(j, 0)
            here = jnp.where(j >= 0, 1.0, 0.0)
            tail = aux[jj] * here
            send[o, r * C : (r + 1) * C, :] = (feats[jj].astype(F32) * tail[7:8]).astype(BF)
            tails.append(tail)
        send[o, CAP * C : CAP * C + 16, :] = jnp.concatenate(tails, axis=0).astype(BF)

    def points_copy(k):
        to = lax.rem(mx + k, GX)
        return pltpu.make_async_remote_copy(
            src_ref=send.at[to], dst_ref=recv.at[mx],
            send_sem=s_send.at[k], recv_sem=s_recv.at[k],
            device_id=(to, my), device_id_type=MESH,
        )

    pl.semaphore_wait(barrier, GX - 1 + GY - 1 + 4)

    @pl.loop(1, GX)
    def _(k):
        place(lax.rem(mx + k, GX))
        points_copy(k).start()

    place(mx)
    recv[mx] = send[mx]

    for name in ("lift", "conv", "read"):
        fetched[name].wait()
    eye = jnp.where(
        lax.broadcasted_iota(jnp.int32, (C, C), 0) == lax.broadcasted_iota(jnp.int32, (C, C), 1),
        1.0, 0.0,
    )
    read_col = dot((eye * read[...].astype(F32)).astype(BF), jnp.ones((C, NZ), BF))
    lift_w = lift[...]

    sub_z = lax.broadcasted_iota(jnp.int32, (NZ, WIDE), 0).astype(F32)
    sub_y = lax.broadcasted_iota(jnp.int32, (CY, WIDE), 0).astype(F32)
    acc[...] = jnp.zeros(acc.shape, F32)

    @pl.loop(0, GROUPS)
    def _(g):
        blocks, tails = [], []
        for n in range(GROUP):
            k = GROUP * g + n
            if n == 0:

                @pl.when(g > 0)
                def _():
                    points_copy(GROUP * g).wait_recv()

            else:
                points_copy(k).wait_recv()
        for n in range(GROUP):
            msg = recv[lax.rem(mx - (GROUP * g + n) + GX, GX)]
            blocks += [msg[0:C], msg[C : 2 * C]]
            tail = msg[2 * C : 2 * C + 16].astype(F32)
            tails += [tail[0:8], tail[8:16]]
        block = jnp.concatenate(blocks, axis=1)
        tail = jnp.concatenate(tails, axis=1)
        near = jnp.exp(-2.0 * tail * tail)
        far = jnp.exp(-2.0 * (tail - 1.0) * (tail - 1.0))
        at_y, at_z = tail[3:4], tail[4:5]
        slope = tail[5:6] + tail[6:7]
        wy = jnp.where(sub_y == at_y, near[1:2], jnp.where(sub_y == at_y + 1.0, far[1:2], 0.0))
        plane = (near[0:1] * wy, far[0:1] * wy)
        planes[g, 0:CY, :] = plane[0]
        planes[g, CY : 2 * CY, :] = plane[1]
        z = jnp.where(sub_z == at_z, near[2:3], jnp.where(sub_z == at_z + 1.0, far[2:3], 0.0))
        z = z.astype(BF)
        zs[g] = z
        lifted = dot(lift_w, block, 0, 0).astype(BF).astype(F32)
        rows = [
            (lifted * plane[x][y : y + 1]).astype(BF) for y in range(CY) for x in range(CX)
        ]
        rows.append(jnp.concatenate([plane[0] * slope, plane[1] * slope], axis=0).astype(BF))
        acc[...] += dot(jnp.concatenate(rows, axis=0), z, 1, 1)

    def halo_copies(buf, sends, recvs):
        ends = (
            (right, my, buf.at[1:9, 2], buf.at[1:9, 0]),
            (left, my, buf.at[1:9, 1], buf.at[1:9, 3]),
            (mx, up, buf.at[8, 1:3], buf.at[0, 1:3]),
            (mx, down, buf.at[1, 1:3], buf.at[9, 1:3]),
            (right, up, buf.at[8, 2], buf.at[0, 0]),
            (right, down, buf.at[1, 2], buf.at[9, 0]),
            (left, up, buf.at[8, 1], buf.at[0, 3]),
            (left, down, buf.at[1, 1], buf.at[9, 3]),
        )
        return [
            pltpu.make_async_remote_copy(
                src_ref=src, dst_ref=dst, send_sem=sends.at[n], recv_sem=recvs.at[n],
                device_id=(px, py), device_id_type=MESH,
            )
            for n, (px, py, src, dst) in enumerate(ends)
        ]

    def clear_ends(buf):
        @pl.when(mx == 0)
        def _():
            buf[:, 0] = jnp.zeros((10, C, NZ), BF)

        @pl.when(mx == GX - 1)
        def _():
            buf[:, 3] = jnp.zeros((10, C, NZ), BF)

        @pl.when(my == 0)
        def _():
            buf[0] = jnp.zeros((4, C, NZ), BF)

        @pl.when(my == GY - 1)
        def _():
            buf[9] = jnp.zeros((4, C, NZ), BF)

    for y in range(CY):
        for x in range(CX):
            row = (y * CX + x) * C
            latp[y + 1, x + 1] = acc[row : row + C, :].astype(BF)
    halos = halo_copies(latp, h_send, h_recv)
    for copy in halos:
        copy.start()

    def place_tap(xp):
        lanes = lax.broadcasted_iota(jnp.int32, (C, 128), 1)
        rows = lax.broadcasted_iota(jnp.int32, (C, 128), 0)
        return jnp.where(lanes == rows + C * xp, 1.0, 0.0).astype(BF)

    spots = [place_tap(xp) for xp in range(4)]
    wf[...] = jnp.zeros(wf.shape, BF)
    wb[...] = jnp.zeros(wb.shape, BF)
    for dz in range(3):
        for dy in range(3):
            for xo in range(2):
                tile_f = sum(
                    dot(conv[9 * dx + 3 * dy + dz], spots[dx + xo], 0, 0) for dx in range(3)
                ).astype(BF)
                tile_b = sum(
                    dot(conv[9 * (2 - dx) + 3 * (2 - dy) + (2 - dz)], spots[dx + xo])
                    for dx in range(3)
                ).astype(BF)
                for yo in range(2):
                    row = ((dz * 2 + yo) * 2 + xo) * C
                    lane = (yo + dy) * 128
                    wf[row : row + C, lane : lane + 128] = tile_f
                    wb[row : row + C, lane : lane + 128] = tile_b
    for copy in halos:
        copy.wait_recv()
    for copy in halos:
        copy.wait_send()
    clear_ends(latp)

    for pair in range(4):
        pre = conv_pair(wf, latp, pair)
        cube = pre * pre
        th = jnp.tanh(0.7978845608028654 * pre * (1.0 + 0.044715 * cube))
        half = 0.5 * (1.0 + th)
        slope = half + 0.5 * pre * (1.0 - th * th) * (
            0.7978845608028654 * (1.0 + 3.0 * 0.044715 * cube)
        )
        own = latp[2 * pair + 1 : 2 * pair + 3, 1:3].reshape(4 * C, NZ).astype(F32)
        out = (own + pre * half).astype(BF).astype(F32)
        grads = []
        for yo in range(2):
            for x in range(CX):
                row = x * CY + 2 * pair + yo
                n = (yo * CX + x) * C
                field[row : row + 1, :] = jnp.sum(
                    out[n : n + C] * read_col, axis=0, keepdims=True
                )
                grads.append(read_col * acc[COLS * C + row : COLS * C + row + 1, :])
        grad_out = jnp.concatenate(grads, axis=0)
        gout[128 * pair : 128 * pair + 128, :] = grad_out
        grad_pre = (grad_out * slope).astype(BF)
        gp[2 * pair + 1 : 2 * pair + 3, 1:3] = grad_pre.reshape(2, 2, C, NZ)
        wide = grad_pre.astype(F32)
        gs[pair, 0:128, :] = shifted(wide, -1).astype(BF)
        gs[pair, 128:256, :] = grad_pre
        gs[pair, 256:384, :] = shifted(wide, 1).astype(BF)
    halos2 = halo_copies(gp, i_send, i_recv)
    for copy in halos2:
        copy.start()

    tap = jnp.zeros((4 * 4 * C, 3 * 128), F32)
    for pair in range(4):
        window = latp[2 * pair : 2 * pair + 4].reshape(4 * 4 * C, NZ)
        tap = tap + dot(window, gs[pair], 1, 1)
    quarter = lax.broadcasted_iota(jnp.int32, (C, 128), 1) // C
    quarter8 = lax.broadcasted_iota(jnp.int32, (8, 128), 1) // C
    for dx in range(3):
        for dy in range(3):
            for dz in range(3):
                total = jnp.zeros((C, 128), F32)
                for yo in range(2):
                    for xo in range(2):
                        n = ((yo + dy) * 4 + xo + dx) * C
                        piece = tap[n : n + C, dz * 128 : dz * 128 + 128]
                        total = jnp.where(quarter == 2 * yo + xo, piece, total)
                total = total + pltpu.roll(total, 64, 1)
                total = total + pltpu.roll(total, 32, 1)
                packed = total[0:8]
                for q in range(1, 4):
                    packed = jnp.where(quarter8 == q, total[8 * q : 8 * q + 8], packed)
                redsrc[9 * dx + 3 * dy + dz] = packed
    redsrc[TAPS:GX] = jnp.zeros((GX - TAPS, 8, 128), F32)

    def taps_copy(k):
        to = lax.rem(mx + k, GX)
        return pltpu.make_async_remote_copy(
            src_ref=redsrc.at[to], dst_ref=red1.at[mx],
            send_sem=a_send.at[k], recv_sem=a_recv.at[k],
            device_id=(to, my), device_id_type=MESH,
        )

    @pl.loop(1, GX)
    def _(k):
        taps_copy(k).start()

    scalar = field[...]
    scalar_hi = scalar.astype(BF)
    scalar_lo = (scalar - scalar_hi.astype(F32)).astype(BF)
    scalars = jnp.concatenate([scalar_hi, scalar_lo], axis=0)

    def pred_copy(k):
        to = lax.rem(mx - k + GX, GX)
        return pltpu.make_async_remote_copy(
            src_ref=predmsg.at[k, 0:CAP], dst_ref=predr.at[mx, 0:CAP],
            send_sem=p_send.at[k], recv_sem=p_recv.at[k],
            device_id=(to, my), device_id_type=MESH,
        )

    @pl.loop(0, GROUPS)
    def _(g):
        got = dot(scalars, zs[g])
        total = jnp.sum((got[0:COLS] + got[COLS:]) * planes[g], axis=0, keepdims=True)
        for n in range(GROUP):
            k = GROUP * g + n
            for r in range(CAP):
                lane = n * PTS + r * BLK
                predmsg[k, r : r + 1, :] = total[:, lane : lane + BLK]
            if n == 0:

                @pl.when(g > 0)
                def _():
                    pred_copy(GROUP * g).start()

            else:
                pred_copy(k).start()

    predr[mx, 0:CAP, :] = predmsg[0, 0:CAP, :]

    for copy in halos2:
        copy.wait_recv()
    for copy in halos2:
        copy.wait_send()
    clear_ends(gp)
    for pair in range(4):
        back = conv_pair(wb, gp, pair)
        gl[128 * pair : 128 * pair + 128, :] = (
            gout[128 * pair : 128 * pair + 128, :] + back
        ).astype(BF)

    def feats_copy(k):
        to = lax.rem(mx - k + GX, GX)
        return pltpu.make_async_remote_copy(
            src_ref=gfs.at[k], dst_ref=gfr.at[pl.ds(CAP * mx, CAP)],
            send_sem=f_send.at[k], recv_sem=f_recv.at[k],
            device_id=(to, my), device_id_type=MESH,
        )

    def rows_copy(k):
        return pltpu.make_async_remote_copy(
            src_ref=red2.at[my], dst_ref=red2.at[my],
            send_sem=b_send.at[k], recv_sem=b_recv.at[k],
            device_id=(mx, lax.rem(my + k, GY)), device_id_type=MESH,
        )

    def send_back(g):
        got = dot(gl[...], zs[g])
        total = jnp.zeros((C, WIDE), F32)
        for y in range(CY):
            for x in range(CX):
                n = (y * CX + x) * C
                total = total + got[n : n + C] * planes[g, x * CY + y : x * CY + y + 1, :]
        back = dot(lift_w, total.astype(BF)).astype(BF)
        for n in range(GROUP):
            k = GROUP * g + n
            for r in range(CAP):
                lane = n * PTS + r * BLK
                gfs[k, r] = back[:, lane : lane + BLK]
            if n == 0:

                @pl.when(g > 0)
                def _():
                    feats_copy(GROUP * g).start()

            else:
                feats_copy(k).start()

    @pl.loop(1, 4)
    def _(g):
        send_back(g)

    red1[mx] = redsrc[mx]

    @pl.loop(1, GX)
    def _(k):
        taps_copy(k).wait_recv()

    red2[my] = jnp.sum(red1[...], axis=0)
    for k in range(1, GY):
        rows_copy(k).start()

    @pl.loop(4, GROUPS)
    def _(g):
        send_back(g)

    for k in range(1, GY):
        rows_copy(k).wait_recv()
    for k in range(1, GY):
        rows_copy(k).wait_send()
    red3[mx] = (red2[0] + red2[1] + red2[2] + red2[3]) * (1.0 / GX)

    def total_copy(k):
        to = lax.rem(mx + k, GX)
        return pltpu.make_async_remote_copy(
            src_ref=red3.at[mx], dst_ref=red3.at[mx],
            send_sem=c_send.at[k], recv_sem=c_recv.at[k],
            device_id=(to, my), device_id_type=MESH,
        )

    @pl.loop(1, GX)
    def _(k):
        total_copy(k).start()

    send_back(0)
    gfr[pl.ds(CAP * mx, CAP)] = gfs[0]

    @pl.loop(1, GX)
    def _(k):
        pred_copy(k).wait()
        total_copy(k).wait()
        feats_copy(k).wait()
        points_copy(k).wait_send()
        taps_copy(k).wait_send()


def finish_kernel(
    gfr, predr, red3, alive, table, pred_out, feats_out, conv_out,
    slots, pred, feats, conv, sems,
):
    to_slots = pltpu.make_async_copy(table, slots, sems.at[0])
    to_slots.start()
    for d in range(TAPS):
        packed = red3[d]
        for q in range(4):
            piece = packed if q == 0 else pltpu.roll(packed, 128 - C * q, 1)
            conv[d, 8 * q : 8 * q + 8, :] = piece[:, 0:C]
    copies = [pltpu.make_async_copy(conv, conv_out, sems.at[1])]
    copies[0].start()
    to_slots.wait()
    for part in range(4):

        @pl.loop(8 * part, 8 * part + 8)
        def _(j):
            s = slots[1, j]
            keep = alive[pl.ds(j, 1), :]
            feats[j] = (gfr[s].astype(F32) * keep).astype(BF)
            both = predr[s // CAP]
            value = jnp.where(lax.rem(s, CAP) == 0, both[0:1], both[1:2])
            pred[pl.ds(j, 1), :] = value * keep

        span = pl.ds(8 * part, 8)
        copies.append(pltpu.make_async_copy(feats.at[span], feats_out.at[span], sems.at[2 + part]))
        copies[-1].start()
    copies.append(pltpu.make_async_copy(pred, pred_out, sems.at[6]))
    copies[-1].start()
    for copy in copies:
        copy.wait()


def local(
    point_feats, point_offsets, base_cells, block_owners, point_counts,
    lift_weight, conv_weight, read_weight, cotangent,
):
    hbm = pl.BlockSpec(memory_space=pltpu.HBM)
    vmem = pl.BlockSpec(memory_space=pltpu.VMEM)
    dma = pltpu.SemaphoreType.DMA
    inputs = (
        point_feats, jnp.transpose(point_offsets, (1, 0, 2)), base_cells,
        block_owners.reshape(1, NB), point_counts.reshape(1, 1), lift_weight, conv_weight,
        read_weight.reshape(1, C), cotangent,
    )
    parts = pl.pallas_call(
        kernel,
        out_shape=(
            pltpu.VMEM((GX * CAP, C, BLK), BF),
            pltpu.VMEM((GX, 8, BLK), F32),
            pltpu.VMEM((GX, 8, 128), F32),
            pltpu.VMEM((NB, BLK), F32),
            pltpu.VMEM((8, BLK), jnp.int32),
        ),
        in_specs=[hbm] * 9,
        out_specs=(vmem,) * 5,
        scratch_shapes=[
            pltpu.VMEM((NB, C, BLK), BF),
            pltpu.VMEM((3, NB, BLK), BF),
            pltpu.VMEM((NB, BLK), jnp.int32),
            pltpu.VMEM((1, NB), jnp.int32),
            pltpu.VMEM((1, 1), jnp.int32),
            pltpu.VMEM((C, C), BF),
            pltpu.VMEM((TAPS, C, C), BF),
            pltpu.VMEM((1, C), BF),
            pltpu.VMEM((NB, BLK), F32),
            pltpu.SMEM((8, BLK), jnp.int32),
            pltpu.VMEM((NB, 8, BLK), F32),
            dma((10,)),
            pltpu.VMEM((GX, CAP * C + 16, BLK), BF),
            pltpu.VMEM((GX, CAP * C + 16, BLK), BF),
            pltpu.VMEM((COLS * C + COLS, NZ), F32),
            pltpu.VMEM((GROUPS, NZ, WIDE), BF),
            pltpu.VMEM((GROUPS, COLS, WIDE), F32),
            pltpu.VMEM((10, 4, C, NZ), BF),
            pltpu.VMEM((10, 4, C, NZ), BF),
            pltpu.VMEM((4, 3 * 128, NZ), BF),
            pltpu.VMEM((3 * 128, 512), BF),
            pltpu.VMEM((3 * 128, 512), BF),
            pltpu.VMEM((COLS * C, NZ), F32),
            pltpu.VMEM((COLS, NZ), F32),
            pltpu.VMEM((COLS * C, NZ), BF),
            pltpu.VMEM((GX, 8, BLK), F32),
            pltpu.VMEM((GX, CAP, C, BLK), BF),
            pltpu.VMEM((GX, 8, 128), F32),
            pltpu.VMEM((GX, 8, 128), F32),
            pltpu.VMEM((GY, 8, 128), F32),
            dma((GX,)), dma((GX,)), dma((8,)), dma((8,)), dma((8,)), dma((8,)),
            dma((GX,)), dma((GX,)), dma((GX,)), dma((GX,)), dma((GX,)), dma((GX,)),
            dma((GY,)), dma((GY,)), dma((GX,)), dma((GX,)),
        ],
        compiler_params=pltpu.CompilerParams(
            collective_id=0, has_side_effects=True, vmem_limit_bytes=40 * 1024 * 1024
        ),
        cost_estimate=pl.CostEstimate(
            flops=8_000_000_000, bytes_accessed=2_000_000, transcendentals=1_000_000
        ),
    )(*(x if x.size == 1 else pltpu.with_memory_space_constraint(x, pltpu.HBM) for x in inputs))
    return pl.pallas_call(
        finish_kernel,
        out_shape=(
            jax.ShapeDtypeStruct((NB, BLK), F32),
            jax.ShapeDtypeStruct((NB, C, BLK), BF),
            jax.ShapeDtypeStruct((TAPS, C, C), F32),
        ),
        in_specs=[vmem] * 5,
        out_specs=(hbm,) * 3,
        scratch_shapes=[
            pltpu.SMEM((8, BLK), jnp.int32),
            pltpu.VMEM((NB, BLK), F32),
            pltpu.VMEM((NB, C, BLK), BF),
            pltpu.VMEM((TAPS, C, C), F32),
            dma((7,)),
        ],
        compiler_params=pltpu.CompilerParams(vmem_limit_bytes=8 * 1024 * 1024),
    )(*(pltpu.with_memory_space_constraint(x, pltpu.VMEM) for x in parts))


def solution(mesh):
    in_specs = (
        P(("gx", "gy"), None, None),
        P(("gx", "gy"), None, None),
        P(("gx", "gy"), None),
        P(("gx", "gy"), None),
        P(("gx", "gy")),
        P(),
        P(),
        P(),
        P(("gx", "gy"), None),
    )
    out_specs = (P(("gx", "gy"), None), P(("gx", "gy"), None, None), P())
    return jax.shard_map(local, mesh=mesh, in_specs=in_specs, out_specs=out_specs, check_vma=False)
```

```python
import functools

import jax
import jax.numpy as jnp
from jax import lax
from jax.experimental import pallas as pl
from jax.experimental.pallas import tpu as pltpu
from jax.sharding import PartitionSpec as P

C = 32
CX = 2
CY = 8
NZ = 256
NB = 32
BLK = 128
GX = 32
GY = 4
CAP = 2
PTS = CAP * BLK
GROUP = 4
GROUPS = GX // GROUP
WIDE = GROUP * PTS
COLS = CX * CY
TAPS = 27
MESH = pl.DeviceIdType.MESH
BF = jnp.bfloat16
F32 = jnp.float32


def partner(mx, n, sign):
    m, dc = n // 2, lax.rem(n, 2)
    dx, dz = lax.rem(m, 4), lax.rem(m // 4 + m, 4)
    if sign < 0:
        dx, dz = 4 - dx, 4 - dz
    x, z, c = mx // 8, lax.rem(mx // 2, 4), lax.rem(mx, 2)
    return lax.rem(x + dx, 4) * 8 + lax.rem(z + dz, 4) * 2 + lax.rem(c + dc, 2)


def whole(ref, sem):
    pltpu.make_async_copy(ref, ref, sem).wait()


def dot(a, b, ca=1, cb=0):
    return lax.dot_general(a, b, (((ca,), (cb,)), ((), ())), preferred_element_type=F32)


def shifted(values, step):
    lanes = lax.broadcasted_iota(jnp.int32, values.shape, 1)
    if step == 1:
        return jnp.where(lanes == 0, 0.0, pltpu.roll(values, 1, 1))
    return jnp.where(lanes == NZ - 1, 0.0, pltpu.roll(values, NZ - 1, 1))


def conv_pair(weights, padded, pair):
    window = padded[2 * pair : 2 * pair + 4].reshape(4 * 4 * C, NZ)
    part = dot(weights[...], window)
    return shifted(part[0:128], 1) + part[128:256] + shifted(part[256:384], -1)


def kernel(
    feats_hbm, offsets_hbm, base_hbm, owners_hbm, count_hbm, lift_hbm, conv_hbm, read_hbm, cot_hbm,
    gfr, predr, red3, alive_out, table,
    feats, offsets, base, owners, count, lift, conv, read, cot, slots, aux, in_sem, send, recv, acc, zs, planes, latp, gp, gs, wf, wb,
    gout, field, gl, predmsg, held, gfs, redsrc, red1, red2,
    s_send, s_recv, h_send, h_recv, i_send, i_recv, p_send, p_recv,
    f_send, f_recv, a_send, a_recv, b_send, b_recv, c_send, c_recv,
):
    mx = lax.axis_index("gx")
    my = lax.axis_index("gy")
    right, left = lax.rem(mx + 1, GX), lax.rem(mx + GX - 1, GX)
    up, down = lax.rem(my + 1, GY), lax.rem(my + GY - 1, GY)

    pairs = {
        "owners": (owners_hbm, owners), "offsets": (offsets_hbm, offsets), "base": (base_hbm, base),
        "count": (count_hbm, count), "cot": (cot_hbm, cot), "feats": (feats_hbm, feats),
        "lift": (lift_hbm, lift), "conv": (conv_hbm, conv), "read": (read_hbm, read),
    }
    fetched = {
        name: pltpu.make_async_copy(src, dst, in_sem.at[n])
        for n, (name, (src, dst)) in enumerate(pairs.items())
    }
    for copy in fetched.values():
        copy.start()

    barrier = pltpu.get_barrier_semaphore()

    @pl.loop(1, GX)
    def _(k):
        pl.semaphore_signal(barrier, inc=1, device_id=(lax.rem(mx + k, GX), my), device_id_type=MESH)

    for k in range(1, GY):
        pl.semaphore_signal(barrier, inc=1, device_id=(mx, lax.rem(my + k, GY)), device_id_type=MESH)

    fetched["owners"].wait()
    named = owners[...]
    rows32 = lax.broadcasted_iota(jnp.int32, (NB, NB), 0)
    lanes32 = lax.broadcasted_iota(jnp.int32, (NB, NB), 1)
    named_col = jnp.sum(jnp.where(rows32 == lanes32, named, 0), axis=1, keepdims=True)
    earlier = (named_col == named) & (rows32 < lanes32)
    slot_row = CAP * named + jnp.sum(jnp.where(earlier, 1, 0), axis=0, keepdims=True)
    slot_col = jnp.sum(jnp.where(rows32 == lanes32, slot_row, 0), axis=1, keepdims=True)
    rows = lax.broadcasted_iota(jnp.int32, (NB, BLK), 0)
    lanes = lax.broadcasted_iota(jnp.int32, (NB, BLK), 1)
    table[0:1, :] = jnp.sum(jnp.where(slot_col == lanes, rows + 1, 0), axis=0, keepdims=True) - 1
    table[1:2, :] = jnp.sum(jnp.where(rows == lanes, slot_col, 0), axis=0, keepdims=True)
    table[2:8, :] = jnp.zeros((6, BLK), jnp.int32)
    to_slots = pltpu.make_async_copy(table, slots, in_sem.at[9])
    to_slots.start()

    for name in ("offsets", "base", "count", "cot"):
        fetched[name].wait()
    cells = base[...].astype(F32)
    cell_y = jnp.floor((cells + 0.5) * (1.0 / (NZ - 1)))
    alive = jnp.where(rows * BLK + lanes < count[...], 1.0, 0.0)
    alive_out[...] = alive
    grad = cot[...] * alive
    high = grad.astype(BF).astype(F32)
    tile_rows = [offsets[n].astype(F32) for n in range(3)]
    tile_rows += [cell_y, cells - cell_y * (NZ - 1.0), high, grad - high, alive]
    for n, value in enumerate(tile_rows):
        aux[:, n, :] = value
    for name in ("lift", "feats"):
        fetched[name].wait()
    lift_w = lift[...]
    for part in range(4):
        raw = jnp.concatenate([feats[8 * part + n] for n in range(8)], axis=1)
        lifted = dot(lift_w, raw, 0, 0).astype(BF)
        for n in range(8):
            feats[8 * part + n] = lifted[:, n * BLK : (n + 1) * BLK]
    to_slots.wait()

    def place(o):
        tails = []
        for r in range(CAP):
            j = slots[0, CAP * o + r]
            jj = jnp.maximum(j, 0)
            here = jnp.where(j >= 0, 1.0, 0.0)
            tail = aux[jj] * here
            send[o, r * C : (r + 1) * C, :] = (feats[jj].astype(F32) * tail[7:8]).astype(BF)
            tails.append(tail)
        send[o, CAP * C : CAP * C + 16, :] = jnp.concatenate(tails, axis=0).astype(BF)

    def points_copy(k):
        to = partner(mx, k, 1)
        return pltpu.make_async_remote_copy(
            src_ref=send.at[to], dst_ref=recv.at[mx],
            send_sem=s_send, recv_sem=s_recv.at[k // GROUP],
            device_id=(to, my), device_id_type=MESH,
        )

    pl.semaphore_wait(barrier, GX - 1 + GY - 1)

    @pl.loop(1, GX)
    def _(k):
        place(partner(mx, k, 1))
        points_copy(k).start()

    place(mx)
    recv[mx] = send[mx]

    for name in ("conv", "read"):
        fetched[name].wait()
    eye = jnp.where(
        lax.broadcasted_iota(jnp.int32, (C, C), 0) == lax.broadcasted_iota(jnp.int32, (C, C), 1),
        1.0, 0.0,
    )
    read_col = dot((eye * read[...].astype(F32)).astype(BF), jnp.ones((C, NZ), BF))

    sub_z = lax.broadcasted_iota(jnp.int32, (NZ, WIDE), 0).astype(F32)
    sub_y = lax.broadcasted_iota(jnp.int32, (CY, WIDE), 0).astype(F32)
    acc[...] = jnp.zeros(acc.shape, F32)

    @pl.loop(0, GROUPS)
    def _(g):
        blocks, tails = [], []

        @pl.when(g == 0)
        def _():
            whole(recv.at[0 : GROUP - 1], s_recv.at[0])

        @pl.when(g > 0)
        def _():
            whole(recv.at[0:GROUP], s_recv.at[g])

        for n in range(GROUP):
            msg = recv[partner(mx, GROUP * g + n, -1)]
            blocks += [msg[0:C], msg[C : 2 * C]]
            tail = msg[2 * C : 2 * C + 16].astype(F32)
            tails += [tail[0:8], tail[8:16]]
        block = jnp.concatenate(blocks, axis=1)
        tail = jnp.concatenate(tails, axis=1)
        near = jnp.exp(-2.0 * tail * tail)
        far = jnp.exp(-2.0 * (tail - 1.0) * (tail - 1.0))
        at_y, at_z = tail[3:4], tail[4:5]
        slope = tail[5:6] + tail[6:7]
        wy = jnp.where(sub_y == at_y, near[1:2], jnp.where(sub_y == at_y + 1.0, far[1:2], 0.0))
        plane = (near[0:1] * wy, far[0:1] * wy)
        planes[g, 0:CY, :] = plane[0]
        planes[g, CY : 2 * CY, :] = plane[1]
        z = jnp.where(sub_z == at_z, near[2:3], jnp.where(sub_z == at_z + 1.0, far[2:3], 0.0))
        z = z.astype(BF)
        zs[g] = z
        lifted = block.astype(F32)
        rows = [
            (lifted * plane[x][y : y + 1]).astype(BF) for y in range(CY) for x in range(CX)
        ]
        rows.append(jnp.concatenate([plane[0] * slope, plane[1] * slope], axis=0).astype(BF))
        acc[...] += dot(jnp.concatenate(rows, axis=0), z, 1, 1)

    def halo_copies(buf, sends, recvs):
        ends = (
            (right, my, buf.at[1:9, 2], buf.at[1:9, 0]),
            (left, my, buf.at[1:9, 1], buf.at[1:9, 3]),
            (mx, up, buf.at[8, 1:3], buf.at[0, 1:3]),
            (mx, down, buf.at[1, 1:3], buf.at[9, 1:3]),
            (right, up, buf.at[8, 2], buf.at[0, 0]),
            (right, down, buf.at[1, 2], buf.at[9, 0]),
            (left, up, buf.at[8, 1], buf.at[0, 3]),
            (left, down, buf.at[1, 1], buf.at[9, 3]),
        )
        return [
            pltpu.make_async_remote_copy(
                src_ref=src, dst_ref=dst, send_sem=sends, recv_sem=recvs,
                device_id=(px, py), device_id_type=MESH,
            )
            for n, (px, py, src, dst) in enumerate(ends)
        ]

    def clear_ends(buf):
        @pl.when(mx == 0)
        def _():
            buf[:, 0] = jnp.zeros((10, C, NZ), BF)

        @pl.when(mx == GX - 1)
        def _():
            buf[:, 3] = jnp.zeros((10, C, NZ), BF)

        @pl.when(my == 0)
        def _():
            buf[0] = jnp.zeros((4, C, NZ), BF)

        @pl.when(my == GY - 1)
        def _():
            buf[9] = jnp.zeros((4, C, NZ), BF)

    for y in range(CY):
        for x in range(CX):
            row = (y * CX + x) * C
            latp[y + 1, x + 1] = acc[row : row + C, :].astype(BF)
    halos = halo_copies(latp, h_send, h_recv)
    for copy in halos:
        copy.start()

    def place_tap(xp):
        lanes = lax.broadcasted_iota(jnp.int32, (C, 128), 1)
        rows = lax.broadcasted_iota(jnp.int32, (C, 128), 0)
        return jnp.where(lanes == rows + C * xp, 1.0, 0.0).astype(BF)

    spots = [place_tap(xp) for xp in range(4)]
    wf[...] = jnp.zeros(wf.shape, BF)
    wb[...] = jnp.zeros(wb.shape, BF)
    for dz in range(3):
        for dy in range(3):
            for xo in range(2):
                tile_f = sum(
                    dot(conv[9 * dx + 3 * dy + dz], spots[dx + xo], 0, 0) for dx in range(3)
                ).astype(BF)
                tile_b = sum(
                    dot(conv[9 * (2 - dx) + 3 * (2 - dy) + (2 - dz)], spots[dx + xo])
                    for dx in range(3)
                ).astype(BF)
                for yo in range(2):
                    row = ((dz * 2 + yo) * 2 + xo) * C
                    lane = (yo + dy) * 128
                    wf[row : row + C, lane : lane + 128] = tile_f
                    wb[row : row + C, lane : lane + 128] = tile_b
    whole(latp.at[0:6], h_recv)
    clear_ends(latp)

    for pair in range(4):
        pre = conv_pair(wf, latp, pair)
        cube = pre * pre
        th = jnp.tanh(0.7978845608028654 * pre * (1.0 + 0.044715 * cube))
        half = 0.5 * (1.0 + th)
        slope = half + 0.5 * pre * (1.0 - th * th) * (
            0.7978845608028654 * (1.0 + 3.0 * 0.044715 * cube)
        )
        own = latp[2 * pair + 1 : 2 * pair + 3, 1:3].reshape(4 * C, NZ).astype(F32)
        out = (own + pre * half).astype(BF).astype(F32)
        grads = []
        for yo in range(2):
            for x in range(CX):
                row = x * CY + 2 * pair + yo
                n = (yo * CX + x) * C
                field[row : row + 1, :] = jnp.sum(
                    out[n : n + C] * read_col, axis=0, keepdims=True
                )
                grads.append(read_col * acc[COLS * C + row : COLS * C + row + 1, :])
        grad_out = jnp.concatenate(grads, axis=0)
        gout[128 * pair : 128 * pair + 128, :] = grad_out
        grad_pre = (grad_out * slope).astype(BF)
        gp[2 * pair + 1 : 2 * pair + 3, 1:3] = grad_pre.reshape(2, 2, C, NZ)
        wide = grad_pre.astype(F32)
        gs[pair, 0:128, :] = shifted(wide, -1).astype(BF)
        gs[pair, 128:256, :] = grad_pre
        gs[pair, 256:384, :] = shifted(wide, 1).astype(BF)
    halos2 = halo_copies(gp, i_send, i_recv)
    for copy in halos2:
        copy.start()

    tap = jnp.zeros((4 * 4 * C, 3 * 128), F32)
    for pair in range(4):
        window = latp[2 * pair : 2 * pair + 4].reshape(4 * 4 * C, NZ)
        tap = tap + dot(window, gs[pair], 1, 1)
    quarter = lax.broadcasted_iota(jnp.int32, (C, 128), 1) // C
    quarter8 = lax.broadcasted_iota(jnp.int32, (8, 128), 1) // C
    for dx in range(3):
        for dy in range(3):
            for dz in range(3):
                total = jnp.zeros((C, 128), F32)
                for yo in range(2):
                    for xo in range(2):
                        n = ((yo + dy) * 4 + xo + dx) * C
                        piece = tap[n : n + C, dz * 128 : dz * 128 + 128]
                        total = jnp.where(quarter == 2 * yo + xo, piece, total)
                total = total + pltpu.roll(total, 64, 1)
                total = total + pltpu.roll(total, 32, 1)
                packed = total[0:8]
                for q in range(1, 4):
                    packed = jnp.where(quarter8 == q, total[8 * q : 8 * q + 8], packed)
                redsrc[9 * dx + 3 * dy + dz] = packed
    redsrc[TAPS:GX] = jnp.zeros((GX - TAPS, 8, 128), F32)

    def taps_copy(k):
        to = partner(mx, k, 1)
        return pltpu.make_async_remote_copy(
            src_ref=redsrc.at[to], dst_ref=red1.at[mx],
            send_sem=a_send, recv_sem=a_recv,
            device_id=(to, my), device_id_type=MESH,
        )

    @pl.loop(1, GX)
    def _(k):
        taps_copy(k).start()

    scalar = field[...]
    scalar_hi = scalar.astype(BF)
    scalar_lo = (scalar - scalar_hi.astype(F32)).astype(BF)
    scalars = jnp.concatenate([scalar_hi, scalar_lo], axis=0)

    def pred_copy(k):
        to = partner(mx, k, -1)
        return pltpu.make_async_remote_copy(
            src_ref=predmsg.at[k, 0:CAP], dst_ref=predr.at[mx, 0:CAP],
            send_sem=p_send, recv_sem=p_recv,
            device_id=(to, my), device_id_type=MESH,
        )

    @pl.loop(0, GROUPS)
    def _(g):
        got = dot(scalars, zs[g])
        total = jnp.sum((got[0:COLS] + got[COLS:]) * planes[g], axis=0, keepdims=True)
        for n in range(GROUP):
            k = GROUP * g + n
            for r in range(CAP):
                lane = n * PTS + r * BLK
                predmsg[k, r : r + 1, :] = total[:, lane : lane + BLK]
            if n == 0:

                @pl.when(g > 0)
                def _():
                    pred_copy(GROUP * g).start()

            else:
                pred_copy(k).start()

    predr[mx, 0:CAP, :] = predmsg[0, 0:CAP, :]

    whole(gp.at[0:6], i_recv)
    clear_ends(gp)
    for pair in range(4):
        back = conv_pair(wb, gp, pair)
        gl[128 * pair : 128 * pair + 128, :] = (
            gout[128 * pair : 128 * pair + 128, :] + back
        ).astype(BF)

    def feats_copy(k):
        to = partner(mx, k, -1)
        return pltpu.make_async_remote_copy(
            src_ref=gfs.at[k], dst_ref=gfr.at[pl.ds(CAP * mx, CAP)],
            send_sem=f_send, recv_sem=f_recv,
            device_id=(to, my), device_id_type=MESH,
        )

    def rows_copy(k):
        return pltpu.make_async_remote_copy(
            src_ref=red2.at[my], dst_ref=red2.at[my],
            send_sem=b_send, recv_sem=b_recv,
            device_id=(mx, lax.rem(my + k, GY)), device_id_type=MESH,
        )

    def collect(g):
        got = dot(gl[...], zs[g])
        total = jnp.zeros((C, WIDE), F32)
        for y in range(CY):
            for x in range(CX):
                n = (y * CX + x) * C
                total = total + got[n : n + C] * planes[g, x * CY + y : x * CY + y + 1, :]
        return total.astype(BF)

    def finish(g, total):
        back = dot(lift_w, total).astype(BF)
        for n in range(GROUP):
            for r in range(CAP):
                lane = n * PTS + r * BLK
                gfs[GROUP * g + n, r] = back[:, lane : lane + BLK]

    def send_back(g):
        for n in range(GROUP):
            feats_copy(GROUP * g + n).start()

    def step(g):
        before = held[...]
        total = collect(g)
        finish(g - 1, before)
        held[...] = total
        send_back(g - 1)

    held[...] = collect(1)

    @pl.loop(2, 4)
    def _(g):
        step(g)

    red1[mx] = redsrc[mx]

    whole(red1.at[0 : GX - 1], a_recv)
    red2[my] = jnp.sum(red1[...], axis=0)
    for k in range(1, GY):
        rows_copy(k).start()

    @pl.loop(4, GROUPS)
    def _(g):
        step(g)

    whole(red2.at[0 : GY - 1], b_recv)
    red3[mx] = (red2[0] + red2[1] + red2[2] + red2[3]) * (1.0 / GX)

    def total_copy(k):
        to = partner(mx, k, 1)
        return pltpu.make_async_remote_copy(
            src_ref=red3.at[mx], dst_ref=red3.at[mx],
            send_sem=c_send, recv_sem=c_recv,
            device_id=(to, my), device_id_type=MESH,
        )

    @pl.loop(1, GX)
    def _(k):
        total_copy(k).start()

    before = held[...]
    total = collect(0)
    finish(GROUPS - 1, before)
    send_back(GROUPS - 1)
    finish(0, total)
    for n in range(1, GROUP):
        feats_copy(n).start()
    gfr[pl.ds(CAP * mx, CAP)] = gfs[0]

    for sem in (p_recv, p_send):
        whole(predr.at[0 : GX - 1, 0:CAP], sem)
    for sem in (c_recv, c_send, a_send):
        whole(red3.at[0 : GX - 1], sem)
    for sem in (f_recv, f_send):
        whole(gfr.at[0 : CAP * (GX - 1)], sem)
    whole(red2.at[0 : GY - 1], b_send)
    whole(latp.at[0:6], h_send)
    whole(gp.at[0:6], i_send)
    whole(recv.at[0 : GX - 1], s_send)


def finish_kernel(
    gfr, predr, red3, alive, table, pred_out, feats_out, conv_out,
    slots, pred, feats, conv, sems,
):
    to_slots = pltpu.make_async_copy(table, slots, sems.at[0])
    to_slots.start()
    for d in range(TAPS):
        packed = red3[d]
        for q in range(4):
            piece = packed if q == 0 else pltpu.roll(packed, 128 - C * q, 1)
            conv[d, 8 * q : 8 * q + 8, :] = piece[:, 0:C]
    copies = [pltpu.make_async_copy(conv, conv_out, sems.at[1])]
    copies[0].start()
    to_slots.wait()
    for part in range(4):

        @pl.loop(8 * part, 8 * part + 8)
        def _(j):
            s = slots[1, j]
            keep = alive[pl.ds(j, 1), :]
            feats[j] = (gfr[s].astype(F32) * keep).astype(BF)
            both = predr[s // CAP]
            value = jnp.where(lax.rem(s, CAP) == 0, both[0:1], both[1:2])
            pred[pl.ds(j, 1), :] = value * keep

        span = pl.ds(8 * part, 8)
        copies.append(pltpu.make_async_copy(feats.at[span], feats_out.at[span], sems.at[2 + part]))
        copies[-1].start()
    copies.append(pltpu.make_async_copy(pred, pred_out, sems.at[6]))
    copies[-1].start()
    for copy in copies:
        copy.wait()


def local(
    point_feats, point_offsets, base_cells, block_owners, point_counts,
    lift_weight, conv_weight, read_weight, cotangent,
):
    hbm = pl.BlockSpec(memory_space=pltpu.HBM)
    vmem = pl.BlockSpec(memory_space=pltpu.VMEM)
    dma = pltpu.SemaphoreType.DMA
    inputs = (
        point_feats, jnp.transpose(point_offsets, (1, 0, 2)), base_cells,
        block_owners.reshape(1, NB), point_counts.reshape(1, 1), lift_weight, conv_weight,
        read_weight.reshape(1, C), cotangent,
    )
    parts = pl.pallas_call(
        kernel,
        out_shape=(
            pltpu.VMEM((GX * CAP, C, BLK), BF),
            pltpu.VMEM((GX, 8, BLK), F32),
            pltpu.VMEM((GX, 8, 128), F32),
            pltpu.VMEM((NB, BLK), F32),
            pltpu.VMEM((8, BLK), jnp.int32),
        ),
        in_specs=[hbm] * 9,
        out_specs=(vmem,) * 5,
        scratch_shapes=[
            pltpu.VMEM((NB, C, BLK), BF),
            pltpu.VMEM((3, NB, BLK), BF),
            pltpu.VMEM((NB, BLK), jnp.int32),
            pltpu.VMEM((1, NB), jnp.int32),
            pltpu.VMEM((1, 1), jnp.int32),
            pltpu.VMEM((C, C), BF),
            pltpu.VMEM((TAPS, C, C), BF),
            pltpu.VMEM((1, C), BF),
            pltpu.VMEM((NB, BLK), F32),
            pltpu.SMEM((8, BLK), jnp.int32),
            pltpu.VMEM((NB, 8, BLK), F32),
            dma((10,)),
            pltpu.VMEM((GX, CAP * C + 16, BLK), BF),
            pltpu.VMEM((GX, CAP * C + 16, BLK), BF),
            pltpu.VMEM((COLS * C + COLS, NZ), F32),
            pltpu.VMEM((GROUPS, NZ, WIDE), BF),
            pltpu.VMEM((GROUPS, COLS, WIDE), F32),
            pltpu.VMEM((10, 4, C, NZ), BF),
            pltpu.VMEM((10, 4, C, NZ), BF),
            pltpu.VMEM((4, 3 * 128, NZ), BF),
            pltpu.VMEM((3 * 128, 512), BF),
            pltpu.VMEM((3 * 128, 512), BF),
            pltpu.VMEM((COLS * C, NZ), F32),
            pltpu.VMEM((COLS, NZ), F32),
            pltpu.VMEM((COLS * C, NZ), BF),
            pltpu.VMEM((GX, 8, BLK), F32),
            pltpu.VMEM((C, WIDE), BF),
            pltpu.VMEM((GX, CAP, C, BLK), BF),
            pltpu.VMEM((GX, 8, 128), F32),
            pltpu.VMEM((GX, 8, 128), F32),
            pltpu.VMEM((GY, 8, 128), F32),
            dma, dma((GROUPS,)), dma, dma, dma, dma, dma, dma, dma, dma, dma, dma, dma, dma, dma, dma,
        ],
        compiler_params=pltpu.CompilerParams(
            collective_id=0, has_side_effects=True, vmem_limit_bytes=40 * 1024 * 1024
        ),
        cost_estimate=pl.CostEstimate(
            flops=8_000_000_000, bytes_accessed=2_000_000, transcendentals=1_000_000
        ),
    )(*(x if x.size == 1 else pltpu.with_memory_space_constraint(x, pltpu.HBM) for x in inputs))
    return pl.pallas_call(
        finish_kernel,
        out_shape=(
            jax.ShapeDtypeStruct((NB, BLK), F32),
            jax.ShapeDtypeStruct((NB, C, BLK), BF),
            jax.ShapeDtypeStruct((TAPS, C, C), F32),
        ),
        in_specs=[vmem] * 5,
        out_specs=(hbm,) * 3,
        scratch_shapes=[
            pltpu.SMEM((8, BLK), jnp.int32),
            pltpu.VMEM((NB, BLK), F32),
            pltpu.VMEM((NB, C, BLK), BF),
            pltpu.VMEM((TAPS, C, C), F32),
            dma((7,)),
        ],
        compiler_params=pltpu.CompilerParams(vmem_limit_bytes=8 * 1024 * 1024),
    )(*(pltpu.with_memory_space_constraint(x, pltpu.VMEM) for x in parts))


def solution(mesh):
    in_specs = (
        P(("gx", "gy"), None, None),
        P(("gx", "gy"), None, None),
        P(("gx", "gy"), None),
        P(("gx", "gy"), None),
        P(("gx", "gy")),
        P(),
        P(),
        P(),
        P(("gx", "gy"), None),
    )
    out_specs = (P(("gx", "gy"), None), P(("gx", "gy"), None, None), P())
    return jax.shard_map(local, mesh=mesh, in_specs=in_specs, out_specs=out_specs, check_vma=False)
```

```python
import functools

import jax
import jax.numpy as jnp
from jax import lax
from jax.experimental import pallas as pl
from jax.experimental.pallas import tpu as pltpu
from jax.sharding import PartitionSpec as P

C = 32
CX = 2
CY = 8
NZ = 256
NB = 32
BLK = 128
GX = 32
GY = 4
CAP = 2
PTS = CAP * BLK
GROUP = 4
GROUPS = GX // GROUP
WIDE = GROUP * PTS
COLS = CX * CY
TAPS = 27
MESH = pl.DeviceIdType.MESH
BF = jnp.bfloat16
F32 = jnp.float32


def partner(mx, n, sign):
    return lax.rem(mx + sign * lax.rem(11 * n, GX) + GX, GX)


def snake(index):
    x, z, core = index // 8, lax.rem(index // 2, 4), lax.rem(index, 2)
    return x * 8 + (z + lax.rem(x, 2) * (3 - 2 * z)) * 2 + core


def whole(ref, sem):
    pltpu.make_async_copy(ref, ref, sem).wait()


def dot(a, b, ca=1, cb=0):
    return lax.dot_general(a, b, (((ca,), (cb,)), ((), ())), preferred_element_type=F32)


def shifted(values, step):
    lanes = lax.broadcasted_iota(jnp.int32, values.shape, 1)
    if step == 1:
        return jnp.where(lanes == 0, 0.0, pltpu.roll(values, 1, 1))
    return jnp.where(lanes == NZ - 1, 0.0, pltpu.roll(values, NZ - 1, 1))


def conv_pair(weights, padded, pair):
    window = padded[2 * pair : 2 * pair + 4].reshape(4 * 4 * C, NZ)
    part = dot(weights[...], window)
    return shifted(part[0:128], 1) + part[128:256] + shifted(part[256:384], -1)


def kernel(
    feats_hbm, offsets_hbm, base_hbm, owners_hbm, count_hbm, lift_hbm, conv_hbm, read_hbm, cot_hbm,
    gfr, predr, red3, alive_out, table,
    feats, offsets, base, owners, count, lift, conv, read, cot, slots, aux, in_sem, send, recv, acc, zs, planes, latp, gp, gs, wf, wb,
    gout, field, gl, predmsg, held, gfs, redsrc, red1, red2,
    s_send, s_recv, h_send, h_recv, i_send, i_recv, p_send, p_recv,
    f_send, f_recv, a_send, a_recv, b_send, b_recv, c_send, c_recv,
):
    mx = lax.axis_index("gx")
    my = lax.axis_index("gy")
    slab = snake(mx)
    right, left = snake(lax.rem(slab + 1, GX)), snake(lax.rem(slab + GX - 1, GX))
    up, down = lax.rem(my + 1, GY), lax.rem(my + GY - 1, GY)

    pairs = {
        "owners": (owners_hbm, owners), "offsets": (offsets_hbm, offsets), "base": (base_hbm, base),
        "count": (count_hbm, count), "cot": (cot_hbm, cot), "feats": (feats_hbm, feats),
        "lift": (lift_hbm, lift), "conv": (conv_hbm, conv), "read": (read_hbm, read),
    }
    fetched = {
        name: pltpu.make_async_copy(src, dst, in_sem.at[n])
        for n, (name, (src, dst)) in enumerate(pairs.items())
    }
    for copy in fetched.values():
        copy.start()

    barrier = pltpu.get_barrier_semaphore()

    @pl.loop(1, GX)
    def _(k):
        pl.semaphore_signal(barrier, inc=1, device_id=(lax.rem(mx + k, GX), my), device_id_type=MESH)

    for k in range(1, GY):
        pl.semaphore_signal(barrier, inc=1, device_id=(mx, lax.rem(my + k, GY)), device_id_type=MESH)

    fetched["owners"].wait()
    named = owners[...]
    rows32 = lax.broadcasted_iota(jnp.int32, (NB, NB), 0)
    lanes32 = lax.broadcasted_iota(jnp.int32, (NB, NB), 1)
    named_col = jnp.sum(jnp.where(rows32 == lanes32, named, 0), axis=1, keepdims=True)
    earlier = (named_col == named) & (rows32 < lanes32)
    slot_row = CAP * named + jnp.sum(jnp.where(earlier, 1, 0), axis=0, keepdims=True)
    slot_col = jnp.sum(jnp.where(rows32 == lanes32, slot_row, 0), axis=1, keepdims=True)
    rows = lax.broadcasted_iota(jnp.int32, (NB, BLK), 0)
    lanes = lax.broadcasted_iota(jnp.int32, (NB, BLK), 1)
    table[0:1, :] = jnp.sum(jnp.where(slot_col == lanes, rows + 1, 0), axis=0, keepdims=True) - 1
    table[1:2, :] = jnp.sum(jnp.where(rows == lanes, slot_col, 0), axis=0, keepdims=True)
    table[2:8, :] = jnp.zeros((6, BLK), jnp.int32)
    to_slots = pltpu.make_async_copy(table, slots, in_sem.at[9])
    to_slots.start()

    for name in ("offsets", "base", "count", "cot"):
        fetched[name].wait()
    cells = base[...].astype(F32)
    cell_y = jnp.floor((cells + 0.5) * (1.0 / (NZ - 1)))
    alive = jnp.where(rows * BLK + lanes < count[...], 1.0, 0.0)
    alive_out[...] = alive
    grad = cot[...] * alive
    high = grad.astype(BF).astype(F32)
    tile_rows = [offsets[n].astype(F32) for n in range(3)]
    tile_rows += [cell_y, cells - cell_y * (NZ - 1.0), high, grad - high, alive]
    for n, value in enumerate(tile_rows):
        aux[:, n, :] = value
    for name in ("lift", "feats"):
        fetched[name].wait()
    lift_w = lift[...]
    for part in range(4):
        raw = jnp.concatenate([feats[8 * part + n] for n in range(8)], axis=1)
        lifted = dot(lift_w, raw, 0, 0).astype(BF)
        for n in range(8):
            feats[8 * part + n] = lifted[:, n * BLK : (n + 1) * BLK]
    to_slots.wait()

    def place(to):
        o = snake(to)
        tails = []
        for r in range(CAP):
            j = slots[0, CAP * o + r]
            jj = jnp.maximum(j, 0)
            here = jnp.where(j >= 0, 1.0, 0.0)
            tail = aux[jj] * here
            send[to, r * C : (r + 1) * C, :] = (feats[jj].astype(F32) * tail[7:8]).astype(BF)
            tails.append(tail)
        send[to, CAP * C : CAP * C + 16, :] = jnp.concatenate(tails, axis=0).astype(BF)

    def points_copy(k):
        to = partner(mx, k, 1)
        return pltpu.make_async_remote_copy(
            src_ref=send.at[to], dst_ref=recv.at[mx],
            send_sem=s_send, recv_sem=s_recv.at[k // GROUP],
            device_id=(to, my), device_id_type=MESH,
        )

    pl.semaphore_wait(barrier, GX - 1 + GY - 1)

    @pl.loop(1, GX)
    def _(k):
        place(partner(mx, k, 1))
        points_copy(k).start()

    place(mx)
    recv[mx] = send[mx]

    for name in ("conv", "read"):
        fetched[name].wait()
    eye = jnp.where(
        lax.broadcasted_iota(jnp.int32, (C, C), 0) == lax.broadcasted_iota(jnp.int32, (C, C), 1),
        1.0, 0.0,
    )
    read_col = dot((eye * read[...].astype(F32)).astype(BF), jnp.ones((C, NZ), BF))

    sub_z = lax.broadcasted_iota(jnp.int32, (NZ, WIDE), 0).astype(F32)
    sub_y = lax.broadcasted_iota(jnp.int32, (CY, WIDE), 0).astype(F32)
    acc[...] = jnp.zeros(acc.shape, F32)

    @pl.loop(0, GROUPS)
    def _(g):
        blocks, tails = [], []

        @pl.when(g == 0)
        def _():
            whole(recv.at[0 : GROUP - 1], s_recv.at[0])

        @pl.when(g > 0)
        def _():
            whole(recv.at[0:GROUP], s_recv.at[g])

        for n in range(GROUP):
            msg = recv[partner(mx, GROUP * g + n, -1)]
            blocks += [msg[0:C], msg[C : 2 * C]]
            tail = msg[2 * C : 2 * C + 16].astype(F32)
            tails += [tail[0:8], tail[8:16]]
        block = jnp.concatenate(blocks, axis=1)
        tail = jnp.concatenate(tails, axis=1)
        near = jnp.exp(-2.0 * tail * tail)
        far = jnp.exp(-2.0 * (tail - 1.0) * (tail - 1.0))
        at_y, at_z = tail[3:4], tail[4:5]
        slope = tail[5:6] + tail[6:7]
        wy = jnp.where(sub_y == at_y, near[1:2], jnp.where(sub_y == at_y + 1.0, far[1:2], 0.0))
        plane = (near[0:1] * wy, far[0:1] * wy)
        planes[g, 0:CY, :] = plane[0]
        planes[g, CY : 2 * CY, :] = plane[1]
        z = jnp.where(sub_z == at_z, near[2:3], jnp.where(sub_z == at_z + 1.0, far[2:3], 0.0))
        z = z.astype(BF)
        zs[g] = z
        lifted = block.astype(F32)
        rows = [
            (lifted * plane[x][y : y + 1]).astype(BF) for y in range(CY) for x in range(CX)
        ]
        rows.append(jnp.concatenate([plane[0] * slope, plane[1] * slope], axis=0).astype(BF))
        acc[...] += dot(jnp.concatenate(rows, axis=0), z, 1, 1)

    def halo_copies(buf, sends, recvs):
        ends = (
            (right, up, buf.at[8, 2], buf.at[0, 0]),
            (right, down, buf.at[1, 2], buf.at[9, 0]),
            (left, up, buf.at[8, 1], buf.at[0, 3]),
            (left, down, buf.at[1, 1], buf.at[9, 3]),
            (mx, up, buf.at[8, 1:3], buf.at[0, 1:3]),
            (mx, down, buf.at[1, 1:3], buf.at[9, 1:3]),
            (right, my, buf.at[1:9, 2], buf.at[1:9, 0]),
            (left, my, buf.at[1:9, 1], buf.at[1:9, 3]),
        )
        return [
            pltpu.make_async_remote_copy(
                src_ref=src, dst_ref=dst, send_sem=sends, recv_sem=recvs,
                device_id=(px, py), device_id_type=MESH,
            )
            for n, (px, py, src, dst) in enumerate(ends)
        ]

    def clear_ends(buf):
        @pl.when(slab == 0)
        def _():
            buf[:, 0] = jnp.zeros((10, C, NZ), BF)

        @pl.when(slab == GX - 1)
        def _():
            buf[:, 3] = jnp.zeros((10, C, NZ), BF)

        @pl.when(my == 0)
        def _():
            buf[0] = jnp.zeros((4, C, NZ), BF)

        @pl.when(my == GY - 1)
        def _():
            buf[9] = jnp.zeros((4, C, NZ), BF)

    for y in range(CY):
        for x in range(CX):
            row = (y * CX + x) * C
            latp[y + 1, x + 1] = acc[row : row + C, :].astype(BF)
    halos = halo_copies(latp, h_send, h_recv)
    for copy in halos:
        copy.start()

    def place_tap(xp):
        lanes = lax.broadcasted_iota(jnp.int32, (C, 128), 1)
        rows = lax.broadcasted_iota(jnp.int32, (C, 128), 0)
        return jnp.where(lanes == rows + C * xp, 1.0, 0.0).astype(BF)

    spots = [place_tap(xp) for xp in range(4)]
    wf[...] = jnp.zeros(wf.shape, BF)
    wb[...] = jnp.zeros(wb.shape, BF)
    for dz in range(3):
        for dy in range(3):
            for xo in range(2):
                tile_f = sum(
                    dot(conv[9 * dx + 3 * dy + dz], spots[dx + xo], 0, 0) for dx in range(3)
                ).astype(BF)
                tile_b = sum(
                    dot(conv[9 * (2 - dx) + 3 * (2 - dy) + (2 - dz)], spots[dx + xo])
                    for dx in range(3)
                ).astype(BF)
                for yo in range(2):
                    row = ((dz * 2 + yo) * 2 + xo) * C
                    lane = (yo + dy) * 128
                    wf[row : row + C, lane : lane + 128] = tile_f
                    wb[row : row + C, lane : lane + 128] = tile_b
    whole(latp.at[0:6], h_recv)
    clear_ends(latp)

    for pair in range(4):
        pre = conv_pair(wf, latp, pair)
        cube = pre * pre
        th = jnp.tanh(0.7978845608028654 * pre * (1.0 + 0.044715 * cube))
        half = 0.5 * (1.0 + th)
        slope = half + 0.5 * pre * (1.0 - th * th) * (
            0.7978845608028654 * (1.0 + 3.0 * 0.044715 * cube)
        )
        own = latp[2 * pair + 1 : 2 * pair + 3, 1:3].reshape(4 * C, NZ).astype(F32)
        out = (own + pre * half).astype(BF).astype(F32)
        grads = []
        for yo in range(2):
            for x in range(CX):
                row = x * CY + 2 * pair + yo
                n = (yo * CX + x) * C
                field[row : row + 1, :] = jnp.sum(
                    out[n : n + C] * read_col, axis=0, keepdims=True
                )
                grads.append(read_col * acc[COLS * C + row : COLS * C + row + 1, :])
        grad_out = jnp.concatenate(grads, axis=0)
        gout[128 * pair : 128 * pair + 128, :] = grad_out
        grad_pre = (grad_out * slope).astype(BF)
        gp[2 * pair + 1 : 2 * pair + 3, 1:3] = grad_pre.reshape(2, 2, C, NZ)
        wide = grad_pre.astype(F32)
        gs[pair, 0:128, :] = shifted(wide, -1).astype(BF)
        gs[pair, 128:256, :] = grad_pre
        gs[pair, 256:384, :] = shifted(wide, 1).astype(BF)
    halos2 = halo_copies(gp, i_send, i_recv)
    for copy in halos2:
        copy.start()

    tap = jnp.zeros((4 * 4 * C, 3 * 128), F32)
    for pair in range(4):
        window = latp[2 * pair : 2 * pair + 4].reshape(4 * 4 * C, NZ)
        tap = tap + dot(window, gs[pair], 1, 1)
    quarter = lax.broadcasted_iota(jnp.int32, (C, 128), 1) // C
    quarter8 = lax.broadcasted_iota(jnp.int32, (8, 128), 1) // C
    for dx in range(3):
        for dy in range(3):
            for dz in range(3):
                total = jnp.zeros((C, 128), F32)
                for yo in range(2):
                    for xo in range(2):
                        n = ((yo + dy) * 4 + xo + dx) * C
                        piece = tap[n : n + C, dz * 128 : dz * 128 + 128]
                        total = jnp.where(quarter == 2 * yo + xo, piece, total)
                total = total + pltpu.roll(total, 64, 1)
                total = total + pltpu.roll(total, 32, 1)
                packed = total[0:8]
                for q in range(1, 4):
                    packed = jnp.where(quarter8 == q, total[8 * q : 8 * q + 8], packed)
                redsrc[9 * dx + 3 * dy + dz] = packed
    redsrc[TAPS:GX] = jnp.zeros((GX - TAPS, 8, 128), F32)

    def taps_copy(k):
        to = partner(mx, k, 1)
        return pltpu.make_async_remote_copy(
            src_ref=redsrc.at[to], dst_ref=red1.at[mx],
            send_sem=a_send, recv_sem=a_recv,
            device_id=(to, my), device_id_type=MESH,
        )

    @pl.loop(1, GX)
    def _(k):
        taps_copy(k).start()

    scalar = field[...]
    scalar_hi = scalar.astype(BF)
    scalar_lo = (scalar - scalar_hi.astype(F32)).astype(BF)
    scalars = jnp.concatenate([scalar_hi, scalar_lo], axis=0)

    def pred_copy(k):
        to = partner(mx, k, -1)
        return pltpu.make_async_remote_copy(
            src_ref=predmsg.at[k, 0:CAP], dst_ref=predr.at[slab, 0:CAP],
            send_sem=p_send, recv_sem=p_recv,
            device_id=(to, my), device_id_type=MESH,
        )

    @pl.loop(0, GROUPS)
    def _(g):
        got = dot(scalars, zs[g])
        total = jnp.sum((got[0:COLS] + got[COLS:]) * planes[g], axis=0, keepdims=True)
        for n in range(GROUP):
            k = GROUP * g + n
            for r in range(CAP):
                lane = n * PTS + r * BLK
                predmsg[k, r : r + 1, :] = total[:, lane : lane + BLK]
            if n == 0:

                @pl.when(g > 0)
                def _():
                    pred_copy(GROUP * g).start()

            else:
                pred_copy(k).start()

    predr[slab, 0:CAP, :] = predmsg[0, 0:CAP, :]

    whole(gp.at[0:6], i_recv)
    clear_ends(gp)
    for pair in range(4):
        back = conv_pair(wb, gp, pair)
        gl[128 * pair : 128 * pair + 128, :] = (
            gout[128 * pair : 128 * pair + 128, :] + back
        ).astype(BF)

    def feats_copy(k):
        to = partner(mx, k, -1)
        return pltpu.make_async_remote_copy(
            src_ref=gfs.at[k], dst_ref=gfr.at[pl.ds(CAP * slab, CAP)],
            send_sem=f_send, recv_sem=f_recv,
            device_id=(to, my), device_id_type=MESH,
        )

    def rows_copy(k):
        return pltpu.make_async_remote_copy(
            src_ref=red2.at[my], dst_ref=red2.at[my],
            send_sem=b_send, recv_sem=b_recv,
            device_id=(mx, lax.rem(my + k, GY)), device_id_type=MESH,
        )

    def collect(g):
        got = dot(gl[...], zs[g])
        total = jnp.zeros((C, WIDE), F32)
        for y in range(CY):
            for x in range(CX):
                n = (y * CX + x) * C
                total = total + got[n : n + C] * planes[g, x * CY + y : x * CY + y + 1, :]
        return total.astype(BF)

    def finish(g, total):
        back = dot(lift_w, total).astype(BF)
        for n in range(GROUP):
            for r in range(CAP):
                lane = n * PTS + r * BLK
                gfs[GROUP * g + n, r] = back[:, lane : lane + BLK]

    def send_back(g):
        for n in range(GROUP):
            feats_copy(GROUP * g + n).start()

    def step(g):
        before = held[...]
        total = collect(g)
        finish(g - 1, before)
        held[...] = total
        send_back(g - 1)

    held[...] = collect(1)

    @pl.loop(2, 4)
    def _(g):
        step(g)

    red1[mx] = redsrc[mx]

    whole(red1.at[0 : GX - 1], a_recv)
    red2[my] = jnp.sum(red1[...], axis=0)
    for k in range(1, GY):
        rows_copy(k).start()

    @pl.loop(4, GROUPS)
    def _(g):
        step(g)

    whole(red2.at[0 : GY - 1], b_recv)
    red3[mx] = (red2[0] + red2[1] + red2[2] + red2[3]) * (1.0 / GX)

    def total_copy(k):
        to = partner(mx, k, 1)
        return pltpu.make_async_remote_copy(
            src_ref=red3.at[mx], dst_ref=red3.at[mx],
            send_sem=c_send, recv_sem=c_recv,
            device_id=(to, my), device_id_type=MESH,
        )

    @pl.loop(1, GX)
    def _(k):
        total_copy(k).start()

    before = held[...]
    total = collect(0)
    finish(GROUPS - 1, before)
    send_back(GROUPS - 1)
    finish(0, total)
    for n in range(1, GROUP):
        feats_copy(n).start()
    gfr[pl.ds(CAP * slab, CAP)] = gfs[0]

    for sem in (p_recv, p_send):
        whole(predr.at[0 : GX - 1, 0:CAP], sem)
    for sem in (c_recv, c_send, a_send):
        whole(red3.at[0 : GX - 1], sem)
    for sem in (f_recv, f_send):
        whole(gfr.at[0 : CAP * (GX - 1)], sem)
    whole(red2.at[0 : GY - 1], b_send)
    whole(latp.at[0:6], h_send)
    whole(gp.at[0:6], i_send)
    whole(recv.at[0 : GX - 1], s_send)


def finish_kernel(
    gfr, predr, red3, alive, table, pred_out, feats_out, conv_out,
    slots, pred, feats, conv, sems,
):
    to_slots = pltpu.make_async_copy(table, slots, sems.at[0])
    to_slots.start()
    for d in range(TAPS):
        packed = red3[d]
        for q in range(4):
            piece = packed if q == 0 else pltpu.roll(packed, 128 - C * q, 1)
            conv[d, 8 * q : 8 * q + 8, :] = piece[:, 0:C]
    copies = [pltpu.make_async_copy(conv, conv_out, sems.at[1])]
    copies[0].start()
    to_slots.wait()
    for part in range(4):

        @pl.loop(8 * part, 8 * part + 8)
        def _(j):
            s = slots[1, j]
            keep = alive[pl.ds(j, 1), :]
            feats[j] = (gfr[s].astype(F32) * keep).astype(BF)
            both = predr[s // CAP]
            value = jnp.where(lax.rem(s, CAP) == 0, both[0:1], both[1:2])
            pred[pl.ds(j, 1), :] = value * keep

        span = pl.ds(8 * part, 8)
        copies.append(pltpu.make_async_copy(feats.at[span], feats_out.at[span], sems.at[2 + part]))
        copies[-1].start()
    copies.append(pltpu.make_async_copy(pred, pred_out, sems.at[6]))
    copies[-1].start()
    for copy in copies:
        copy.wait()


def local(
    point_feats, point_offsets, base_cells, block_owners, point_counts,
    lift_weight, conv_weight, read_weight, cotangent,
):
    hbm = pl.BlockSpec(memory_space=pltpu.HBM)
    vmem = pl.BlockSpec(memory_space=pltpu.VMEM)
    dma = pltpu.SemaphoreType.DMA
    inputs = (
        point_feats, jnp.transpose(point_offsets, (1, 0, 2)), base_cells,
        block_owners.reshape(1, NB), point_counts.reshape(1, 1), lift_weight, conv_weight,
        read_weight.reshape(1, C), cotangent,
    )
    parts = pl.pallas_call(
        kernel,
        out_shape=(
            pltpu.VMEM((GX * CAP, C, BLK), BF),
            pltpu.VMEM((GX, 8, BLK), F32),
            pltpu.VMEM((GX, 8, 128), F32),
            pltpu.VMEM((NB, BLK), F32),
            pltpu.VMEM((8, BLK), jnp.int32),
        ),
        in_specs=[hbm] * 9,
        out_specs=(vmem,) * 5,
        scratch_shapes=[
            pltpu.VMEM((NB, C, BLK), BF),
            pltpu.VMEM((3, NB, BLK), BF),
            pltpu.VMEM((NB, BLK), jnp.int32),
            pltpu.VMEM((1, NB), jnp.int32),
            pltpu.VMEM((1, 1), jnp.int32),
            pltpu.VMEM((C, C), BF),
            pltpu.VMEM((TAPS, C, C), BF),
            pltpu.VMEM((1, C), BF),
            pltpu.VMEM((NB, BLK), F32),
            pltpu.SMEM((8, BLK), jnp.int32),
            pltpu.VMEM((NB, 8, BLK), F32),
            dma((10,)),
            pltpu.VMEM((GX, CAP * C + 16, BLK), BF),
            pltpu.VMEM((GX, CAP * C + 16, BLK), BF),
            pltpu.VMEM((COLS * C + COLS, NZ), F32),
            pltpu.VMEM((GROUPS, NZ, WIDE), BF),
            pltpu.VMEM((GROUPS, COLS, WIDE), F32),
            pltpu.VMEM((10, 4, C, NZ), BF),
            pltpu.VMEM((10, 4, C, NZ), BF),
            pltpu.VMEM((4, 3 * 128, NZ), BF),
            pltpu.VMEM((3 * 128, 512), BF),
            pltpu.VMEM((3 * 128, 512), BF),
            pltpu.VMEM((COLS * C, NZ), F32),
            pltpu.VMEM((COLS, NZ), F32),
            pltpu.VMEM((COLS * C, NZ), BF),
            pltpu.VMEM((GX, 8, BLK), F32),
            pltpu.VMEM((C, WIDE), BF),
            pltpu.VMEM((GX, CAP, C, BLK), BF),
            pltpu.VMEM((GX, 8, 128), F32),
            pltpu.VMEM((GX, 8, 128), F32),
            pltpu.VMEM((GY, 8, 128), F32),
            dma, dma((GROUPS,)), dma, dma, dma, dma, dma, dma, dma, dma, dma, dma, dma, dma, dma, dma,
        ],
        compiler_params=pltpu.CompilerParams(
            collective_id=0, has_side_effects=True, vmem_limit_bytes=40 * 1024 * 1024
        ),
        cost_estimate=pl.CostEstimate(
            flops=8_000_000_000, bytes_accessed=2_000_000, transcendentals=1_000_000
        ),
    )(*(x if x.size == 1 else pltpu.with_memory_space_constraint(x, pltpu.HBM) for x in inputs))
    return pl.pallas_call(
        finish_kernel,
        out_shape=(
            jax.ShapeDtypeStruct((NB, BLK), F32),
            jax.ShapeDtypeStruct((NB, C, BLK), BF),
            jax.ShapeDtypeStruct((TAPS, C, C), F32),
        ),
        in_specs=[vmem] * 5,
        out_specs=(hbm,) * 3,
        scratch_shapes=[
            pltpu.SMEM((8, BLK), jnp.int32),
            pltpu.VMEM((NB, BLK), F32),
            pltpu.VMEM((NB, C, BLK), BF),
            pltpu.VMEM((TAPS, C, C), F32),
            dma((7,)),
        ],
        compiler_params=pltpu.CompilerParams(vmem_limit_bytes=8 * 1024 * 1024),
    )(*(pltpu.with_memory_space_constraint(x, pltpu.VMEM) for x in parts))


def solution(mesh):
    in_specs = (
        P(("gx", "gy"), None, None),
        P(("gx", "gy"), None, None),
        P(("gx", "gy"), None),
        P(("gx", "gy"), None),
        P(("gx", "gy")),
        P(),
        P(),
        P(),
        P(("gx", "gy"), None),
    )
    out_specs = (P(("gx", "gy"), None), P(("gx", "gy"), None, None), P())
    return jax.shard_map(local, mesh=mesh, in_specs=in_specs, out_specs=out_specs, check_vma=False)
```

```python
import functools

import jax
import jax.numpy as jnp
from jax import lax
from jax.experimental import pallas as pl
from jax.experimental.pallas import tpu as pltpu
from jax.sharding import PartitionSpec as P

C = 32
CX = 2
CY = 8
NZ = 256
NB = 32
BLK = 128
GX = 32
GY = 4
CAP = 2
PTS = CAP * BLK
GROUP = 4
GROUPS = GX // GROUP
WIDE = GROUP * PTS
COLS = CX * CY
TAPS = 27
MESH = pl.DeviceIdType.MESH
BF = jnp.bfloat16
F32 = jnp.float32


def partner(mx, n, sign):
    return lax.rem(mx + sign * lax.rem(11 * n, GX) + GX, GX)


def snake(index):
    x, z, core = index // 8, lax.rem(index // 2, 4), lax.rem(index, 2)
    return x * 8 + (z + lax.rem(x, 2) * (3 - 2 * z)) * 2 + core


def whole(ref, sem):
    pltpu.make_async_copy(ref, ref, sem).wait()


def dot(a, b, ca=1, cb=0):
    return lax.dot_general(a, b, (((ca,), (cb,)), ((), ())), preferred_element_type=F32)


def shifted(values, step):
    lanes = lax.broadcasted_iota(jnp.int32, values.shape, 1)
    if step == 1:
        return jnp.where(lanes == 0, 0.0, pltpu.roll(values, 1, 1))
    return jnp.where(lanes == NZ - 1, 0.0, pltpu.roll(values, NZ - 1, 1))


def conv_pair(weights, padded, pair):
    window = padded[2 * pair : 2 * pair + 4].reshape(4 * 4 * C, NZ)
    part = dot(weights[...], window)
    return shifted(part[0:128], 1) + part[128:256] + shifted(part[256:384], -1)


def kernel(
    feats_hbm, offsets_hbm, base_hbm, owners_hbm, count_hbm, lift_hbm, conv_hbm, read_hbm, cot_hbm,
    pred_out, feats_out, conv_out,
    feats, offsets, base, owners, count, lift, conv, read, cot, table, slots, aux, gfr, predr, red3, in_sem, send, recv, acc, zs, planes, latp, gp, gs, wf, wb,
    gout, field, gl, predmsg, held, gfs, redsrc, red1, red2,
    s_send, s_recv, h_send, h_recv, i_send, i_recv, p_send, p_recv,
    f_send, f_recv, a_send, a_recv, b_send, b_recv, c_send, c_recv,
):
    mx = lax.axis_index("gx")
    my = lax.axis_index("gy")
    slab = snake(mx)
    right, left = snake(lax.rem(slab + 1, GX)), snake(lax.rem(slab + GX - 1, GX))
    up, down = lax.rem(my + 1, GY), lax.rem(my + GY - 1, GY)

    pairs = {
        "owners": (owners_hbm, owners), "offsets": (offsets_hbm, offsets), "base": (base_hbm, base),
        "count": (count_hbm, count), "cot": (cot_hbm, cot), "feats": (feats_hbm, feats),
        "lift": (lift_hbm, lift), "conv": (conv_hbm, conv), "read": (read_hbm, read),
    }
    fetched = {
        name: pltpu.make_async_copy(src, dst, in_sem.at[n])
        for n, (name, (src, dst)) in enumerate(pairs.items())
    }
    for copy in fetched.values():
        copy.start()

    barrier = pltpu.get_barrier_semaphore()

    @pl.loop(1, GX)
    def _(k):
        pl.semaphore_signal(barrier, inc=1, device_id=(lax.rem(mx + k, GX), my), device_id_type=MESH)

    for k in range(1, GY):
        pl.semaphore_signal(barrier, inc=1, device_id=(mx, lax.rem(my + k, GY)), device_id_type=MESH)

    fetched["owners"].wait()
    named = owners[...]
    rows32 = lax.broadcasted_iota(jnp.int32, (NB, NB), 0)
    lanes32 = lax.broadcasted_iota(jnp.int32, (NB, NB), 1)
    named_col = jnp.sum(jnp.where(rows32 == lanes32, named, 0), axis=1, keepdims=True)
    earlier = (named_col == named) & (rows32 < lanes32)
    slot_row = CAP * named + jnp.sum(jnp.where(earlier, 1, 0), axis=0, keepdims=True)
    slot_col = jnp.sum(jnp.where(rows32 == lanes32, slot_row, 0), axis=1, keepdims=True)
    rows = lax.broadcasted_iota(jnp.int32, (NB, BLK), 0)
    lanes = lax.broadcasted_iota(jnp.int32, (NB, BLK), 1)
    table[0:1, :] = jnp.sum(jnp.where(slot_col == lanes, rows + 1, 0), axis=0, keepdims=True) - 1
    table[1:2, :] = jnp.sum(jnp.where(rows == lanes, slot_col, 0), axis=0, keepdims=True)
    table[2:8, :] = jnp.zeros((6, BLK), jnp.int32)
    to_slots = pltpu.make_async_copy(table, slots, in_sem.at[9])
    to_slots.start()

    for name in ("offsets", "base", "count", "cot"):
        fetched[name].wait()
    cells = base[...].astype(F32)
    cell_y = jnp.floor((cells + 0.5) * (1.0 / (NZ - 1)))
    alive = jnp.where(rows * BLK + lanes < count[...], 1.0, 0.0)
    grad = cot[...] * alive
    high = grad.astype(BF).astype(F32)
    tile_rows = [offsets[n].astype(F32) for n in range(3)]
    tile_rows += [cell_y, cells - cell_y * (NZ - 1.0), high, grad - high, alive]
    for n, value in enumerate(tile_rows):
        aux[:, n, :] = value
    for name in ("lift", "feats"):
        fetched[name].wait()
    lift_w = lift[...]
    for part in range(4):
        raw = jnp.concatenate([feats[8 * part + n] for n in range(8)], axis=1)
        lifted = dot(lift_w, raw, 0, 0).astype(BF)
        for n in range(8):
            feats[8 * part + n] = lifted[:, n * BLK : (n + 1) * BLK]
    to_slots.wait()

    def place(to):
        o = snake(to)
        tails = []
        for r in range(CAP):
            j = slots[0, CAP * o + r]
            jj = jnp.maximum(j, 0)
            here = jnp.where(j >= 0, 1.0, 0.0)
            tail = aux[jj] * here
            send[to, r * C : (r + 1) * C, :] = (feats[jj].astype(F32) * tail[7:8]).astype(BF)
            tails.append(tail)
        send[to, CAP * C : CAP * C + 16, :] = jnp.concatenate(tails, axis=0).astype(BF)

    def points_copy(k):
        to = partner(mx, k, 1)
        return pltpu.make_async_remote_copy(
            src_ref=send.at[to], dst_ref=recv.at[mx],
            send_sem=s_send, recv_sem=s_recv.at[k // GROUP],
            device_id=(to, my), device_id_type=MESH,
        )

    pl.semaphore_wait(barrier, GX - 1 + GY - 1)

    @pl.loop(1, GX)
    def _(k):
        place(partner(mx, k, 1))
        points_copy(k).start()

    place(mx)
    recv[mx] = send[mx]

    for name in ("conv", "read"):
        fetched[name].wait()
    eye = jnp.where(
        lax.broadcasted_iota(jnp.int32, (C, C), 0) == lax.broadcasted_iota(jnp.int32, (C, C), 1),
        1.0, 0.0,
    )
    read_col = dot((eye * read[...].astype(F32)).astype(BF), jnp.ones((C, NZ), BF))

    sub_z = lax.broadcasted_iota(jnp.int32, (NZ, WIDE), 0).astype(F32)
    sub_y = lax.broadcasted_iota(jnp.int32, (CY, WIDE), 0).astype(F32)
    acc[...] = jnp.zeros(acc.shape, F32)

    @pl.loop(0, GROUPS)
    def _(g):
        blocks, tails = [], []

        @pl.when(g == 0)
        def _():
            whole(recv.at[0 : GROUP - 1], s_recv.at[0])

        @pl.when(g > 0)
        def _():
            whole(recv.at[0:GROUP], s_recv.at[g])

        for n in range(GROUP):
            msg = recv[partner(mx, GROUP * g + n, -1)]
            blocks += [msg[0:C], msg[C : 2 * C]]
            tail = msg[2 * C : 2 * C + 16].astype(F32)
            tails += [tail[0:8], tail[8:16]]
        block = jnp.concatenate(blocks, axis=1)
        tail = jnp.concatenate(tails, axis=1)
        near = jnp.exp(-2.0 * tail * tail)
        far = jnp.exp(-2.0 * (tail - 1.0) * (tail - 1.0))
        at_y, at_z = tail[3:4], tail[4:5]
        slope = tail[5:6] + tail[6:7]
        wy = jnp.where(sub_y == at_y, near[1:2], jnp.where(sub_y == at_y + 1.0, far[1:2], 0.0))
        plane = (near[0:1] * wy, far[0:1] * wy)
        planes[g, 0:CY, :] = plane[0]
        planes[g, CY : 2 * CY, :] = plane[1]
        z = jnp.where(sub_z == at_z, near[2:3], jnp.where(sub_z == at_z + 1.0, far[2:3], 0.0))
        z = z.astype(BF)
        zs[g] = z
        lifted = block.astype(F32)
        rows = [
            (lifted * plane[x][y : y + 1]).astype(BF) for y in range(CY) for x in range(CX)
        ]
        rows.append(jnp.concatenate([plane[0] * slope, plane[1] * slope], axis=0).astype(BF))
        acc[...] += dot(jnp.concatenate(rows, axis=0), z, 1, 1)

    def halo_copies(buf, sends, recvs):
        ends = (
            (right, up, buf.at[8, 2], buf.at[0, 0]),
            (right, down, buf.at[1, 2], buf.at[9, 0]),
            (left, up, buf.at[8, 1], buf.at[0, 3]),
            (left, down, buf.at[1, 1], buf.at[9, 3]),
            (mx, up, buf.at[8, 1:3], buf.at[0, 1:3]),
            (mx, down, buf.at[1, 1:3], buf.at[9, 1:3]),
            (right, my, buf.at[1:9, 2], buf.at[1:9, 0]),
            (left, my, buf.at[1:9, 1], buf.at[1:9, 3]),
        )
        return [
            pltpu.make_async_remote_copy(
                src_ref=src, dst_ref=dst, send_sem=sends, recv_sem=recvs,
                device_id=(px, py), device_id_type=MESH,
            )
            for n, (px, py, src, dst) in enumerate(ends)
        ]

    def clear_ends(buf):
        @pl.when(slab == 0)
        def _():
            buf[:, 0] = jnp.zeros((10, C, NZ), BF)

        @pl.when(slab == GX - 1)
        def _():
            buf[:, 3] = jnp.zeros((10, C, NZ), BF)

        @pl.when(my == 0)
        def _():
            buf[0] = jnp.zeros((4, C, NZ), BF)

        @pl.when(my == GY - 1)
        def _():
            buf[9] = jnp.zeros((4, C, NZ), BF)

    for y in range(CY):
        for x in range(CX):
            row = (y * CX + x) * C
            latp[y + 1, x + 1] = acc[row : row + C, :].astype(BF)
    halos = halo_copies(latp, h_send, h_recv)
    for copy in halos:
        copy.start()

    def place_tap(xp):
        lanes = lax.broadcasted_iota(jnp.int32, (C, 128), 1)
        rows = lax.broadcasted_iota(jnp.int32, (C, 128), 0)
        return jnp.where(lanes == rows + C * xp, 1.0, 0.0).astype(BF)

    spots = [place_tap(xp) for xp in range(4)]
    wf[...] = jnp.zeros(wf.shape, BF)
    wb[...] = jnp.zeros(wb.shape, BF)
    for dz in range(3):
        for dy in range(3):
            for xo in range(2):
                tile_f = sum(
                    dot(conv[9 * dx + 3 * dy + dz], spots[dx + xo], 0, 0) for dx in range(3)
                ).astype(BF)
                tile_b = sum(
                    dot(conv[9 * (2 - dx) + 3 * (2 - dy) + (2 - dz)], spots[dx + xo])
                    for dx in range(3)
                ).astype(BF)
                for yo in range(2):
                    row = ((dz * 2 + yo) * 2 + xo) * C
                    lane = (yo + dy) * 128
                    wf[row : row + C, lane : lane + 128] = tile_f
                    wb[row : row + C, lane : lane + 128] = tile_b
    whole(latp.at[0:6], h_recv)
    clear_ends(latp)

    for pair in range(4):
        pre = conv_pair(wf, latp, pair)
        cube = pre * pre
        th = jnp.tanh(0.7978845608028654 * pre * (1.0 + 0.044715 * cube))
        half = 0.5 * (1.0 + th)
        slope = half + 0.5 * pre * (1.0 - th * th) * (
            0.7978845608028654 * (1.0 + 3.0 * 0.044715 * cube)
        )
        own = latp[2 * pair + 1 : 2 * pair + 3, 1:3].reshape(4 * C, NZ).astype(F32)
        out = (own + pre * half).astype(BF).astype(F32)
        grads = []
        for yo in range(2):
            for x in range(CX):
                row = x * CY + 2 * pair + yo
                n = (yo * CX + x) * C
                field[row : row + 1, :] = jnp.sum(
                    out[n : n + C] * read_col, axis=0, keepdims=True
                )
                grads.append(read_col * acc[COLS * C + row : COLS * C + row + 1, :])
        grad_out = jnp.concatenate(grads, axis=0)
        gout[128 * pair : 128 * pair + 128, :] = grad_out
        grad_pre = (grad_out * slope).astype(BF)
        gp[2 * pair + 1 : 2 * pair + 3, 1:3] = grad_pre.reshape(2, 2, C, NZ)
        wide = grad_pre.astype(F32)
        gs[pair, 0:128, :] = shifted(wide, -1).astype(BF)
        gs[pair, 128:256, :] = grad_pre
        gs[pair, 256:384, :] = shifted(wide, 1).astype(BF)
    halos2 = halo_copies(gp, i_send, i_recv)
    for copy in halos2:
        copy.start()

    windows = [latp[2 * pair : 2 * pair + 4].reshape(4 * 4 * C, NZ) for pair in range(4)]
    tap = dot(
        jnp.concatenate(windows, axis=1),
        jnp.concatenate([gs[pair] for pair in range(4)], axis=1), 1, 1,
    )
    quarter = lax.broadcasted_iota(jnp.int32, (C, 128), 1) // C
    quarter8 = lax.broadcasted_iota(jnp.int32, (8, 128), 1) // C
    for dx in range(3):
        for dy in range(3):
            for dz in range(3):
                total = jnp.zeros((C, 128), F32)
                for yo in range(2):
                    for xo in range(2):
                        n = ((yo + dy) * 4 + xo + dx) * C
                        piece = tap[n : n + C, dz * 128 : dz * 128 + 128]
                        total = jnp.where(quarter == 2 * yo + xo, piece, total)
                total = total + pltpu.roll(total, 64, 1)
                total = total + pltpu.roll(total, 32, 1)
                packed = total[0:8]
                for q in range(1, 4):
                    packed = jnp.where(quarter8 == q, total[8 * q : 8 * q + 8], packed)
                redsrc[9 * dx + 3 * dy + dz] = packed
    redsrc[TAPS:GX] = jnp.zeros((GX - TAPS, 8, 128), F32)

    def taps_copy(k):
        to = partner(mx, k, 1)
        return pltpu.make_async_remote_copy(
            src_ref=redsrc.at[to], dst_ref=red1.at[mx],
            send_sem=a_send, recv_sem=a_recv,
            device_id=(to, my), device_id_type=MESH,
        )

    @pl.loop(1, GX)
    def _(k):
        taps_copy(k).start()

    scalar = field[...]
    scalar_hi = scalar.astype(BF)
    scalar_lo = (scalar - scalar_hi.astype(F32)).astype(BF)
    scalars = jnp.concatenate([scalar_hi, scalar_lo], axis=0)

    def pred_copy(k):
        to = partner(mx, k, -1)
        return pltpu.make_async_remote_copy(
            src_ref=predmsg.at[k, 0:CAP], dst_ref=predr.at[slab, 0:CAP],
            send_sem=p_send, recv_sem=p_recv,
            device_id=(to, my), device_id_type=MESH,
        )

    @pl.loop(0, GROUPS)
    def _(g):
        got = dot(scalars, zs[g])
        total = jnp.sum((got[0:COLS] + got[COLS:]) * planes[g], axis=0, keepdims=True)
        for n in range(GROUP):
            k = GROUP * g + n
            for r in range(CAP):
                lane = n * PTS + r * BLK
                predmsg[k, r : r + 1, :] = total[:, lane : lane + BLK]
            if n == 0:

                @pl.when(g > 0)
                def _():
                    pred_copy(GROUP * g).start()

            else:
                pred_copy(k).start()

    predr[slab, 0:CAP, :] = predmsg[0, 0:CAP, :]

    whole(gp.at[0:6], i_recv)
    clear_ends(gp)
    for pair in range(4):
        back = conv_pair(wb, gp, pair)
        gl[128 * pair : 128 * pair + 128, :] = (
            gout[128 * pair : 128 * pair + 128, :] + back
        ).astype(BF)

    def feats_copy(k):
        to = partner(mx, k, -1)
        return pltpu.make_async_remote_copy(
            src_ref=gfs.at[k], dst_ref=gfr.at[pl.ds(CAP * slab, CAP)],
            send_sem=f_send, recv_sem=f_recv,
            device_id=(to, my), device_id_type=MESH,
        )

    def rows_copy(k):
        return pltpu.make_async_remote_copy(
            src_ref=red2.at[my], dst_ref=red2.at[my],
            send_sem=b_send, recv_sem=b_recv,
            device_id=(mx, lax.rem(my + k, GY)), device_id_type=MESH,
        )

    def collect(g):
        got = dot(gl[...], zs[g])
        total = jnp.zeros((C, WIDE), F32)
        for y in range(CY):
            for x in range(CX):
                n = (y * CX + x) * C
                total = total + got[n : n + C] * planes[g, x * CY + y : x * CY + y + 1, :]
        return total.astype(BF)

    def finish(g, total):
        back = dot(lift_w, total).astype(BF)
        for n in range(GROUP):
            for r in range(CAP):
                lane = n * PTS + r * BLK
                gfs[GROUP * g + n, r] = back[:, lane : lane + BLK]

    def send_back(g):
        for n in range(GROUP):
            feats_copy(GROUP * g + n).start()

    def step(g):
        before = held[...]
        total = collect(g)
        finish(g - 1, before)
        held[...] = total
        send_back(g - 1)

    held[...] = collect(1)

    @pl.loop(2, 5)
    def _(g):
        step(g)

    red1[mx] = redsrc[mx]

    whole(red1.at[0 : GX - 1], a_recv)
    red2[my] = jnp.sum(red1[...], axis=0)
    for k in range(1, GY):
        rows_copy(k).start()

    @pl.loop(5, GROUPS)
    def _(g):
        step(g)

    before = held[...]
    total = collect(0)
    finish(GROUPS - 1, before)
    send_back(GROUPS - 1)
    finish(0, total)
    for n in range(1, GROUP):
        feats_copy(n).start()
    gfr[pl.ds(CAP * slab, CAP)] = gfs[0]

    whole(red2.at[0 : GY - 1], b_recv)
    red3[mx] = (red2[0] + red2[1] + red2[2] + red2[3]) * (1.0 / GX)

    def total_copy(k):
        to = partner(mx, k, 1)
        return pltpu.make_async_remote_copy(
            src_ref=red3.at[mx], dst_ref=red3.at[mx],
            send_sem=c_send, recv_sem=c_recv,
            device_id=(to, my), device_id_type=MESH,
        )

    @pl.loop(1, GX)
    def _(k):
        total_copy(k).start()

    whole(predr.at[0 : GX - 1, 0:CAP], p_recv)
    whole(gfr.at[0 : CAP * (GX - 1)], f_recv)

    @pl.loop(0, NB)
    def _(j):
        s = slots[1, j]
        keep = aux[j, 7:8, :]
        feats_out[j] = (gfr[s].astype(F32) * keep).astype(BF)
        both = predr[s // CAP]
        value = jnp.where(lax.rem(s, CAP) == 0, both[0:1], both[1:2])
        pred_out[pl.ds(j, 1), :] = value * keep

    whole(red3.at[0 : GX - 1], c_recv)
    for d in range(TAPS):
        packed = red3[d]
        for q in range(4):
            piece = packed if q == 0 else pltpu.roll(packed, 128 - C * q, 1)
            conv_out[d, 8 * q : 8 * q + 8, :] = piece[:, 0:C]

    whole(predr.at[0 : GX - 1, 0:CAP], p_send)
    whole(gfr.at[0 : CAP * (GX - 1)], f_send)
    for sem in (c_send, a_send):
        whole(red3.at[0 : GX - 1], sem)
    whole(red2.at[0 : GY - 1], b_send)
    whole(latp.at[0:6], h_send)
    whole(gp.at[0:6], i_send)
    whole(recv.at[0 : GX - 1], s_send)


def finish_kernel(pred, feats, conv, pred_out, feats_out, conv_out, sems):
    copies = [
        pltpu.make_async_copy(src, dst, sems.at[n])
        for n, (src, dst) in enumerate(((conv, conv_out), (feats, feats_out), (pred, pred_out)))
    ]
    for copy in copies:
        copy.start()
    for copy in copies:
        copy.wait()


def local(
    point_feats, point_offsets, base_cells, block_owners, point_counts,
    lift_weight, conv_weight, read_weight, cotangent,
):
    hbm = pl.BlockSpec(memory_space=pltpu.HBM)
    vmem = pl.BlockSpec(memory_space=pltpu.VMEM)
    dma = pltpu.SemaphoreType.DMA
    inputs = (
        point_feats, jnp.transpose(point_offsets, (1, 0, 2)), base_cells,
        block_owners.reshape(1, NB), point_counts.reshape(1, 1), lift_weight, conv_weight,
        read_weight.reshape(1, C), cotangent,
    )
    parts = pl.pallas_call(
        kernel,
        out_shape=(
            pltpu.VMEM((NB, BLK), F32),
            pltpu.VMEM((NB, C, BLK), BF),
            pltpu.VMEM((TAPS, C, C), F32),
        ),
        in_specs=[hbm] * 9,
        out_specs=(vmem,) * 3,
        scratch_shapes=[
            pltpu.VMEM((NB, C, BLK), BF),
            pltpu.VMEM((3, NB, BLK), BF),
            pltpu.VMEM((NB, BLK), jnp.int32),
            pltpu.VMEM((1, NB), jnp.int32),
            pltpu.VMEM((1, 1), jnp.int32),
            pltpu.VMEM((C, C), BF),
            pltpu.VMEM((TAPS, C, C), BF),
            pltpu.VMEM((1, C), BF),
            pltpu.VMEM((NB, BLK), F32),
            pltpu.VMEM((8, BLK), jnp.int32),
            pltpu.SMEM((8, BLK), jnp.int32),
            pltpu.VMEM((NB, 8, BLK), F32),
            pltpu.VMEM((GX * CAP, C, BLK), BF),
            pltpu.VMEM((GX, 8, BLK), F32),
            pltpu.VMEM((GX, 8, 128), F32),
            dma((10,)),
            pltpu.VMEM((GX, CAP * C + 16, BLK), BF),
            pltpu.VMEM((GX, CAP * C + 16, BLK), BF),
            pltpu.VMEM((COLS * C + COLS, NZ), F32),
            pltpu.VMEM((GROUPS, NZ, WIDE), BF),
            pltpu.VMEM((GROUPS, COLS, WIDE), F32),
            pltpu.VMEM((10, 4, C, NZ), BF),
            pltpu.VMEM((10, 4, C, NZ), BF),
            pltpu.VMEM((4, 3 * 128, NZ), BF),
            pltpu.VMEM((3 * 128, 512), BF),
            pltpu.VMEM((3 * 128, 512), BF),
            pltpu.VMEM((COLS * C, NZ), F32),
            pltpu.VMEM((COLS, NZ), F32),
            pltpu.VMEM((COLS * C, NZ), BF),
            pltpu.VMEM((GX, 8, BLK), F32),
            pltpu.VMEM((C, WIDE), BF),
            pltpu.VMEM((GX, CAP, C, BLK), BF),
            pltpu.VMEM((GX, 8, 128), F32),
            pltpu.VMEM((GX, 8, 128), F32),
            pltpu.VMEM((GY, 8, 128), F32),
            dma, dma((GROUPS,)), dma, dma, dma, dma, dma, dma, dma, dma, dma, dma, dma, dma, dma, dma,
        ],
        compiler_params=pltpu.CompilerParams(
            collective_id=0, has_side_effects=True, vmem_limit_bytes=40 * 1024 * 1024
        ),
        cost_estimate=pl.CostEstimate(
            flops=8_000_000_000, bytes_accessed=2_000_000, transcendentals=1_000_000
        ),
    )(*(x if x.size == 1 else pltpu.with_memory_space_constraint(x, pltpu.HBM) for x in inputs))
    return pl.pallas_call(
        finish_kernel,
        out_shape=(
            jax.ShapeDtypeStruct((NB, BLK), F32),
            jax.ShapeDtypeStruct((NB, C, BLK), BF),
            jax.ShapeDtypeStruct((TAPS, C, C), F32),
        ),
        in_specs=[vmem] * 3,
        out_specs=(hbm,) * 3,
        scratch_shapes=[dma((3,))],
        compiler_params=pltpu.CompilerParams(vmem_limit_bytes=8 * 1024 * 1024),
    )(*(pltpu.with_memory_space_constraint(x, pltpu.VMEM) for x in parts))


def solution(mesh):
    in_specs = (
        P(("gx", "gy"), None, None),
        P(("gx", "gy"), None, None),
        P(("gx", "gy"), None),
        P(("gx", "gy"), None),
        P(("gx", "gy")),
        P(),
        P(),
        P(),
        P(("gx", "gy"), None),
    )
    out_specs = (P(("gx", "gy"), None), P(("gx", "gy"), None, None), P())
    return jax.shard_map(local, mesh=mesh, in_specs=in_specs, out_specs=out_specs, check_vma=False)
```

```python
import functools

import jax
import jax.numpy as jnp
from jax import lax
from jax.experimental import pallas as pl
from jax.experimental.pallas import tpu as pltpu
from jax.sharding import PartitionSpec as P

C = 32
CX = 2
CY = 8
NZ = 256
NB = 32
BLK = 128
GX = 32
GY = 4
CAP = 2
PTS = CAP * BLK
GROUP = 4
GROUPS = GX // GROUP
WIDE = GROUP * PTS
COLS = CX * CY
TAPS = 27
MESH = pl.DeviceIdType.MESH
BF = jnp.bfloat16
F32 = jnp.float32


def partner(mx, n, sign):
    return lax.rem(mx + sign * lax.rem(13 * n, GX) + GX, GX)


def snake(index):
    x, z, core = index // 8, lax.rem(index // 2, 4), lax.rem(index, 2)
    return x * 8 + (z + lax.rem(x, 2) * (3 - 2 * z)) * 2 + core


def whole(ref, sem):
    pltpu.make_async_copy(ref, ref, sem).wait()


def dot(a, b, ca=1, cb=0):
    return lax.dot_general(a, b, (((ca,), (cb,)), ((), ())), preferred_element_type=F32)


def shifted(values, step):
    lanes = lax.broadcasted_iota(jnp.int32, values.shape, 1)
    if step == 1:
        return jnp.where(lanes == 0, 0.0, pltpu.roll(values, 1, 1))
    return jnp.where(lanes == NZ - 1, 0.0, pltpu.roll(values, NZ - 1, 1))


def conv_pair(weights, padded, pair):
    window = padded[2 * pair : 2 * pair + 4].reshape(4 * 4 * C, NZ)
    part = dot(weights[...], window)
    return shifted(part[0:128], 1) + part[128:256] + shifted(part[256:384], -1)


def kernel(
    feats_hbm, offsets_hbm, base_hbm, owners_hbm, count_hbm, lift_hbm, conv_hbm, read_hbm, cot_hbm,
    pred_out, feats_out, conv_out,
    feats, offsets, base, owners, count, lift, conv, read, cot, table, slots, aux, gfr, predr, red3, in_sem, send, recv, acc, zs, planes, latp, gp, gs, wf, wb,
    gout, field, gl, predmsg, held, gfs, redsrc, red1, red2,
    s_send, s_recv, h_send, h_recv, i_send, i_recv, p_send, p_recv,
    f_send, f_recv, a_send, a_recv, b_send, b_recv, c_send, c_recv,
):
    mx = lax.axis_index("gx")
    my = lax.axis_index("gy")
    slab = snake(mx)
    right, left = snake(lax.rem(slab + 1, GX)), snake(lax.rem(slab + GX - 1, GX))
    up, down = lax.rem(my + 1, GY), lax.rem(my + GY - 1, GY)

    pairs = {
        "owners": (owners_hbm, owners), "offsets": (offsets_hbm, offsets), "base": (base_hbm, base),
        "count": (count_hbm, count), "cot": (cot_hbm, cot), "feats": (feats_hbm, feats),
        "lift": (lift_hbm, lift), "conv": (conv_hbm, conv), "read": (read_hbm, read),
    }
    fetched = {
        name: pltpu.make_async_copy(src, dst, in_sem.at[n])
        for n, (name, (src, dst)) in enumerate(pairs.items())
    }
    for copy in fetched.values():
        copy.start()

    barrier = pltpu.get_barrier_semaphore()

    @pl.loop(1, GX)
    def _(k):
        pl.semaphore_signal(barrier, inc=1, device_id=(lax.rem(mx + k, GX), my), device_id_type=MESH)

    for k in range(1, GY):
        pl.semaphore_signal(barrier, inc=1, device_id=(mx, lax.rem(my + k, GY)), device_id_type=MESH)

    fetched["owners"].wait()
    named = owners[...]
    rows32 = lax.broadcasted_iota(jnp.int32, (NB, NB), 0)
    lanes32 = lax.broadcasted_iota(jnp.int32, (NB, NB), 1)
    named_col = jnp.sum(jnp.where(rows32 == lanes32, named, 0), axis=1, keepdims=True)
    earlier = (named_col == named) & (rows32 < lanes32)
    slot_row = CAP * named + jnp.sum(jnp.where(earlier, 1, 0), axis=0, keepdims=True)
    slot_col = jnp.sum(jnp.where(rows32 == lanes32, slot_row, 0), axis=1, keepdims=True)
    rows = lax.broadcasted_iota(jnp.int32, (NB, BLK), 0)
    lanes = lax.broadcasted_iota(jnp.int32, (NB, BLK), 1)
    table[0:1, :] = jnp.sum(jnp.where(slot_col == lanes, rows + 1, 0), axis=0, keepdims=True) - 1
    table[1:2, :] = jnp.sum(jnp.where(rows == lanes, slot_col, 0), axis=0, keepdims=True)
    table[2:8, :] = jnp.zeros((6, BLK), jnp.int32)
    to_slots = pltpu.make_async_copy(table, slots, in_sem.at[9])
    to_slots.start()

    for name in ("offsets", "base", "count", "cot"):
        fetched[name].wait()
    cells = base[...].astype(F32)
    cell_y = jnp.floor((cells + 0.5) * (1.0 / (NZ - 1)))
    alive = jnp.where(rows * BLK + lanes < count[...], 1.0, 0.0)
    grad = cot[...] * alive
    high = grad.astype(BF).astype(F32)
    tile_rows = [offsets[n].astype(F32) for n in range(3)]
    tile_rows += [cell_y, cells - cell_y * (NZ - 1.0), high, grad - high, alive]
    for n, value in enumerate(tile_rows):
        aux[:, n, :] = value
    for name in ("lift", "feats"):
        fetched[name].wait()
    lift_w = lift[...]
    for part in range(4):
        raw = jnp.concatenate([feats[8 * part + n] for n in range(8)], axis=1)
        lifted = dot(lift_w, raw, 0, 0).astype(BF)
        for n in range(8):
            feats[8 * part + n] = lifted[:, n * BLK : (n + 1) * BLK]
    to_slots.wait()

    def place(to):
        o = snake(to)
        tails = []
        for r in range(CAP):
            j = slots[0, CAP * o + r]
            jj = jnp.maximum(j, 0)
            here = jnp.where(j >= 0, 1.0, 0.0)
            tail = aux[jj] * here
            send[to, r * C : (r + 1) * C, :] = (feats[jj].astype(F32) * tail[7:8]).astype(BF)
            tails.append(tail)
        send[to, CAP * C : CAP * C + 16, :] = jnp.concatenate(tails, axis=0).astype(BF)

    def points_copy(k):
        to = partner(mx, k, 1)
        return pltpu.make_async_remote_copy(
            src_ref=send.at[to], dst_ref=recv.at[mx],
            send_sem=s_send, recv_sem=s_recv.at[k // GROUP],
            device_id=(to, my), device_id_type=MESH,
        )

    pl.semaphore_wait(barrier, GX - 1 + GY - 1)

    @pl.loop(1, GX)
    def _(k):
        place(partner(mx, k, 1))
        points_copy(k).start()

    place(mx)
    recv[mx] = send[mx]

    for name in ("conv", "read"):
        fetched[name].wait()
    eye = jnp.where(
        lax.broadcasted_iota(jnp.int32, (C, C), 0) == lax.broadcasted_iota(jnp.int32, (C, C), 1),
        1.0, 0.0,
    )
    read_col = dot((eye * read[...].astype(F32)).astype(BF), jnp.ones((C, NZ), BF))

    sub_z = lax.broadcasted_iota(jnp.int32, (NZ, WIDE), 0).astype(F32)
    sub_y = lax.broadcasted_iota(jnp.int32, (CY, WIDE), 0).astype(F32)
    acc[...] = jnp.zeros(acc.shape, F32)

    @pl.loop(0, GROUPS)
    def _(g):
        blocks, tails = [], []

        @pl.when(g == 0)
        def _():
            whole(recv.at[0 : GROUP - 1], s_recv.at[0])

        @pl.when(g > 0)
        def _():
            whole(recv.at[0:GROUP], s_recv.at[g])

        for n in range(GROUP):
            msg = recv[partner(mx, GROUP * g + n, -1)]
            blocks += [msg[0:C], msg[C : 2 * C]]
            tail = msg[2 * C : 2 * C + 16].astype(F32)
            tails += [tail[0:8], tail[8:16]]
        block = jnp.concatenate(blocks, axis=1)
        tail = jnp.concatenate(tails, axis=1)
        near = jnp.exp(-2.0 * tail * tail)
        far = jnp.exp(-2.0 * (tail - 1.0) * (tail - 1.0))
        at_y, at_z = tail[3:4], tail[4:5]
        slope = tail[5:6] + tail[6:7]
        wy = jnp.where(sub_y == at_y, near[1:2], jnp.where(sub_y == at_y + 1.0, far[1:2], 0.0))
        plane = (near[0:1] * wy, far[0:1] * wy)
        planes[g, 0:CY, :] = plane[0]
        planes[g, CY : 2 * CY, :] = plane[1]
        z = jnp.where(sub_z == at_z, near[2:3], jnp.where(sub_z == at_z + 1.0, far[2:3], 0.0))
        z = z.astype(BF)
        zs[g] = z
        lifted = block.astype(F32)
        rows = [
            (lifted * plane[x][y : y + 1]).astype(BF) for y in range(CY) for x in range(CX)
        ]
        rows.append(jnp.concatenate([plane[0] * slope, plane[1] * slope], axis=0).astype(BF))
        acc[...] += dot(jnp.concatenate(rows, axis=0), z, 1, 1)

    def halo_copies(buf, sends, recvs):
        ends = (
            (right, up, buf.at[8, 2], buf.at[0, 0]),
            (right, down, buf.at[1, 2], buf.at[9, 0]),
            (left, up, buf.at[8, 1], buf.at[0, 3]),
            (left, down, buf.at[1, 1], buf.at[9, 3]),
            (mx, up, buf.at[8, 1:3], buf.at[0, 1:3]),
            (mx, down, buf.at[1, 1:3], buf.at[9, 1:3]),
            (right, my, buf.at[1:9, 2], buf.at[1:9, 0]),
            (left, my, buf.at[1:9, 1], buf.at[1:9, 3]),
        )
        return [
            pltpu.make_async_remote_copy(
                src_ref=src, dst_ref=dst, send_sem=sends, recv_sem=recvs,
                device_id=(px, py), device_id_type=MESH,
            )
            for n, (px, py, src, dst) in enumerate(ends)
        ]

    def clear_ends(buf):
        @pl.when(slab == 0)
        def _():
            buf[:, 0] = jnp.zeros((10, C, NZ), BF)

        @pl.when(slab == GX - 1)
        def _():
            buf[:, 3] = jnp.zeros((10, C, NZ), BF)

        @pl.when(my == 0)
        def _():
            buf[0] = jnp.zeros((4, C, NZ), BF)

        @pl.when(my == GY - 1)
        def _():
            buf[9] = jnp.zeros((4, C, NZ), BF)

    for y in range(CY):
        for x in range(CX):
            row = (y * CX + x) * C
            latp[y + 1, x + 1] = acc[row : row + C, :].astype(BF)
    halos = halo_copies(latp, h_send, h_recv)
    for copy in halos:
        copy.start()

    def place_tap(xp):
        lanes = lax.broadcasted_iota(jnp.int32, (C, 128), 1)
        rows = lax.broadcasted_iota(jnp.int32, (C, 128), 0)
        return jnp.where(lanes == rows + C * xp, 1.0, 0.0).astype(BF)

    spots = [place_tap(xp) for xp in range(4)]
    wf[...] = jnp.zeros(wf.shape, BF)
    wb[...] = jnp.zeros(wb.shape, BF)
    for dz in range(3):
        for dy in range(3):
            for xo in range(2):
                tile_f = sum(
                    dot(conv[9 * dx + 3 * dy + dz], spots[dx + xo], 0, 0) for dx in range(3)
                ).astype(BF)
                tile_b = sum(
                    dot(conv[9 * (2 - dx) + 3 * (2 - dy) + (2 - dz)], spots[dx + xo])
                    for dx in range(3)
                ).astype(BF)
                for yo in range(2):
                    row = ((dz * 2 + yo) * 2 + xo) * C
                    lane = (yo + dy) * 128
                    wf[row : row + C, lane : lane + 128] = tile_f
                    wb[row : row + C, lane : lane + 128] = tile_b
    whole(latp.at[0:6], h_recv)
    clear_ends(latp)

    for pair in range(4):
        pre = conv_pair(wf, latp, pair)
        cube = pre * pre
        th = jnp.tanh(0.7978845608028654 * pre * (1.0 + 0.044715 * cube))
        half = 0.5 * (1.0 + th)
        slope = half + 0.5 * pre * (1.0 - th * th) * (
            0.7978845608028654 * (1.0 + 3.0 * 0.044715 * cube)
        )
        own = latp[2 * pair + 1 : 2 * pair + 3, 1:3].reshape(4 * C, NZ).astype(F32)
        out = (own + pre * half).astype(BF).astype(F32)
        grads = []
        for yo in range(2):
            for x in range(CX):
                row = x * CY + 2 * pair + yo
                n = (yo * CX + x) * C
                field[row : row + 1, :] = jnp.sum(
                    out[n : n + C] * read_col, axis=0, keepdims=True
                )
                grads.append(read_col * acc[COLS * C + row : COLS * C + row + 1, :])
        grad_out = jnp.concatenate(grads, axis=0)
        gout[128 * pair : 128 * pair + 128, :] = grad_out
        grad_pre = (grad_out * slope).astype(BF)
        gp[2 * pair + 1 : 2 * pair + 3, 1:3] = grad_pre.reshape(2, 2, C, NZ)
        wide = grad_pre.astype(F32)
        gs[pair, 0:128, :] = shifted(wide, -1).astype(BF)
        gs[pair, 128:256, :] = grad_pre
        gs[pair, 256:384, :] = shifted(wide, 1).astype(BF)
    halos2 = halo_copies(gp, i_send, i_recv)
    for copy in halos2:
        copy.start()

    windows = [latp[2 * pair : 2 * pair + 4].reshape(4 * 4 * C, NZ) for pair in range(4)]
    tap = dot(
        jnp.concatenate(windows, axis=1),
        jnp.concatenate([gs[pair] for pair in range(4)], axis=1), 1, 1,
    )
    quarter = lax.broadcasted_iota(jnp.int32, (C, 128), 1) // C
    quarter8 = lax.broadcasted_iota(jnp.int32, (8, 128), 1) // C
    for dx in range(3):
        for dy in range(3):
            for dz in range(3):
                total = jnp.zeros((C, 128), F32)
                for yo in range(2):
                    for xo in range(2):
                        n = ((yo + dy) * 4 + xo + dx) * C
                        piece = tap[n : n + C, dz * 128 : dz * 128 + 128]
                        total = jnp.where(quarter == 2 * yo + xo, piece, total)
                total = total + pltpu.roll(total, 64, 1)
                total = total + pltpu.roll(total, 32, 1)
                packed = total[0:8]
                for q in range(1, 4):
                    packed = jnp.where(quarter8 == q, total[8 * q : 8 * q + 8], packed)
                redsrc[9 * dx + 3 * dy + dz] = packed
    redsrc[TAPS:GX] = jnp.zeros((GX - TAPS, 8, 128), F32)

    def taps_copy(k):
        to = partner(mx, k, 1)
        return pltpu.make_async_remote_copy(
            src_ref=redsrc.at[to], dst_ref=red1.at[mx],
            send_sem=a_send, recv_sem=a_recv,
            device_id=(to, my), device_id_type=MESH,
        )

    @pl.loop(1, GX)
    def _(k):
        taps_copy(k).start()

    scalar = field[...]
    scalar_hi = scalar.astype(BF)
    scalar_lo = (scalar - scalar_hi.astype(F32)).astype(BF)
    scalars = jnp.concatenate([scalar_hi, scalar_lo], axis=0)

    def pred_copy(k):
        to = partner(mx, k, -1)
        return pltpu.make_async_remote_copy(
            src_ref=predmsg.at[k, 0:CAP], dst_ref=predr.at[slab, 0:CAP],
            send_sem=p_send, recv_sem=p_recv,
            device_id=(to, my), device_id_type=MESH,
        )

    @pl.loop(0, GROUPS)
    def _(g):
        got = dot(scalars, zs[g])
        total = jnp.sum((got[0:COLS] + got[COLS:]) * planes[g], axis=0, keepdims=True)
        for n in range(GROUP):
            k = GROUP * g + n
            for r in range(CAP):
                lane = n * PTS + r * BLK
                predmsg[k, r : r + 1, :] = total[:, lane : lane + BLK]
            if n == 0:

                @pl.when(g > 0)
                def _():
                    pred_copy(GROUP * g).start()

            else:
                pred_copy(k).start()

    predr[slab, 0:CAP, :] = predmsg[0, 0:CAP, :]

    whole(gp.at[0:6], i_recv)
    clear_ends(gp)
    for pair in range(4):
        back = conv_pair(wb, gp, pair)
        gl[128 * pair : 128 * pair + 128, :] = (
            gout[128 * pair : 128 * pair + 128, :] + back
        ).astype(BF)

    def feats_copy(k):
        to = partner(mx, k, -1)
        return pltpu.make_async_remote_copy(
            src_ref=gfs.at[k], dst_ref=gfr.at[pl.ds(CAP * slab, CAP)],
            send_sem=f_send, recv_sem=f_recv,
            device_id=(to, my), device_id_type=MESH,
        )

    def rows_copy(k):
        return pltpu.make_async_remote_copy(
            src_ref=red2.at[my], dst_ref=red2.at[my],
            send_sem=b_send, recv_sem=b_recv,
            device_id=(mx, lax.rem(my + k, GY)), device_id_type=MESH,
        )

    def collect(g):
        got = dot(gl[...], zs[g])
        total = jnp.zeros((C, WIDE), F32)
        for y in range(CY):
            for x in range(CX):
                n = (y * CX + x) * C
                total = total + got[n : n + C] * planes[g, x * CY + y : x * CY + y + 1, :]
        return total.astype(BF)

    def finish(g, total):
        back = dot(lift_w, total).astype(BF)
        for n in range(GROUP):
            for r in range(CAP):
                lane = n * PTS + r * BLK
                gfs[GROUP * g + n, r] = back[:, lane : lane + BLK]

    def send_back(g):
        for n in range(GROUP):
            feats_copy(GROUP * g + n).start()

    def step(g):
        before = held[...]
        total = collect(g)
        finish(g - 1, before)
        held[...] = total
        send_back(g - 1)

    held[...] = collect(1)

    @pl.loop(2, 5)
    def _(g):
        step(g)

    red1[mx] = redsrc[mx]

    whole(red1.at[0 : GX - 1], a_recv)
    red2[my] = jnp.sum(red1[...], axis=0)
    for k in range(1, GY):
        rows_copy(k).start()

    @pl.loop(5, GROUPS)
    def _(g):
        step(g)

    before = held[...]
    total = collect(0)
    finish(GROUPS - 1, before)
    send_back(GROUPS - 1)
    finish(0, total)
    for n in range(1, GROUP):
        feats_copy(n).start()
    gfr[pl.ds(CAP * slab, CAP)] = gfs[0]

    whole(red2.at[0 : GY - 1], b_recv)
    red3[mx] = (red2[0] + red2[1] + red2[2] + red2[3]) * (1.0 / GX)

    def total_copy(k):
        to = partner(mx, k, 1)
        return pltpu.make_async_remote_copy(
            src_ref=red3.at[mx], dst_ref=red3.at[mx],
            send_sem=c_send, recv_sem=c_recv,
            device_id=(to, my), device_id_type=MESH,
        )

    @pl.loop(1, GX)
    def _(k):
        total_copy(k).start()

    whole(predr.at[0 : GX - 1, 0:CAP], p_recv)
    whole(gfr.at[0 : CAP * (GX - 1)], f_recv)

    @pl.loop(0, NB)
    def _(j):
        s = slots[1, j]
        keep = aux[j, 7:8, :]
        feats_out[j] = (gfr[s].astype(F32) * keep).astype(BF)
        both = predr[s // CAP]
        value = jnp.where(lax.rem(s, CAP) == 0, both[0:1], both[1:2])
        pred_out[pl.ds(j, 1), :] = value * keep

    whole(red3.at[0 : GX - 1], c_recv)
    for d in range(TAPS):
        packed = red3[d]
        for q in range(4):
            piece = packed if q == 0 else pltpu.roll(packed, 128 - C * q, 1)
            conv_out[d, 8 * q : 8 * q + 8, :] = piece[:, 0:C]

    whole(predr.at[0 : GX - 1, 0:CAP], p_send)
    whole(gfr.at[0 : CAP * (GX - 1)], f_send)
    for sem in (c_send, a_send):
        whole(red3.at[0 : GX - 1], sem)
    whole(red2.at[0 : GY - 1], b_send)
    whole(latp.at[0:6], h_send)
    whole(gp.at[0:6], i_send)
    whole(recv.at[0 : GX - 1], s_send)


def finish_kernel(pred, feats, conv, pred_out, feats_out, conv_out, sems):
    copies = [
        pltpu.make_async_copy(src, dst, sems.at[n])
        for n, (src, dst) in enumerate(((conv, conv_out), (feats, feats_out), (pred, pred_out)))
    ]
    for copy in copies:
        copy.start()
    for copy in copies:
        copy.wait()


def local(
    point_feats, point_offsets, base_cells, block_owners, point_counts,
    lift_weight, conv_weight, read_weight, cotangent,
):
    hbm = pl.BlockSpec(memory_space=pltpu.HBM)
    vmem = pl.BlockSpec(memory_space=pltpu.VMEM)
    dma = pltpu.SemaphoreType.DMA
    inputs = (
        point_feats, jnp.transpose(point_offsets, (1, 0, 2)), base_cells,
        block_owners.reshape(1, NB), point_counts.reshape(1, 1), lift_weight, conv_weight,
        read_weight.reshape(1, C), cotangent,
    )
    parts = pl.pallas_call(
        kernel,
        out_shape=(
            pltpu.VMEM((NB, BLK), F32),
            pltpu.VMEM((NB, C, BLK), BF),
            pltpu.VMEM((TAPS, C, C), F32),
        ),
        in_specs=[hbm] * 9,
        out_specs=(vmem,) * 3,
        scratch_shapes=[
            pltpu.VMEM((NB, C, BLK), BF),
            pltpu.VMEM((3, NB, BLK), BF),
            pltpu.VMEM((NB, BLK), jnp.int32),
            pltpu.VMEM((1, NB), jnp.int32),
            pltpu.VMEM((1, 1), jnp.int32),
            pltpu.VMEM((C, C), BF),
            pltpu.VMEM((TAPS, C, C), BF),
            pltpu.VMEM((1, C), BF),
            pltpu.VMEM((NB, BLK), F32),
            pltpu.VMEM((8, BLK), jnp.int32),
            pltpu.SMEM((8, BLK), jnp.int32),
            pltpu.VMEM((NB, 8, BLK), F32),
            pltpu.VMEM((GX * CAP, C, BLK), BF),
            pltpu.VMEM((GX, 8, BLK), F32),
            pltpu.VMEM((GX, 8, 128), F32),
            dma((10,)),
            pltpu.VMEM((GX, CAP * C + 16, BLK), BF),
            pltpu.VMEM((GX, CAP * C + 16, BLK), BF),
            pltpu.VMEM((COLS * C + COLS, NZ), F32),
            pltpu.VMEM((GROUPS, NZ, WIDE), BF),
            pltpu.VMEM((GROUPS, COLS, WIDE), F32),
            pltpu.VMEM((10, 4, C, NZ), BF),
            pltpu.VMEM((10, 4, C, NZ), BF),
            pltpu.VMEM((4, 3 * 128, NZ), BF),
            pltpu.VMEM((3 * 128, 512), BF),
            pltpu.VMEM((3 * 128, 512), BF),
            pltpu.VMEM((COLS * C, NZ), F32),
            pltpu.VMEM((COLS, NZ), F32),
            pltpu.VMEM((COLS * C, NZ), BF),
            pltpu.VMEM((GX, 8, BLK), F32),
            pltpu.VMEM((C, WIDE), BF),
            pltpu.VMEM((GX, CAP, C, BLK), BF),
            pltpu.VMEM((GX, 8, 128), F32),
            pltpu.VMEM((GX, 8, 128), F32),
            pltpu.VMEM((GY, 8, 128), F32),
            dma, dma((GROUPS,)), dma, dma, dma, dma, dma, dma, dma, dma, dma, dma, dma, dma, dma, dma,
        ],
        compiler_params=pltpu.CompilerParams(
            collective_id=0, has_side_effects=True, vmem_limit_bytes=40 * 1024 * 1024
        ),
        cost_estimate=pl.CostEstimate(
            flops=8_000_000_000, bytes_accessed=2_000_000, transcendentals=1_000_000
        ),
    )(*(x if x.size == 1 else pltpu.with_memory_space_constraint(x, pltpu.HBM) for x in inputs))
    return pl.pallas_call(
        finish_kernel,
        out_shape=(
            jax.ShapeDtypeStruct((NB, BLK), F32),
            jax.ShapeDtypeStruct((NB, C, BLK), BF),
            jax.ShapeDtypeStruct((TAPS, C, C), F32),
        ),
        in_specs=[vmem] * 3,
        out_specs=(hbm,) * 3,
        scratch_shapes=[dma((3,))],
        compiler_params=pltpu.CompilerParams(vmem_limit_bytes=8 * 1024 * 1024),
    )(*(pltpu.with_memory_space_constraint(x, pltpu.VMEM) for x in parts))


def solution(mesh):
    in_specs = (
        P(("gx", "gy"), None, None),
        P(("gx", "gy"), None, None),
        P(("gx", "gy"), None),
        P(("gx", "gy"), None),
        P(("gx", "gy")),
        P(),
        P(),
        P(),
        P(("gx", "gy"), None),
    )
    out_specs = (P(("gx", "gy"), None), P(("gx", "gy"), None, None), P())
    return jax.shard_map(local, mesh=mesh, in_specs=in_specs, out_specs=out_specs, check_vma=False)
```

```python
import functools

import jax
import jax.numpy as jnp
from jax import lax
from jax.experimental import pallas as pl
from jax.experimental.pallas import tpu as pltpu
from jax.sharding import PartitionSpec as P

C = 32
CX = 2
CY = 8
NZ = 256
NB = 32
BLK = 128
GX = 32
GY = 4
CAP = 2
PTS = CAP * BLK
GROUP = 4
GROUPS = GX // GROUP
WIDE = GROUP * PTS
COLS = CX * CY
TAPS = 27
MESH = pl.DeviceIdType.MESH
BF = jnp.bfloat16
F32 = jnp.float32


def partner(mx, n, sign):
    return lax.rem(mx + sign * lax.rem(13 * n, GX) + GX, GX)


def snake(index):
    x, z, core = index // 8, lax.rem(index // 2, 4), lax.rem(index, 2)
    return x * 8 + (z + lax.rem(x, 2) * (3 - 2 * z)) * 2 + core


def whole(ref, sem):
    pltpu.make_async_copy(ref, ref, sem).wait()


def dot(a, b, ca=1, cb=0):
    return lax.dot_general(a, b, (((ca,), (cb,)), ((), ())), preferred_element_type=F32)


def shifted(values, step):
    lanes = lax.broadcasted_iota(jnp.int32, values.shape, 1)
    if step == 1:
        return jnp.where(lanes == 0, 0.0, pltpu.roll(values, 1, 1))
    return jnp.where(lanes == NZ - 1, 0.0, pltpu.roll(values, NZ - 1, 1))


def conv_pair(weights, padded, pair):
    window = padded[2 * pair : 2 * pair + 4].reshape(4 * 4 * C, NZ)
    part = dot(weights[...], window)
    return shifted(part[0:128], 1) + part[128:256] + shifted(part[256:384], -1)


def kernel(
    feats_hbm, offsets_hbm, base_hbm, owners_hbm, count_hbm, lift_hbm, conv_hbm, read_hbm, cot_hbm,
    pred_out, feats_out, conv_out,
    feats, offsets, base, owners, count, lift, conv, read, cot, table, slots, aux, gfr, predr, red3, in_sem, send, recv, acc, zs, planes, latp, gp, gs, wf, wb,
    gout, field, gl, predmsg, held, gfs, redsrc, red1, red2,
    s_send, s_recv, h_send, h_recv, i_send, i_recv, p_send, p_recv,
    f_send, f_recv, a_send, a_recv, b_send, b_recv, c_send, c_recv,
):
    mx = lax.axis_index("gx")
    my = lax.axis_index("gy")
    slab = snake(mx)
    right, left = snake(lax.rem(slab + 1, GX)), snake(lax.rem(slab + GX - 1, GX))
    up, down = lax.rem(my + 1, GY), lax.rem(my + GY - 1, GY)

    pairs = {
        "owners": (owners_hbm, owners), "offsets": (offsets_hbm, offsets), "base": (base_hbm, base),
        "count": (count_hbm, count), "cot": (cot_hbm, cot), "feats": (feats_hbm, feats),
        "lift": (lift_hbm, lift), "conv": (conv_hbm, conv), "read": (read_hbm, read),
    }
    fetched = {
        name: pltpu.make_async_copy(src, dst, in_sem.at[n])
        for n, (name, (src, dst)) in enumerate(pairs.items())
    }
    for copy in fetched.values():
        copy.start()

    barrier = pltpu.get_barrier_semaphore()

    @pl.loop(1, GX)
    def _(k):
        pl.semaphore_signal(barrier, inc=1, device_id=(lax.rem(mx + k, GX), my), device_id_type=MESH)

    for k in range(1, GY):
        pl.semaphore_signal(barrier, inc=1, device_id=(mx, lax.rem(my + k, GY)), device_id_type=MESH)

    fetched["owners"].wait()
    named = owners[...]
    rows32 = lax.broadcasted_iota(jnp.int32, (NB, NB), 0)
    lanes32 = lax.broadcasted_iota(jnp.int32, (NB, NB), 1)
    named_col = jnp.sum(jnp.where(rows32 == lanes32, named, 0), axis=1, keepdims=True)
    earlier = (named_col == named) & (rows32 < lanes32)
    slot_row = CAP * named + jnp.sum(jnp.where(earlier, 1, 0), axis=0, keepdims=True)
    slot_col = jnp.sum(jnp.where(rows32 == lanes32, slot_row, 0), axis=1, keepdims=True)
    rows = lax.broadcasted_iota(jnp.int32, (NB, BLK), 0)
    lanes = lax.broadcasted_iota(jnp.int32, (NB, BLK), 1)
    table[0:1, :] = jnp.sum(jnp.where(slot_col == lanes, rows + 1, 0), axis=0, keepdims=True) - 1
    table[1:2, :] = jnp.sum(jnp.where(rows == lanes, slot_col, 0), axis=0, keepdims=True)
    table[2:8, :] = jnp.zeros((6, BLK), jnp.int32)
    to_slots = pltpu.make_async_copy(table, slots, in_sem.at[9])
    to_slots.start()

    for name in ("offsets", "base", "count", "cot"):
        fetched[name].wait()
    cells = base[...].astype(F32)
    cell_y = jnp.floor((cells + 0.5) * (1.0 / (NZ - 1)))
    alive = jnp.where(rows * BLK + lanes < count[...], 1.0, 0.0)
    grad = cot[...] * alive
    high = grad.astype(BF).astype(F32)
    tile_rows = [offsets[n].astype(F32) for n in range(3)]
    tile_rows += [cell_y, cells - cell_y * (NZ - 1.0), high, grad - high, alive]
    for n, value in enumerate(tile_rows):
        aux[:, n, :] = value
    for name in ("lift", "feats"):
        fetched[name].wait()
    lift_w = lift[...]
    for part in range(4):
        raw = jnp.concatenate([feats[8 * part + n] for n in range(8)], axis=1)
        lifted = dot(lift_w, raw, 0, 0).astype(BF)
        for n in range(8):
            feats[8 * part + n] = lifted[:, n * BLK : (n + 1) * BLK]
    to_slots.wait()

    def place(to):
        o = snake(to)
        tails = []
        for r in range(CAP):
            j = slots[0, CAP * o + r]
            jj = jnp.maximum(j, 0)
            here = jnp.where(j >= 0, 1.0, 0.0)
            tail = aux[jj] * here
            send[to, r * C : (r + 1) * C, :] = (feats[jj].astype(F32) * tail[7:8]).astype(BF)
            tails.append(tail)
        send[to, CAP * C : CAP * C + 16, :] = jnp.concatenate(tails, axis=0).astype(BF)

    def points_copy(k):
        to = partner(mx, k, 1)
        return pltpu.make_async_remote_copy(
            src_ref=send.at[to], dst_ref=recv.at[mx],
            send_sem=s_send, recv_sem=s_recv.at[k // GROUP],
            device_id=(to, my), device_id_type=MESH,
        )

    pl.semaphore_wait(barrier, GX - 1 + GY - 1)

    @pl.loop(1, GX)
    def _(k):
        place(partner(mx, k, 1))
        points_copy(k).start()

    place(mx)
    recv[mx] = send[mx]

    for name in ("conv", "read"):
        fetched[name].wait()
    eye = jnp.where(
        lax.broadcasted_iota(jnp.int32, (C, C), 0) == lax.broadcasted_iota(jnp.int32, (C, C), 1),
        1.0, 0.0,
    )
    read_col = dot((eye * read[...].astype(F32)).astype(BF), jnp.ones((C, NZ), BF))

    sub_z = lax.broadcasted_iota(jnp.int32, (NZ, WIDE), 0).astype(F32)
    sub_y = lax.broadcasted_iota(jnp.int32, (CY, WIDE), 0).astype(F32)
    acc[...] = jnp.zeros(acc.shape, F32)

    @pl.loop(0, GROUPS)
    def _(g):
        blocks, tails = [], []

        @pl.when(g == 0)
        def _():
            whole(recv.at[0 : GROUP - 1], s_recv.at[0])

        @pl.when(g > 0)
        def _():
            whole(recv.at[0:GROUP], s_recv.at[g])

        for n in range(GROUP):
            msg = recv[partner(mx, GROUP * g + n, -1)]
            blocks += [msg[0:C], msg[C : 2 * C]]
            tail = msg[2 * C : 2 * C + 16].astype(F32)
            tails += [tail[0:8], tail[8:16]]
        block = jnp.concatenate(blocks, axis=1)
        tail = jnp.concatenate(tails, axis=1)
        near = jnp.exp(-2.0 * tail * tail)
        far = jnp.exp(-2.0 * (tail - 1.0) * (tail - 1.0))
        at_y, at_z = tail[3:4], tail[4:5]
        slope = tail[5:6] + tail[6:7]
        wy = jnp.where(sub_y == at_y, near[1:2], jnp.where(sub_y == at_y + 1.0, far[1:2], 0.0))
        plane = (near[0:1] * wy, far[0:1] * wy)
        planes[g, 0:CY, :] = plane[0]
        planes[g, CY : 2 * CY, :] = plane[1]
        z = jnp.where(sub_z == at_z, near[2:3], jnp.where(sub_z == at_z + 1.0, far[2:3], 0.0))
        z = z.astype(BF)
        zs[g] = z
        lifted = block.astype(F32)
        rows = [
            (lifted * plane[x][y : y + 1]).astype(BF) for y in range(CY) for x in range(CX)
        ]
        rows.append(jnp.concatenate([plane[0] * slope, plane[1] * slope], axis=0).astype(BF))
        acc[...] += dot(jnp.concatenate(rows, axis=0), z, 1, 1)

    def halo_copies(buf, sends, recvs):
        ends = (
            (right, up, buf.at[8, 2], buf.at[0, 0]),
            (right, down, buf.at[1, 2], buf.at[9, 0]),
            (left, up, buf.at[8, 1], buf.at[0, 3]),
            (left, down, buf.at[1, 1], buf.at[9, 3]),
            (mx, up, buf.at[8, 1:3], buf.at[0, 1:3]),
            (mx, down, buf.at[1, 1:3], buf.at[9, 1:3]),
            (right, my, buf.at[1:9, 2], buf.at[1:9, 0]),
            (left, my, buf.at[1:9, 1], buf.at[1:9, 3]),
        )
        return [
            pltpu.make_async_remote_copy(
                src_ref=src, dst_ref=dst, send_sem=sends, recv_sem=recvs,
                device_id=(px, py), device_id_type=MESH,
            )
            for n, (px, py, src, dst) in enumerate(ends)
        ]

    def clear_ends(buf):
        @pl.when(slab == 0)
        def _():
            buf[:, 0] = jnp.zeros((10, C, NZ), BF)

        @pl.when(slab == GX - 1)
        def _():
            buf[:, 3] = jnp.zeros((10, C, NZ), BF)

        @pl.when(my == 0)
        def _():
            buf[0] = jnp.zeros((4, C, NZ), BF)

        @pl.when(my == GY - 1)
        def _():
            buf[9] = jnp.zeros((4, C, NZ), BF)

    for y in range(CY):
        for x in range(CX):
            row = (y * CX + x) * C
            latp[y + 1, x + 1] = acc[row : row + C, :].astype(BF)
    halos = halo_copies(latp, h_send, h_recv)
    for copy in halos:
        copy.start()

    def place_tap(xp):
        lanes = lax.broadcasted_iota(jnp.int32, (C, 128), 1)
        rows = lax.broadcasted_iota(jnp.int32, (C, 128), 0)
        return jnp.where(lanes == rows + C * xp, 1.0, 0.0).astype(BF)

    spots = [place_tap(xp) for xp in range(4)]
    wf[...] = jnp.zeros(wf.shape, BF)
    wb[...] = jnp.zeros(wb.shape, BF)
    for dz in range(3):
        for dy in range(3):
            for xo in range(2):
                tile_f = sum(
                    dot(conv[9 * dx + 3 * dy + dz], spots[dx + xo], 0, 0) for dx in range(3)
                ).astype(BF)
                tile_b = sum(
                    dot(conv[9 * (2 - dx) + 3 * (2 - dy) + (2 - dz)], spots[dx + xo])
                    for dx in range(3)
                ).astype(BF)
                for yo in range(2):
                    row = ((dz * 2 + yo) * 2 + xo) * C
                    lane = (yo + dy) * 128
                    wf[row : row + C, lane : lane + 128] = tile_f
                    wb[row : row + C, lane : lane + 128] = tile_b
    whole(latp.at[0:6], h_recv)
    clear_ends(latp)

    for pair in range(4):
        pre = conv_pair(wf, latp, pair)
        cube = pre * pre
        th = jnp.tanh(0.7978845608028654 * pre * (1.0 + 0.044715 * cube))
        half = 0.5 * (1.0 + th)
        slope = half + 0.5 * pre * (1.0 - th * th) * (
            0.7978845608028654 * (1.0 + 3.0 * 0.044715 * cube)
        )
        own = latp[2 * pair + 1 : 2 * pair + 3, 1:3].reshape(4 * C, NZ).astype(F32)
        out = (own + pre * half).astype(BF).astype(F32)
        grads = []
        for yo in range(2):
            for x in range(CX):
                row = x * CY + 2 * pair + yo
                n = (yo * CX + x) * C
                field[row : row + 1, :] = jnp.sum(
                    out[n : n + C] * read_col, axis=0, keepdims=True
                )
                grads.append(read_col * acc[COLS * C + row : COLS * C + row + 1, :])
        grad_out = jnp.concatenate(grads, axis=0)
        gout[128 * pair : 128 * pair + 128, :] = grad_out
        grad_pre = (grad_out * slope).astype(BF)
        gp[2 * pair + 1 : 2 * pair + 3, 1:3] = grad_pre.reshape(2, 2, C, NZ)
        wide = grad_pre.astype(F32)
        gs[pair, 0:128, :] = shifted(wide, -1).astype(BF)
        gs[pair, 128:256, :] = grad_pre
        gs[pair, 256:384, :] = shifted(wide, 1).astype(BF)
    halos2 = halo_copies(gp, i_send, i_recv)
    for copy in halos2:
        copy.start()

    windows = [latp[2 * pair : 2 * pair + 4].reshape(4 * 4 * C, NZ) for pair in range(4)]
    tap = dot(
        jnp.concatenate(windows, axis=1),
        jnp.concatenate([gs[pair] for pair in range(4)], axis=1), 1, 1,
    )
    quarter = lax.broadcasted_iota(jnp.int32, (C, 128), 1) // C
    quarter8 = lax.broadcasted_iota(jnp.int32, (8, 128), 1) // C
    for dx in range(3):
        for dy in range(3):
            for dz in range(3):
                total = jnp.zeros((C, 128), F32)
                for yo in range(2):
                    for xo in range(2):
                        n = ((yo + dy) * 4 + xo + dx) * C
                        piece = tap[n : n + C, dz * 128 : dz * 128 + 128]
                        total = jnp.where(quarter == 2 * yo + xo, piece, total)
                total = total + pltpu.roll(total, 64, 1)
                total = total + pltpu.roll(total, 32, 1)
                packed = total[0:8]
                for q in range(1, 4):
                    packed = jnp.where(quarter8 == q, total[8 * q : 8 * q + 8], packed)
                redsrc[9 * dx + 3 * dy + dz] = packed
    redsrc[TAPS:GX] = jnp.zeros((GX - TAPS, 8, 128), F32)

    def taps_copy(k):
        to = partner(mx, k, 1)
        return pltpu.make_async_remote_copy(
            src_ref=redsrc.at[to], dst_ref=red1.at[mx],
            send_sem=a_send, recv_sem=a_recv,
            device_id=(to, my), device_id_type=MESH,
        )

    @pl.loop(1, GX)
    def _(k):
        taps_copy(k).start()

    scalar = field[...]
    scalar_hi = scalar.astype(BF)
    scalar_lo = (scalar - scalar_hi.astype(F32)).astype(BF)
    scalars = jnp.concatenate([scalar_hi, scalar_lo], axis=0)

    def pred_copy(k):
        to = partner(mx, k, -1)
        return pltpu.make_async_remote_copy(
            src_ref=predmsg.at[k, 0:CAP], dst_ref=predr.at[slab, 0:CAP],
            send_sem=p_send, recv_sem=p_recv,
            device_id=(to, my), device_id_type=MESH,
        )

    @pl.loop(0, GROUPS)
    def _(g):
        got = dot(scalars, zs[g])
        total = jnp.sum((got[0:COLS] + got[COLS:]) * planes[g], axis=0, keepdims=True)
        for n in range(GROUP):
            k = GROUP * g + n
            for r in range(CAP):
                lane = n * PTS + r * BLK
                predmsg[k, r : r + 1, :] = total[:, lane : lane + BLK]
            if n == 0:

                @pl.when(g > 0)
                def _():
                    pred_copy(GROUP * g).start()

            else:
                pred_copy(k).start()

    predr[slab, 0:CAP, :] = predmsg[0, 0:CAP, :]

    whole(gp.at[0:6], i_recv)
    clear_ends(gp)
    for pair in range(4):
        back = conv_pair(wb, gp, pair)
        gl[128 * pair : 128 * pair + 128, :] = (
            gout[128 * pair : 128 * pair + 128, :] + back
        ).astype(BF)

    def feats_copy(k):
        to = partner(mx, k, -1)
        return pltpu.make_async_remote_copy(
            src_ref=gfs.at[k], dst_ref=gfr.at[pl.ds(CAP * slab, CAP)],
            send_sem=f_send, recv_sem=f_recv,
            device_id=(to, my), device_id_type=MESH,
        )

    def rows_copy(k):
        return pltpu.make_async_remote_copy(
            src_ref=red2.at[my], dst_ref=red2.at[my],
            send_sem=b_send, recv_sem=b_recv,
            device_id=(mx, lax.rem(my + k, GY)), device_id_type=MESH,
        )

    def collect(g):
        got = dot(gl[...], zs[g])
        total = jnp.zeros((C, WIDE), F32)
        for y in range(CY):
            for x in range(CX):
                n = (y * CX + x) * C
                total = total + got[n : n + C] * planes[g, x * CY + y : x * CY + y + 1, :]
        return total.astype(BF)

    def finish(g, total):
        back = dot(lift_w, total).astype(BF)
        for n in range(GROUP):
            for r in range(CAP):
                lane = n * PTS + r * BLK
                gfs[GROUP * g + n, r] = back[:, lane : lane + BLK]

    def first_half(h):
        span = slice(h * WIDE // 2, (h + 1) * WIDE // 2)
        got = dot(gl[...], zs[1, :, span])
        total = jnp.zeros((C, WIDE // 2), F32)
        for y in range(CY):
            for x in range(CX):
                n = (y * CX + x) * C
                total = total + got[n : n + C] * planes[1, x * CY + y : x * CY + y + 1, span]
        back = dot(lift_w, total.astype(BF)).astype(BF)
        for n in range(GROUP // 2):
            k = GROUP + h * GROUP // 2 + n
            for r in range(CAP):
                lane = n * PTS + r * BLK
                gfs[k, r] = back[:, lane : lane + BLK]
            feats_copy(k).start()

    def send_back(g):
        for n in range(GROUP):
            feats_copy(GROUP * g + n).start()

    def step(g):
        before = held[...]
        total = collect(g)
        finish(g - 1, before)
        held[...] = total
        send_back(g - 1)

    first_half(0)
    first_half(1)
    held[...] = collect(2)

    @pl.loop(3, 5)
    def _(g):
        step(g)

    red1[mx] = redsrc[mx]

    whole(red1.at[0 : GX - 1], a_recv)
    red2[my] = jnp.sum(red1[...], axis=0)
    for k in range(1, GY):
        rows_copy(k).start()

    @pl.loop(5, GROUPS)
    def _(g):
        step(g)

    before = held[...]
    total = collect(0)
    finish(GROUPS - 1, before)
    send_back(GROUPS - 1)
    finish(0, total)
    for n in range(1, GROUP):
        feats_copy(n).start()
    gfr[pl.ds(CAP * slab, CAP)] = gfs[0]

    whole(red2.at[0 : GY - 1], b_recv)
    red3[mx] = (red2[0] + red2[1] + red2[2] + red2[3]) * (1.0 / GX)

    def total_copy(k):
        to = partner(mx, k, 1)
        return pltpu.make_async_remote_copy(
            src_ref=red3.at[mx], dst_ref=red3.at[mx],
            send_sem=c_send, recv_sem=c_recv,
            device_id=(to, my), device_id_type=MESH,
        )

    @pl.loop(1, GX)
    def _(k):
        total_copy(k).start()

    whole(predr.at[0 : GX - 1, 0:CAP], p_recv)
    whole(gfr.at[0 : CAP * (GX - 1)], f_recv)

    @pl.loop(0, NB)
    def _(j):
        s = slots[1, j]
        keep = aux[j, 7:8, :]
        feats_out[j] = (gfr[s].astype(F32) * keep).astype(BF)
        both = predr[s // CAP]
        value = jnp.where(lax.rem(s, CAP) == 0, both[0:1], both[1:2])
        pred_out[pl.ds(j, 1), :] = value * keep

    whole(red3.at[0 : GX - 1], c_recv)
    for d in range(TAPS):
        packed = red3[d]
        for q in range(4):
            piece = packed if q == 0 else pltpu.roll(packed, 128 - C * q, 1)
            conv_out[d, 8 * q : 8 * q + 8, :] = piece[:, 0:C]

    whole(predr.at[0 : GX - 1, 0:CAP], p_send)
    whole(gfr.at[0 : CAP * (GX - 1)], f_send)
    for sem in (c_send, a_send):
        whole(red3.at[0 : GX - 1], sem)
    whole(red2.at[0 : GY - 1], b_send)
    whole(latp.at[0:6], h_send)
    whole(gp.at[0:6], i_send)
    whole(recv.at[0 : GX - 1], s_send)


def finish_kernel(pred, feats, conv, pred_out, feats_out, conv_out, sems):
    copies = [
        pltpu.make_async_copy(src, dst, sems.at[n])
        for n, (src, dst) in enumerate(((conv, conv_out), (feats, feats_out), (pred, pred_out)))
    ]
    for copy in copies:
        copy.start()
    for copy in copies:
        copy.wait()


def local(
    point_feats, point_offsets, base_cells, block_owners, point_counts,
    lift_weight, conv_weight, read_weight, cotangent,
):
    hbm = pl.BlockSpec(memory_space=pltpu.HBM)
    vmem = pl.BlockSpec(memory_space=pltpu.VMEM)
    dma = pltpu.SemaphoreType.DMA
    inputs = (
        point_feats, jnp.transpose(point_offsets, (1, 0, 2)), base_cells,
        block_owners.reshape(1, NB), point_counts.reshape(1, 1), lift_weight, conv_weight,
        read_weight.reshape(1, C), cotangent,
    )
    parts = pl.pallas_call(
        kernel,
        out_shape=(
            pltpu.VMEM((NB, BLK), F32),
            pltpu.VMEM((NB, C, BLK), BF),
            pltpu.VMEM((TAPS, C, C), F32),
        ),
        in_specs=[hbm] * 9,
        out_specs=(vmem,) * 3,
        scratch_shapes=[
            pltpu.VMEM((NB, C, BLK), BF),
            pltpu.VMEM((3, NB, BLK), BF),
            pltpu.VMEM((NB, BLK), jnp.int32),
            pltpu.VMEM((1, NB), jnp.int32),
            pltpu.VMEM((1, 1), jnp.int32),
            pltpu.VMEM((C, C), BF),
            pltpu.VMEM((TAPS, C, C), BF),
            pltpu.VMEM((1, C), BF),
            pltpu.VMEM((NB, BLK), F32),
            pltpu.VMEM((8, BLK), jnp.int32),
            pltpu.SMEM((8, BLK), jnp.int32),
            pltpu.VMEM((NB, 8, BLK), F32),
            pltpu.VMEM((GX * CAP, C, BLK), BF),
            pltpu.VMEM((GX, 8, BLK), F32),
            pltpu.VMEM((GX, 8, 128), F32),
            dma((10,)),
            pltpu.VMEM((GX, CAP * C + 16, BLK), BF),
            pltpu.VMEM((GX, CAP * C + 16, BLK), BF),
            pltpu.VMEM((COLS * C + COLS, NZ), F32),
            pltpu.VMEM((GROUPS, NZ, WIDE), BF),
            pltpu.VMEM((GROUPS, COLS, WIDE), F32),
            pltpu.VMEM((10, 4, C, NZ), BF),
            pltpu.VMEM((10, 4, C, NZ), BF),
            pltpu.VMEM((4, 3 * 128, NZ), BF),
            pltpu.VMEM((3 * 128, 512), BF),
            pltpu.VMEM((3 * 128, 512), BF),
            pltpu.VMEM((COLS * C, NZ), F32),
            pltpu.VMEM((COLS, NZ), F32),
            pltpu.VMEM((COLS * C, NZ), BF),
            pltpu.VMEM((GX, 8, BLK), F32),
            pltpu.VMEM((C, WIDE), BF),
            pltpu.VMEM((GX, CAP, C, BLK), BF),
            pltpu.VMEM((GX, 8, 128), F32),
            pltpu.VMEM((GX, 8, 128), F32),
            pltpu.VMEM((GY, 8, 128), F32),
            dma, dma((GROUPS,)), dma, dma, dma, dma, dma, dma, dma, dma, dma, dma, dma, dma, dma, dma,
        ],
        compiler_params=pltpu.CompilerParams(
            collective_id=0, has_side_effects=True, vmem_limit_bytes=40 * 1024 * 1024
        ),
        cost_estimate=pl.CostEstimate(
            flops=8_000_000_000, bytes_accessed=2_000_000, transcendentals=1_000_000
        ),
    )(*(x if x.size == 1 else pltpu.with_memory_space_constraint(x, pltpu.HBM) for x in inputs))
    return pl.pallas_call(
        finish_kernel,
        out_shape=(
            jax.ShapeDtypeStruct((NB, BLK), F32),
            jax.ShapeDtypeStruct((NB, C, BLK), BF),
            jax.ShapeDtypeStruct((TAPS, C, C), F32),
        ),
        in_specs=[vmem] * 3,
        out_specs=(hbm,) * 3,
        scratch_shapes=[dma((3,))],
        compiler_params=pltpu.CompilerParams(vmem_limit_bytes=8 * 1024 * 1024),
    )(*(pltpu.with_memory_space_constraint(x, pltpu.VMEM) for x in parts))


def solution(mesh):
    in_specs = (
        P(("gx", "gy"), None, None),
        P(("gx", "gy"), None, None),
        P(("gx", "gy"), None),
        P(("gx", "gy"), None),
        P(("gx", "gy")),
        P(),
        P(),
        P(),
        P(("gx", "gy"), None),
    )
    out_specs = (P(("gx", "gy"), None), P(("gx", "gy"), None, None), P())
    return jax.shard_map(local, mesh=mesh, in_specs=in_specs, out_specs=out_specs, check_vma=False)
```

```python
import functools

import jax
import jax.numpy as jnp
from jax import lax
from jax.experimental import pallas as pl
from jax.experimental.pallas import tpu as pltpu
from jax.sharding import PartitionSpec as P

C = 32
CX = 2
CY = 8
NZ = 256
NB = 32
BLK = 128
GX = 32
GY = 4
CAP = 2
PTS = CAP * BLK
GROUP = 4
GROUPS = GX // GROUP
WIDE = GROUP * PTS
COLS = CX * CY
TAPS = 27
MESH = pl.DeviceIdType.MESH
BF = jnp.bfloat16
F32 = jnp.float32


def partner(mx, n, sign):
    return lax.rem(mx + sign * lax.rem(13 * n, GX) + GX, GX)


def snake(index):
    x, z, core = index // 8, lax.rem(index // 2, 4), lax.rem(index, 2)
    return x * 8 + (z + lax.rem(x, 2) * (3 - 2 * z)) * 2 + core


def whole(ref, sem):
    pltpu.make_async_copy(ref, ref, sem).wait()


def dot(a, b, ca=1, cb=0):
    return lax.dot_general(a, b, (((ca,), (cb,)), ((), ())), preferred_element_type=F32)


def shifted(values, step):
    lanes = lax.broadcasted_iota(jnp.int32, values.shape, 1)
    if step == 1:
        return jnp.where(lanes == 0, 0.0, pltpu.roll(values, 1, 1))
    return jnp.where(lanes == NZ - 1, 0.0, pltpu.roll(values, NZ - 1, 1))


def conv_pair(weights, padded, pair):
    window = padded[2 * pair : 2 * pair + 4].reshape(4 * 4 * C, NZ)
    part = dot(weights[...], window)
    return shifted(part[0:128], 1) + part[128:256] + shifted(part[256:384], -1)


def kernel(
    feats_hbm, offsets_hbm, base_hbm, owners_hbm, count_hbm, lift_hbm, conv_hbm, read_hbm, cot_hbm,
    pred_out, feats_out, conv_out,
    feats, offsets, base, owners, count, lift, conv, read, cot, table, slots, aux, gfr, predr, red3, in_sem, send, recv, acc, zs, planes, latp, gp, gs, wf, wb,
    gout, field, gl, predmsg, held, gfs, redsrc, red1, red2,
    s_send, s_recv, h_send, h_recv, i_send, i_recv, p_send, p_recv,
    f_send, f_recv, a_send, a_recv, b_send, b_recv, c_send, c_recv,
):
    mx = lax.axis_index("gx")
    my = lax.axis_index("gy")
    slab = snake(mx)
    right, left = snake(lax.rem(slab + 1, GX)), snake(lax.rem(slab + GX - 1, GX))
    up, down = lax.rem(my + 1, GY), lax.rem(my + GY - 1, GY)

    pairs = {
        "owners": (owners_hbm, owners), "offsets": (offsets_hbm, offsets), "base": (base_hbm, base),
        "count": (count_hbm, count), "cot": (cot_hbm, cot), "feats": (feats_hbm, feats),
        "lift": (lift_hbm, lift), "conv": (conv_hbm, conv), "read": (read_hbm, read),
    }
    fetched = {
        name: pltpu.make_async_copy(src, dst, in_sem.at[n])
        for n, (name, (src, dst)) in enumerate(pairs.items())
    }
    for copy in fetched.values():
        copy.start()

    barrier = pltpu.get_barrier_semaphore()

    @pl.loop(1, GX)
    def _(k):
        pl.semaphore_signal(barrier, inc=1, device_id=(lax.rem(mx + k, GX), my), device_id_type=MESH)

    for k in range(1, GY):
        pl.semaphore_signal(barrier, inc=1, device_id=(mx, lax.rem(my + k, GY)), device_id_type=MESH)

    fetched["owners"].wait()
    named = owners[...]
    rows32 = lax.broadcasted_iota(jnp.int32, (NB, NB), 0)
    lanes32 = lax.broadcasted_iota(jnp.int32, (NB, NB), 1)
    named_col = jnp.sum(jnp.where(rows32 == lanes32, named, 0), axis=1, keepdims=True)
    earlier = (named_col == named) & (rows32 < lanes32)
    slot_row = CAP * named + jnp.sum(jnp.where(earlier, 1, 0), axis=0, keepdims=True)
    slot_col = jnp.sum(jnp.where(rows32 == lanes32, slot_row, 0), axis=1, keepdims=True)
    rows = lax.broadcasted_iota(jnp.int32, (NB, BLK), 0)
    lanes = lax.broadcasted_iota(jnp.int32, (NB, BLK), 1)
    table[0:1, :] = jnp.sum(jnp.where(slot_col == lanes, rows + 1, 0), axis=0, keepdims=True) - 1
    table[1:2, :] = jnp.sum(jnp.where(rows == lanes, slot_col, 0), axis=0, keepdims=True)
    table[2:8, :] = jnp.zeros((6, BLK), jnp.int32)
    to_slots = pltpu.make_async_copy(table, slots, in_sem.at[9])
    to_slots.start()

    for name in ("offsets", "base", "count", "cot"):
        fetched[name].wait()
    cells = base[...].astype(F32)
    cell_y = jnp.floor((cells + 0.5) * (1.0 / (NZ - 1)))
    alive = jnp.where(rows * BLK + lanes < count[...], 1.0, 0.0)
    grad = cot[...] * alive
    high = grad.astype(BF).astype(F32)
    tile_rows = [offsets[n].astype(F32) for n in range(3)]
    tile_rows += [cell_y, cells - cell_y * (NZ - 1.0), high, grad - high, alive]
    for n, value in enumerate(tile_rows):
        aux[:, n, :] = value
    for name in ("lift", "feats"):
        fetched[name].wait()
    lift_w = lift[...]
    for part in range(4):
        raw = jnp.concatenate([feats[8 * part + n] for n in range(8)], axis=1)
        lifted = dot(lift_w, raw, 0, 0).astype(BF)
        for n in range(8):
            feats[8 * part + n] = lifted[:, n * BLK : (n + 1) * BLK]
    to_slots.wait()

    def place(to):
        o = snake(to)
        tails = []
        for r in range(CAP):
            j = slots[0, CAP * o + r]
            jj = jnp.maximum(j, 0)
            here = jnp.where(j >= 0, 1.0, 0.0)
            tail = aux[jj] * here
            send[to, r * C : (r + 1) * C, :] = (feats[jj].astype(F32) * tail[7:8]).astype(BF)
            tails.append(tail)
        send[to, CAP * C : CAP * C + 16, :] = jnp.concatenate(tails, axis=0).astype(BF)

    def points_copy(k):
        to = partner(mx, k, 1)
        return pltpu.make_async_remote_copy(
            src_ref=send.at[to], dst_ref=recv.at[mx],
            send_sem=s_send, recv_sem=s_recv.at[k // GROUP],
            device_id=(to, my), device_id_type=MESH,
        )

    pl.semaphore_wait(barrier, GX - 1 + GY - 1)

    @pl.loop(1, GX)
    def _(k):
        place(partner(mx, k, 1))
        points_copy(k).start()

    place(mx)
    recv[mx] = send[mx]

    for name in ("conv", "read"):
        fetched[name].wait()
    eye = jnp.where(
        lax.broadcasted_iota(jnp.int32, (C, C), 0) == lax.broadcasted_iota(jnp.int32, (C, C), 1),
        1.0, 0.0,
    )
    read_col = dot((eye * read[...].astype(F32)).astype(BF), jnp.ones((C, NZ), BF))

    sub_z = lax.broadcasted_iota(jnp.int32, (NZ, WIDE), 0).astype(F32)
    sub_y = lax.broadcasted_iota(jnp.int32, (CY, WIDE), 0).astype(F32)
    acc[...] = jnp.zeros(acc.shape, F32)

    @pl.loop(0, GROUPS)
    def _(g):
        blocks, tails = [], []

        @pl.when(g == 0)
        def _():
            whole(recv.at[0 : GROUP - 1], s_recv.at[0])

        @pl.when(g > 0)
        def _():
            whole(recv.at[0:GROUP], s_recv.at[g])

        for n in range(GROUP):
            msg = recv[partner(mx, GROUP * g + n, -1)]
            blocks += [msg[0:C], msg[C : 2 * C]]
            tail = msg[2 * C : 2 * C + 16].astype(F32)
            tails += [tail[0:8], tail[8:16]]
        block = jnp.concatenate(blocks, axis=1)
        tail = jnp.concatenate(tails, axis=1)
        near = jnp.exp(-2.0 * tail * tail)
        far = jnp.exp(-2.0 * (tail - 1.0) * (tail - 1.0))
        at_y, at_z = tail[3:4], tail[4:5]
        slope = tail[5:6] + tail[6:7]
        wy = jnp.where(sub_y == at_y, near[1:2], jnp.where(sub_y == at_y + 1.0, far[1:2], 0.0))
        plane = (near[0:1] * wy, far[0:1] * wy)
        planes[g, 0:CY, :] = plane[0]
        planes[g, CY : 2 * CY, :] = plane[1]
        z = jnp.where(sub_z == at_z, near[2:3], jnp.where(sub_z == at_z + 1.0, far[2:3], 0.0))
        z = z.astype(BF)
        zs[g] = z
        lifted = block.astype(F32)
        rows = [
            (lifted * plane[x][y : y + 1]).astype(BF) for y in range(CY) for x in range(CX)
        ]
        rows.append(jnp.concatenate([plane[0] * slope, plane[1] * slope], axis=0).astype(BF))
        acc[...] += dot(jnp.concatenate(rows, axis=0), z, 1, 1)

    def halo_copies(buf, sends, recvs):
        ends = (
            (right, up, buf.at[8, 2], buf.at[0, 0]),
            (right, down, buf.at[1, 2], buf.at[9, 0]),
            (left, up, buf.at[8, 1], buf.at[0, 3]),
            (left, down, buf.at[1, 1], buf.at[9, 3]),
            (mx, up, buf.at[8, 1:3], buf.at[0, 1:3]),
            (mx, down, buf.at[1, 1:3], buf.at[9, 1:3]),
            (right, my, buf.at[1:9, 2], buf.at[1:9, 0]),
            (left, my, buf.at[1:9, 1], buf.at[1:9, 3]),
        )
        return [
            pltpu.make_async_remote_copy(
                src_ref=src, dst_ref=dst, send_sem=sends, recv_sem=recvs,
                device_id=(px, py), device_id_type=MESH,
            )
            for n, (px, py, src, dst) in enumerate(ends)
        ]

    def clear_ends(buf):
        @pl.when(slab == 0)
        def _():
            buf[:, 0] = jnp.zeros((10, C, NZ), BF)

        @pl.when(slab == GX - 1)
        def _():
            buf[:, 3] = jnp.zeros((10, C, NZ), BF)

        @pl.when(my == 0)
        def _():
            buf[0] = jnp.zeros((4, C, NZ), BF)

        @pl.when(my == GY - 1)
        def _():
            buf[9] = jnp.zeros((4, C, NZ), BF)

    for y in range(CY):
        for x in range(CX):
            row = (y * CX + x) * C
            latp[y + 1, x + 1] = acc[row : row + C, :].astype(BF)
    halos = halo_copies(latp, h_send, h_recv)
    for copy in halos:
        copy.start()

    def place_tap(xp):
        lanes = lax.broadcasted_iota(jnp.int32, (C, 128), 1)
        rows = lax.broadcasted_iota(jnp.int32, (C, 128), 0)
        return jnp.where(lanes == rows + C * xp, 1.0, 0.0).astype(BF)

    spots = [place_tap(xp) for xp in range(4)]
    wf[...] = jnp.zeros(wf.shape, BF)
    wb[...] = jnp.zeros(wb.shape, BF)
    for dz in range(3):
        for dy in range(3):
            for xo in range(2):
                tile_f = sum(
                    dot(conv[9 * dx + 3 * dy + dz], spots[dx + xo], 0, 0) for dx in range(3)
                ).astype(BF)
                tile_b = sum(
                    dot(conv[9 * (2 - dx) + 3 * (2 - dy) + (2 - dz)], spots[dx + xo])
                    for dx in range(3)
                ).astype(BF)
                for yo in range(2):
                    row = ((dz * 2 + yo) * 2 + xo) * C
                    lane = (yo + dy) * 128
                    wf[row : row + C, lane : lane + 128] = tile_f
                    wb[row : row + C, lane : lane + 128] = tile_b
    whole(latp.at[0:6], h_recv)
    clear_ends(latp)

    for pair in range(4):
        pre = conv_pair(wf, latp, pair)
        cube = pre * pre
        th = jnp.tanh(0.7978845608028654 * pre * (1.0 + 0.044715 * cube))
        half = 0.5 * (1.0 + th)
        slope = half + 0.5 * pre * (1.0 - th * th) * (
            0.7978845608028654 * (1.0 + 3.0 * 0.044715 * cube)
        )
        own = latp[2 * pair + 1 : 2 * pair + 3, 1:3].reshape(4 * C, NZ).astype(F32)
        out = (own + pre * half).astype(BF).astype(F32)
        grads = []
        for yo in range(2):
            for x in range(CX):
                row = x * CY + 2 * pair + yo
                n = (yo * CX + x) * C
                field[row : row + 1, :] = jnp.sum(
                    out[n : n + C] * read_col, axis=0, keepdims=True
                )
                grads.append(read_col * acc[COLS * C + row : COLS * C + row + 1, :])
        grad_out = jnp.concatenate(grads, axis=0)
        gout[128 * pair : 128 * pair + 128, :] = grad_out
        grad_pre = (grad_out * slope).astype(BF)
        gp[2 * pair + 1 : 2 * pair + 3, 1:3] = grad_pre.reshape(2, 2, C, NZ)
        wide = grad_pre.astype(F32)
        gs[pair, 0:128, :] = shifted(wide, -1).astype(BF)
        gs[pair, 128:256, :] = grad_pre
        gs[pair, 256:384, :] = shifted(wide, 1).astype(BF)
    halos2 = halo_copies(gp, i_send, i_recv)
    for copy in halos2:
        copy.start()

    windows = [latp[2 * pair : 2 * pair + 4].reshape(4 * 4 * C, NZ) for pair in range(4)]
    tap = dot(
        jnp.concatenate(windows, axis=1),
        jnp.concatenate([gs[pair] for pair in range(4)], axis=1), 1, 1,
    )
    quarter = lax.broadcasted_iota(jnp.int32, (C, 128), 1) // C
    quarter8 = lax.broadcasted_iota(jnp.int32, (8, 128), 1) // C
    for dx in range(3):
        for dy in range(3):
            for dz in range(3):
                total = jnp.zeros((C, 128), F32)
                for yo in range(2):
                    for xo in range(2):
                        n = ((yo + dy) * 4 + xo + dx) * C
                        piece = tap[n : n + C, dz * 128 : dz * 128 + 128]
                        total = jnp.where(quarter == 2 * yo + xo, piece, total)
                total = total + pltpu.roll(total, 64, 1)
                total = total + pltpu.roll(total, 32, 1)
                packed = total[0:8]
                for q in range(1, 4):
                    packed = jnp.where(quarter8 == q, total[8 * q : 8 * q + 8], packed)
                redsrc[9 * dx + 3 * dy + dz] = packed
    redsrc[TAPS:GX] = jnp.zeros((GX - TAPS, 8, 128), F32)

    def taps_copy(k):
        to = partner(mx, k, 1)
        return pltpu.make_async_remote_copy(
            src_ref=redsrc.at[to], dst_ref=red1.at[mx],
            send_sem=a_send, recv_sem=a_recv,
            device_id=(to, my), device_id_type=MESH,
        )

    @pl.loop(1, GX)
    def _(k):
        taps_copy(k).start()

    scalar = field[...]
    scalar_hi = scalar.astype(BF)
    scalar_lo = (scalar - scalar_hi.astype(F32)).astype(BF)
    scalars = jnp.concatenate([scalar_hi, scalar_lo], axis=0)

    def pred_copy(k):
        to = partner(mx, k, -1)
        return pltpu.make_async_remote_copy(
            src_ref=predmsg.at[k, 0:CAP], dst_ref=predr.at[slab, 0:CAP],
            send_sem=p_send, recv_sem=p_recv,
            device_id=(to, my), device_id_type=MESH,
        )

    @pl.loop(0, GROUPS)
    def _(g):
        got = dot(scalars, zs[g])
        total = jnp.sum((got[0:COLS] + got[COLS:]) * planes[g], axis=0, keepdims=True)
        for n in range(GROUP):
            k = GROUP * g + n
            for r in range(CAP):
                lane = n * PTS + r * BLK
                predmsg[k, r : r + 1, :] = total[:, lane : lane + BLK]
            if n == 0:

                @pl.when(g > 0)
                def _():
                    pred_copy(GROUP * g).start()

            else:
                pred_copy(k).start()

    predr[slab, 0:CAP, :] = predmsg[0, 0:CAP, :]

    whole(gp.at[0:6], i_recv)
    clear_ends(gp)
    for pair in range(4):
        back = conv_pair(wb, gp, pair)
        gl[128 * pair : 128 * pair + 128, :] = (
            gout[128 * pair : 128 * pair + 128, :] + back
        ).astype(BF)

    def feats_copy(k):
        to = partner(mx, k, -1)
        return pltpu.make_async_remote_copy(
            src_ref=gfs.at[k], dst_ref=gfr.at[pl.ds(CAP * slab, CAP)],
            send_sem=f_send, recv_sem=f_recv,
            device_id=(to, my), device_id_type=MESH,
        )

    def rows_copy(k):
        return pltpu.make_async_remote_copy(
            src_ref=red2.at[my], dst_ref=red2.at[my],
            send_sem=b_send, recv_sem=b_recv,
            device_id=(mx, lax.rem(my + k, GY)), device_id_type=MESH,
        )

    def collect(g):
        got = dot(gl[...], zs[g])
        total = jnp.zeros((C, WIDE), F32)
        for y in range(CY):
            for x in range(CX):
                n = (y * CX + x) * C
                total = total + got[n : n + C] * planes[g, x * CY + y : x * CY + y + 1, :]
        return total.astype(BF)

    def finish(g, total):
        back = dot(lift_w, total).astype(BF)
        for n in range(GROUP):
            for r in range(CAP):
                lane = n * PTS + r * BLK
                gfs[GROUP * g + n, r] = back[:, lane : lane + BLK]

    def first_half(h):
        span = slice(h * WIDE // 2, (h + 1) * WIDE // 2)
        got = dot(gl[...], zs[1, :, span])
        total = jnp.zeros((C, WIDE // 2), F32)
        for y in range(CY):
            for x in range(CX):
                n = (y * CX + x) * C
                total = total + got[n : n + C] * planes[1, x * CY + y : x * CY + y + 1, span]
        back = dot(lift_w, total.astype(BF)).astype(BF)
        for n in range(GROUP // 2):
            k = GROUP + h * GROUP // 2 + n
            for r in range(CAP):
                lane = n * PTS + r * BLK
                gfs[k, r] = back[:, lane : lane + BLK]
            feats_copy(k).start()

    def send_back(g):
        for n in range(GROUP):
            feats_copy(GROUP * g + n).start()

    def step(g):
        before = held[...]
        total = collect(g)
        finish(g - 1, before)
        held[...] = total
        send_back(g - 1)

    first_half(0)
    first_half(1)
    held[...] = collect(2)

    @pl.loop(3, 6)
    def _(g):
        step(g)

    red1[mx] = redsrc[mx]

    whole(red1.at[0 : GX - 1], a_recv)
    red2[my] = jnp.sum(red1[...], axis=0)
    for k in range(1, GY):
        rows_copy(k).start()

    @pl.loop(6, GROUPS)
    def _(g):
        step(g)

    before = held[...]
    total = collect(0)
    finish(GROUPS - 1, before)
    send_back(GROUPS - 1)
    finish(0, total)
    for n in range(1, GROUP):
        feats_copy(n).start()
    gfr[pl.ds(CAP * slab, CAP)] = gfs[0]

    whole(red2.at[0 : GY - 1], b_recv)
    red3[mx] = (red2[0] + red2[1] + red2[2] + red2[3]) * (1.0 / GX)

    def total_copy(k):
        to = partner(mx, k, 1)
        return pltpu.make_async_remote_copy(
            src_ref=red3.at[mx], dst_ref=red3.at[mx],
            send_sem=c_send, recv_sem=c_recv,
            device_id=(to, my), device_id_type=MESH,
        )

    @pl.loop(1, GX)
    def _(k):
        total_copy(k).start()

    whole(predr.at[0 : GX - 1, 0:CAP], p_recv)
    whole(gfr.at[0 : CAP * (GX - 1)], f_recv)

    @pl.loop(0, NB)
    def _(j):
        s = slots[1, j]
        keep = aux[j, 7:8, :]
        feats_out[j] = (gfr[s].astype(F32) * keep).astype(BF)
        both = predr[s // CAP]
        value = jnp.where(lax.rem(s, CAP) == 0, both[0:1], both[1:2])
        pred_out[pl.ds(j, 1), :] = value * keep

    whole(red3.at[0 : GX - 1], c_recv)
    for d in range(TAPS):
        packed = red3[d]
        for q in range(4):
            piece = packed if q == 0 else pltpu.roll(packed, 128 - C * q, 1)
            conv_out[d, 8 * q : 8 * q + 8, :] = piece[:, 0:C]

    whole(predr.at[0 : GX - 1, 0:CAP], p_send)
    whole(gfr.at[0 : CAP * (GX - 1)], f_send)
    for sem in (c_send, a_send):
        whole(red3.at[0 : GX - 1], sem)
    whole(red2.at[0 : GY - 1], b_send)
    whole(latp.at[0:6], h_send)
    whole(gp.at[0:6], i_send)
    whole(recv.at[0 : GX - 1], s_send)


def finish_kernel(pred, feats, conv, pred_out, feats_out, conv_out, sems):
    copies = [
        pltpu.make_async_copy(src, dst, sems.at[n])
        for n, (src, dst) in enumerate(((conv, conv_out), (feats, feats_out), (pred, pred_out)))
    ]
    for copy in copies:
        copy.start()
    for copy in copies:
        copy.wait()


def local(
    point_feats, point_offsets, base_cells, block_owners, point_counts,
    lift_weight, conv_weight, read_weight, cotangent,
):
    hbm = pl.BlockSpec(memory_space=pltpu.HBM)
    vmem = pl.BlockSpec(memory_space=pltpu.VMEM)
    dma = pltpu.SemaphoreType.DMA
    inputs = (
        point_feats, jnp.transpose(point_offsets, (1, 0, 2)), base_cells,
        block_owners.reshape(1, NB), point_counts.reshape(1, 1), lift_weight, conv_weight,
        read_weight.reshape(1, C), cotangent,
    )
    parts = pl.pallas_call(
        kernel,
        out_shape=(
            pltpu.VMEM((NB, BLK), F32),
            pltpu.VMEM((NB, C, BLK), BF),
            pltpu.VMEM((TAPS, C, C), F32),
        ),
        in_specs=[hbm] * 9,
        out_specs=(vmem,) * 3,
        scratch_shapes=[
            pltpu.VMEM((NB, C, BLK), BF),
            pltpu.VMEM((3, NB, BLK), BF),
            pltpu.VMEM((NB, BLK), jnp.int32),
            pltpu.VMEM((1, NB), jnp.int32),
            pltpu.VMEM((1, 1), jnp.int32),
            pltpu.VMEM((C, C), BF),
            pltpu.VMEM((TAPS, C, C), BF),
            pltpu.VMEM((1, C), BF),
            pltpu.VMEM((NB, BLK), F32),
            pltpu.VMEM((8, BLK), jnp.int32),
            pltpu.SMEM((8, BLK), jnp.int32),
            pltpu.VMEM((NB, 8, BLK), F32),
            pltpu.VMEM((GX * CAP, C, BLK), BF),
            pltpu.VMEM((GX, 8, BLK), F32),
            pltpu.VMEM((GX, 8, 128), F32),
            dma((10,)),
            pltpu.VMEM((GX, CAP * C + 16, BLK), BF),
            pltpu.VMEM((GX, CAP * C + 16, BLK), BF),
            pltpu.VMEM((COLS * C + COLS, NZ), F32),
            pltpu.VMEM((GROUPS, NZ, WIDE), BF),
            pltpu.VMEM((GROUPS, COLS, WIDE), F32),
            pltpu.VMEM((10, 4, C, NZ), BF),
            pltpu.VMEM((10, 4, C, NZ), BF),
            pltpu.VMEM((4, 3 * 128, NZ), BF),
            pltpu.VMEM((3 * 128, 512), BF),
            pltpu.VMEM((3 * 128, 512), BF),
            pltpu.VMEM((COLS * C, NZ), F32),
            pltpu.VMEM((COLS, NZ), F32),
            pltpu.VMEM((COLS * C, NZ), BF),
            pltpu.VMEM((GX, 8, BLK), F32),
            pltpu.VMEM((C, WIDE), BF),
            pltpu.VMEM((GX, CAP, C, BLK), BF),
            pltpu.VMEM((GX, 8, 128), F32),
            pltpu.VMEM((GX, 8, 128), F32),
            pltpu.VMEM((GY, 8, 128), F32),
            dma, dma((GROUPS,)), dma, dma, dma, dma, dma, dma, dma, dma, dma, dma, dma, dma, dma, dma,
        ],
        compiler_params=pltpu.CompilerParams(
            collective_id=0, has_side_effects=True, vmem_limit_bytes=40 * 1024 * 1024
        ),
        cost_estimate=pl.CostEstimate(
            flops=8_000_000_000, bytes_accessed=2_000_000, transcendentals=1_000_000
        ),
    )(*(x if x.size == 1 else pltpu.with_memory_space_constraint(x, pltpu.HBM) for x in inputs))
    return pl.pallas_call(
        finish_kernel,
        out_shape=(
            jax.ShapeDtypeStruct((NB, BLK), F32),
            jax.ShapeDtypeStruct((NB, C, BLK), BF),
            jax.ShapeDtypeStruct((TAPS, C, C), F32),
        ),
        in_specs=[vmem] * 3,
        out_specs=(hbm,) * 3,
        scratch_shapes=[dma((3,))],
        compiler_params=pltpu.CompilerParams(vmem_limit_bytes=8 * 1024 * 1024),
    )(*(pltpu.with_memory_space_constraint(x, pltpu.VMEM) for x in parts))


def solution(mesh):
    in_specs = (
        P(("gx", "gy"), None, None),
        P(("gx", "gy"), None, None),
        P(("gx", "gy"), None),
        P(("gx", "gy"), None),
        P(("gx", "gy")),
        P(),
        P(),
        P(),
        P(("gx", "gy"), None),
    )
    out_specs = (P(("gx", "gy"), None), P(("gx", "gy"), None, None), P())
    return jax.shard_map(local, mesh=mesh, in_specs=in_specs, out_specs=out_specs, check_vma=False)
```
